32 devices in a mesh: stripe: 2 (over x), tile: 16 (over z, y, core).
Axes of the slice: x: 2, y: 2, z: 4, core: 2. Of those that a mesh axis runs over, the one named last changes fastest.
Arguments:
- mask_tiles: float32 [32, 1024, 1024], P(('stripe', 'tile')), parts along dimension 0, may hold values from -1 to 1
- target_grid: float32 [32, 16384], P(('stripe', 'tile')), parts along dimension 0, may hold values from 0 to 1
- kernels: float32 [16, 2, 24, 64, 96], P('tile'), may hold values from -48 to 48
- kern_weight: float32 [24], replicated, may hold values from 0.05 to 1
- owner_list: int32 [32, 1], P('stripe'), parts along dimension 0, may hold values from 0 to 15, as said below
Outputs:
- mask_out: float32 [32, 1024, 1024], P(('stripe', 'tile')), parts along dimension 0
- owner_error: float32 [32], P(('stripe', 'tile')), parts along dimension 0
The draws below stay inside these ranges and needn't reach their ends.
There are 2 independent parts, one for each index of `stripe`. The reference program is written for one: setup_inputs(seed, part) draws one part's arguments, and reference() takes and returns one part's arrays. A program takes and returns all parts, laid end to end along the dimension named above; an argument that names none is the same for every part. Nothing has to cross between parts.
Inputs may be any that keep to these rules, and one draw needn't show every extreme that they name: `owner_list`: every owner is named by 0 to 2 tiles of a stripe, and some owner by exactly 2.
All inputs are finite; a program needn't handle non-finite values.
Results may differ from the reference program's by a relative error of at most 0.0001.
Values sent between devices are 32-bit elements; how exact they have to be, the bound alone decides.
No kernel may reach another device: no remote copies, remote signals or barrier semaphores. Data moves between devices by JAX's collectives and lax.ppermute only.
A program may use at most 128 MiB of HBM per device.

```python
import math
import jax
import jax.numpy as jnp
from jax import lax

TILE_PX = 1024
AMBIT = 256
KERN = 24
ITERS = 1
DIFF_STEPS = 2
WIN = 1536
FREQ_X = 96
FREQ_Y = 64
GRID_X = 192
GRID_Y = 128
CORE_X = 128
TILES = 16
OWNERS = 16


def draw_owner_list(key, part):
    shuffled = jax.random.permutation(jax.random.fold_in(key, 11), TILES).astype(jnp.int32)
    pair_bits = jax.random.randint(jax.random.fold_in(key, 12), (TILES,), 0, 2, dtype=jnp.int32)
    positions = jnp.arange(TILES, dtype=jnp.int32)
    pair_bits = jnp.where(positions == 1, 1, pair_bits)
    odd_flags = positions % 2
    source_pos = positions - odd_flags * pair_bits
    return shuffled[source_pos][:, None]


def level_of(rng, shape, shards, least, high):
    def one(position, shards_of):
        steps = jax.random.uniform(jax.random.fold_in(jax.random.fold_in(rng, 6), position), (shards_of,), jnp.float32, least / len(shards), high / len(shards))
        return jnp.repeat(jnp.exp(steps), shape[position] // shards_of).reshape((-1,) + (1,) * (len(shape) - position - 1))

    loudness = one(*shards[0])
    for cut in shards[1:]:
        loudness = loudness * one(*cut)
    return loudness


def noise(own_key, shape, deviation, limit, pieces=(), held_as=jnp.bfloat16):
    result = jax.random.normal(own_key, shape, jnp.float32) * deviation
    if len(pieces) > 0:
        result = level_of(own_key, shape, pieces, -0.22, 0.18) * result
    return jnp.clip(result, min=-limit, max=limit).astype(held_as)


def setup_inputs(seed: int = 0, part: int = 0) -> dict:
    key_list = jax.random.split(jax.random.key(seed), 6)
    part_splits = jax.random.split(jax.random.fold_in(key_list[5], part), 6)
    return {
        "mask_tiles": jnp.clip(jax.random.uniform(part_splits[0], (TILES, TILE_PX, TILE_PX), jnp.float32, -1.0, 1.0) * level_of(part_splits[0], (TILES, TILE_PX, TILE_PX), ((0, 16),), -0.4, 0.0), -1.0, 1.0),
        "target_grid": jnp.clip(1.0 * jax.random.uniform(part_splits[1], (TILES, GRID_Y * CORE_X), jnp.float32) ** level_of(part_splits[1], (TILES, GRID_Y * CORE_X), ((0, 16),), -0.2, 0.2), 0.0, 1.0),
        "kernels": noise(key_list[2], (OWNERS, 2, KERN, FREQ_Y, FREQ_X), 8.0, 48.0, ((0, 16),), jnp.float32),
        "kern_weight": jnp.clip(jnp.exp(jax.random.uniform(key_list[3], (KERN,), jnp.float32, math.log(0.05), math.log(1.0))), 0.05, 1.0),
        "owner_list": draw_owner_list(jax.random.fold_in(jax.random.fold_in(key_list[5], part), 71), part),
    }


HIGHEST_PREC = lax.Precision.HIGHEST
RESIST_SLOPE = 3.0
RESIST_LEVEL = 1.2
DIFFUSE_RATE = 0.2
STEP_SIZE = 1.0

def phase_table(length, count):
    positions = jnp.arange(length, dtype=jnp.int32)[:, None]
    freq_ids = jnp.arange(count, dtype=jnp.int32)[None, :] - count // 2
    phase_turns = jnp.mod(positions * freq_ids, length).astype(jnp.float32) / length
    angles = 2.0 * math.pi * phase_turns
    return (jnp.cos(angles), jnp.sin(angles))

def spectra_of(windows, row_cos, row_sin, col_table):
    col_terms = jnp.einsum('npx,xb->npb', windows, col_table, precision=HIGHEST_PREC)
    half_cols = col_table.shape[1] // 2
    with_cos = col_terms[:, :, :half_cols]
    with_sin = col_terms[:, :, half_cols:]
    spec_real = jnp.einsum('pa,npb->nab', row_cos, with_cos, precision=HIGHEST_PREC) - jnp.einsum('pa,npb->nab', row_sin, with_sin, precision=HIGHEST_PREC)
    spec_imag = -(jnp.einsum('pa,npb->nab', row_sin, with_cos, precision=HIGHEST_PREC) + jnp.einsum('pa,npb->nab', row_cos, with_sin, precision=HIGHEST_PREC))
    tile_count = windows.shape[0]
    return jnp.concatenate([spec_real.reshape(tile_count, -1), spec_imag.reshape(tile_count, -1)], axis=1)

def diffuse(field):
    padded = jnp.pad(field, ((0, 0), (1, 1), (1, 1)), mode='edge')
    laplacian = padded[:, 2:, 1:-1] + padded[:, :-2, 1:-1] + padded[:, 1:-1, 2:] + padded[:, 1:-1, :-2] - 4.0 * field
    return field + DIFFUSE_RATE * laplacian

def tile_errors(spectra, targets, kern_sets, kern_weight, grid_tables):
    grid_row_cos, grid_row_sin, grid_col_cos, grid_col_sin = grid_tables
    tile_count = spectra.shape[0]
    freq_y, freq_x = (kern_sets.shape[3], kern_sets.shape[4])
    grid_y, grid_x = (grid_row_cos.shape[0], grid_col_cos.shape[0])
    spec_real = spectra[:, :freq_y * freq_x].reshape(tile_count, 1, freq_y, freq_x)
    spec_imag = spectra[:, freq_y * freq_x:].reshape(tile_count, 1, freq_y, freq_x)
    kern_real = kern_sets[:, 0]
    kern_imag = kern_sets[:, 1]
    field_real = kern_real * spec_real - kern_imag * spec_imag
    field_imag = kern_real * spec_imag + kern_imag * spec_real
    rows_real = jnp.einsum('ua,nkab->nkub', grid_row_cos, field_real, precision=HIGHEST_PREC) - jnp.einsum('ua,nkab->nkub', grid_row_sin, field_imag, precision=HIGHEST_PREC)
    rows_imag = jnp.einsum('ua,nkab->nkub', grid_row_cos, field_imag, precision=HIGHEST_PREC) + jnp.einsum('ua,nkab->nkub', grid_row_sin, field_real, precision=HIGHEST_PREC)
    amp_real = jnp.einsum('nkub,vb->nkuv', rows_real, grid_col_cos, precision=HIGHEST_PREC) - jnp.einsum('nkub,vb->nkuv', rows_imag, grid_col_sin, precision=HIGHEST_PREC)
    amp_imag = jnp.einsum('nkub,vb->nkuv', rows_real, grid_col_sin, precision=HIGHEST_PREC) + jnp.einsum('nkub,vb->nkuv', rows_imag, grid_col_cos, precision=HIGHEST_PREC)
    scale_norm = 1.0 / (64.0 * grid_y * grid_x)
    power = amp_real * amp_real + amp_imag * amp_imag
    intensity = jnp.einsum('k,nkuv->nuv', kern_weight, power, precision=HIGHEST_PREC) * (scale_norm * scale_norm)
    blurred = intensity
    for rounds in range(DIFF_STEPS):
        blurred = diffuse(blurred)
    resist = jax.nn.sigmoid(RESIST_SLOPE * (blurred - RESIST_LEVEL))
    core_cols = targets.shape[1] // grid_y
    offset = (grid_x - core_cols) // 2
    inner_cols = resist[:, :, offset:offset + core_cols]
    misfit = inner_cols - targets.reshape(tile_count, grid_y, core_cols)
    return lax.optimization_barrier(jnp.sum(misfit * misfit, axis=(1, 2)))

def window_stack(current):
    zero_cols = jnp.zeros((1, TILE_PX, AMBIT), current.dtype)
    left_parts = jnp.concatenate([zero_cols, current[:-1, :, TILE_PX - AMBIT:]], axis=0)
    right_parts = jnp.concatenate([current[1:, :, :AMBIT], zero_cols], axis=0)
    return jnp.concatenate([left_parts, current, right_parts], axis=2)

def reference(mask_tiles, target_grid, kernels, kern_weight, owner_list):
    row_cos, row_sin = phase_table(TILE_PX, FREQ_Y)
    col_cos, col_sin = phase_table(WIN, FREQ_X)
    col_table = jnp.concatenate([col_cos, col_sin], axis=1)
    grid_tables = phase_table(GRID_Y, FREQ_Y) + phase_table(GRID_X, FREQ_X)
    owner_column = owner_list[:, 0].astype(jnp.int32)

    def one_tile(tile_items):
        spectra_row, target_row, owner_id = tile_items
        kern_set = lax.dynamic_index_in_dim(kernels, owner_id, 0, keepdims=True)
        return tile_errors(spectra_row[None], target_row[None], kern_set, kern_weight, grid_tables)[0]

    def total_error(current):
        spectra = spectra_of(window_stack(current), row_cos, row_sin, col_table)
        errors = lax.map(one_tile, (spectra, target_grid, owner_column))
        return (jnp.sum(errors), errors)
    current = mask_tiles
    errors = None
    for rounds in range(ITERS):
        total_err, pullback, errors = jax.vjp(total_error, current, has_aux=True)
        gradient = pullback(jnp.ones_like(total_err))[0]
        current = current - STEP_SIZE * gradient
    owner_ids = jnp.arange(OWNERS, dtype=jnp.int32)[:, None]
    onehot = (owner_column[None, :] == owner_ids).astype(jnp.float32)
    owner_error = jnp.dot(onehot, errors, precision=HIGHEST_PREC) / (GRID_Y * CORE_X)
    return (current, owner_error)
```

```python
import math

import jax
import jax.numpy as jnp
import numpy as np
from jax import lax
from jax.experimental import pallas as pl
from jax.experimental.pallas import tpu as pltpu
from jax.sharding import PartitionSpec as P

AMBIT = 256
GRID_X = 192
GRID_Y = 128
CORE_X = 128
RESIST_SLOPE = 3.0
RESIST_LEVEL = 1.2
DIFFUSE_RATE = 0.2
STEP_SIZE = 1.0

LANES = 128
ROWS = 72
ROWS_PAD = 80
F32 = jnp.float32
BF16 = jnp.bfloat16


def halves_np(table):
    table = np.asarray(table, np.float32)
    top = table.astype(BF16)
    rest = (table - top.astype(np.float32)).astype(BF16)
    return top, rest


def halves(value):
    top = value.astype(BF16)
    rest = (value - top.astype(F32)).astype(BF16)
    return top, rest


def mm(left, right):
    return jnp.dot(left, right, preferred_element_type=F32)


def real_waves(places, period, most, width):
    angles = 2.0 * np.pi * np.outer(places, np.arange(most + 1)) / period
    waves = np.concatenate([np.cos(angles), np.sin(angles[:, 1:])], axis=1)
    return np.pad(waves, ((0, 0), (0, width - waves.shape[1])))


def signed_picks(count, width):
    freqs = np.arange(count) - count // 2
    most = count // 2
    even = np.zeros((count, width))
    odd = np.zeros((count, width))
    for at, freq in enumerate(freqs):
        even[at, abs(freq)] = 1.0
        if freq != 0:
            odd[at, most + abs(freq)] = np.sign(freq)
    return even, odd


def mask_tables(tile_px, freq_y, freq_x):
    win = tile_px + 2 * AMBIT
    mid_x = (GRID_X - 1) / 2 * (win // GRID_X)
    mid_y = (GRID_Y - 1) / 2 * (tile_px // GRID_Y)
    cols = real_waves(np.arange(win) - mid_x, win, freq_x // 2, LANES)
    rows = real_waves(np.arange(tile_px) - mid_y, tile_px, freq_y // 2, ROWS_PAD)
    return cols, rows


def spectrum_kernel(mask_ref, own_ref, low_ref, high_ref, rows_ref, out_ref, total):
    step = pl.program_id(0)

    @pl.when(step == 0)
    def _():
        total[...] = jnp.zeros_like(total)

    top, rest = halves(mask_ref[0])
    own_table = own_ref[...]
    low_table = low_ref[...]
    high_table = high_ref[...]
    width = top.shape[1]

    def columns(top_part, rest_part, table):
        both = mm(top_part, table)
        return both[:, :LANES] + both[:, LANES:] + mm(rest_part, table[:, :LANES])

    parts = (
        columns(top, rest, own_table),
        columns(top[:, :AMBIT], rest[:, :AMBIT], low_table),
        columns(top[:, width - AMBIT :], rest[:, width - AMBIT :], high_table),
    )
    for part, terms in enumerate(parts):
        total[part] += mm(rows_ref[...], jnp.concatenate(halves(terms), axis=1))

    @pl.when(step == pl.num_programs(0) - 1)
    def _():
        for part in range(3):
            out_ref[part] = (
                total[part, :ROWS, :LANES]
                + total[part, :ROWS, LANES:]
                + total[part, ROWS_PAD : ROWS_PAD + ROWS, :LANES]
            )


def mask_spectrum(mask_tiles, cols, rows):
    tile_px = mask_tiles.shape[1]
    block = 256
    stack = [
        np.concatenate(halves_np(part), axis=1)
        for part in (
            cols[AMBIT : AMBIT + tile_px],
            cols[AMBIT + tile_px :],
            cols[:AMBIT],
        )
    ]
    row_stack = np.concatenate(halves_np(rows.T), axis=0)
    full = lambda arr: pl.BlockSpec(arr.shape, lambda i: (0,) * arr.ndim)
    return pl.pallas_call(
        spectrum_kernel,
        grid=(tile_px // block,),
        in_specs=[pl.BlockSpec((1, block, tile_px), lambda i: (0, i, 0))]
        + [full(part) for part in stack]
        + [pl.BlockSpec((2 * ROWS_PAD, block), lambda i: (0, i))],
        out_specs=pl.BlockSpec((3, ROWS, LANES), lambda i: (0, 0, 0)),
        out_shape=jax.ShapeDtypeStruct((3, ROWS, LANES), F32),
        scratch_shapes=[pltpu.VMEM((3, 2 * ROWS_PAD, 2 * LANES), F32)],
        compiler_params=pltpu.CompilerParams(vmem_limit_bytes=24 * 2**20),
        name="mask_spectrum",
    )(mask_tiles, *[jnp.asarray(part) for part in stack], jnp.asarray(row_stack))


def update_kernel(tile_ref, mask_ref, own_ref, low_ref, high_ref, cols_ref, rows_ref, out_ref, held):
    step = pl.program_id(0)

    @pl.when(step == 0)
    def _():
        def spread(packet, table):
            top, rest = halves(packet)
            both = mm(jnp.concatenate([top, rest], axis=1), jnp.concatenate([table[:LANES], table[:LANES]], axis=0))
            return both + mm(top, table[LANES:])

        width = out_ref.shape[2]
        wide = spread(own_ref[0], cols_ref[:, AMBIT : AMBIT + width])
        left = spread(low_ref[0], cols_ref[:, AMBIT + width :])
        right = spread(high_ref[0], cols_ref[:, :AMBIT])
        wide = jnp.concatenate(
            [
                wide[:, :AMBIT] + left,
                wide[:, AMBIT : width - AMBIT],
                wide[:, width - AMBIT :] + right,
            ],
            axis=1,
        )
        wide = jnp.concatenate([wide, jnp.zeros((ROWS_PAD - ROWS, width), F32)], axis=0)
        top, rest = halves(wide)
        held[:ROWS_PAD] = top
        held[ROWS_PAD : 2 * ROWS_PAD] = rest
        held[2 * ROWS_PAD :] = top

    out_ref[0] = mask_ref[0] - STEP_SIZE * mm(rows_ref[...], held[...])


def mask_update(mask_tiles, own, low, high, cols, rows):
    tile_px = mask_tiles.shape[1]
    block = 256
    col_stack = np.concatenate(halves_np(cols.T), axis=0)
    top, rest = halves_np(rows)
    row_stack = np.concatenate([top, top, rest], axis=1)
    return pl.pallas_call(
        update_kernel,
        grid=(tile_px // block,),
        in_specs=[
            pl.BlockSpec(memory_space=pltpu.SMEM),
            pl.BlockSpec((1, block, tile_px), lambda i: (0, i, 0)),
            pl.BlockSpec((1, ROWS, LANES), lambda i: (0, 0, 0)),
            pl.BlockSpec((1, ROWS, LANES), lambda i: (0, 0, 0)),
            pl.BlockSpec((1, ROWS, LANES), lambda i: (0, 0, 0)),
            pl.BlockSpec(col_stack.shape, lambda i: (0, 0)),
            pl.BlockSpec((block, row_stack.shape[1]), lambda i: (i, 0)),
        ],
        out_specs=pl.BlockSpec((1, block, tile_px), lambda i: (0, i, 0)),
        out_shape=jax.ShapeDtypeStruct(mask_tiles.shape, F32),
        scratch_shapes=[pltpu.VMEM((3 * ROWS_PAD, tile_px), BF16)],
        compiler_params=pltpu.CompilerParams(vmem_limit_bytes=24 * 2**20),
        name="mask_update",
    )(
        jnp.zeros((1,), jnp.int32),
        mask_tiles,
        own,
        low,
        high,
        jnp.asarray(col_stack),
        jnp.asarray(row_stack),
    )


def image_tables(freq_y, freq_x):
    places_v = np.arange(GRID_X) - (GRID_X - 1) / 2
    freqs_b = np.arange(freq_x) - (freq_x - 1) / 2
    beta = 2.0 * np.pi * np.outer(freqs_b, places_v) / GRID_X
    first = (GRID_X - CORE_X) // 2

    def block(lane_of):
        table = np.zeros((2 * LANES, 2 * LANES))
        for place, lane in lane_of:
            table[:freq_x, lane] = np.cos(beta[:, place])
            table[:freq_x, LANES + lane] = np.sin(beta[:, place])
            table[LANES : LANES + freq_x, lane] = -np.sin(beta[:, place])
            table[LANES : LANES + freq_x, LANES + lane] = np.cos(beta[:, place])
        return table

    core = block([(first + lane, lane) for lane in range(CORE_X)])
    last = first + CORE_X
    rim = block(
        [(first - 2, LANES - 2), (first - 1, LANES - 1), (last, 0), (last + 1, 1)]
    )
    places_u = np.arange(GRID_Y // 2) + 0.5
    freqs_a = np.arange(freq_y) - (freq_y - 1) / 2
    alpha = 2.0 * np.pi * np.outer(places_u, freqs_a) / GRID_Y
    rows = np.concatenate([np.cos(alpha), np.sin(alpha)], axis=0)
    return core, rim, rows


def pick_tables(freq_y, freq_x):
    col_even, col_odd = signed_picks(freq_x, LANES)
    row_even, row_odd = signed_picks(freq_y, ROWS)
    lanes = np.zeros((LANES, 2 * LANES))
    lanes[:, :freq_x] = col_even.T
    lanes[:, LANES : LANES + freq_x] = col_odd.T
    rows = np.block([[row_even, -row_odd], [-row_odd, -row_even]])
    return lanes, rows


def imaging_kernel(
    me_ref, owner_ref, weight_ref, packets_ref, targets_ref, kern_ref,
    core_ref, core_t_ref, rim_ref, rim_t_ref, rows_ref, rows_t_ref,
    lanes_ref, lanes_t_ref, pick_ref, pick_t_ref, turn_ref,
    slopes_ref, error_ref,
    spec, field, rim_field, rim_lanes, rim_slope, slope_acc, scale_ref,
):
    me = me_ref[0]
    tiles = owner_ref.shape[0]
    kern_count, freq_y, freq_x = kern_ref.shape[2:]

    def find(tile, carry):
        count, first, second = carry
        mine = owner_ref[tile, 0] == me
        first = jnp.where(mine & (count == 0), tile, first)
        second = jnp.where(mine & (count == 1), tile, second)
        return count + mine.astype(jnp.int32), first, second

    zero = jnp.int32(0)
    count, first, second = lax.fori_loop(0, tiles, find, (zero, zero, zero))
    slots = (first, second)

    def pair(value):
        top, rest = halves(value)
        return jnp.concatenate([top, rest], axis=0)

    for slot in range(2):
        packet = packets_ref[slots[slot]]
        packet = jnp.where(slot < count, packet, jnp.zeros_like(packet))
        both = mm(pair(packet), lanes_ref[...])
        both = both[:ROWS] + both[ROWS:]
        tall = jnp.concatenate([both[:, :LANES], both[:, LANES:]], axis=0)
        top, rest = halves(tall)
        spec[slot] = mm(pick_ref[...], top) + mm(pick_ref[...], rest)

    half = GRID_Y // 2
    lane = lax.broadcasted_iota(jnp.int32, (freq_y, LANES), 1)
    live_lane = lane < freq_x

    def kern_at(k):
        def one(part):
            raw = kern_ref[0, part, k]
            wide = jnp.concatenate([raw, jnp.zeros((freq_y, LANES - freq_x), F32)], axis=1)
            return wide
        return one(0), one(1)

    def to_image(stack):
        top, rest = halves(stack)
        return mm(rows_ref[...], jnp.concatenate([top, rest, top], axis=0))

    def from_image(stack):
        top, rest = halves(stack)
        return mm(rows_t_ref[...], jnp.concatenate([top, rest, top], axis=0))

    def thrice(top, rest, table_ref):
        return (
            mm(top, table_ref[: 2 * LANES])
            + mm(rest, table_ref[: 2 * LANES])
            + mm(top, table_ref[2 * LANES :])
        )

    def waves(stack):
        even_re, even_im = stack[:half, :LANES], stack[:half, LANES:]
        odd_re, odd_im = stack[half:, :LANES], stack[half:, LANES:]
        return even_re - odd_im, even_im + odd_re, even_re + odd_im, even_im - odd_re

    def unwaves(plus_re, plus_im, minus_re, minus_im):
        above = jnp.concatenate([plus_re + minus_re, plus_im + minus_im], axis=1)
        below = jnp.concatenate([plus_im - minus_im, minus_re - plus_re], axis=1)
        return jnp.concatenate([above, below], axis=0)

    rim_lanes[...] = jnp.zeros_like(rim_lanes)

    def forward(k, sums):
        kern_re, kern_im = kern_at(k)
        weight = weight_ref[k]
        new = []
        for slot in range(2):
            spec_re, spec_im = spec[slot, :freq_y], spec[slot, freq_y:]
            wave = jnp.concatenate(
                [kern_re * spec_re - kern_im * spec_im, kern_re * spec_im + kern_im * spec_re], axis=1
            )
            top, rest = halves(wave)
            cols = thrice(top, rest, core_ref)
            edge = thrice(top, rest, rim_ref)
            rim_lanes[slot, :, :LANES] += pltpu.roll(edge[:, :LANES], 4 * k, 1)
            rim_lanes[slot, :, LANES:] += pltpu.roll(edge[:, LANES:], 4 * k, 1)
            parts = waves(to_image(cols))
            for part in range(4):
                field[slot, k, part] = parts[part]
            plus, minus = sums[slot]
            plus = plus + weight * (parts[0] * parts[0] + parts[1] * parts[1])
            minus = minus + weight * (parts[2] * parts[2] + parts[3] * parts[3])
            new.append((plus, minus))
        return tuple(new)

    blank = jnp.zeros((half, LANES), F32)
    sums = lax.fori_loop(0, kern_count, forward, ((blank, blank), (blank, blank)))

    def set_scale(k, carry):
        lane_row = lax.broadcasted_iota(jnp.int32, (1, LANES), 1)
        group = lax.rem(lane_row + 2, LANES) // 4
        return jnp.where(group == k, weight_ref[k], carry)

    lane_weight = lax.fori_loop(0, kern_count, set_scale, jnp.zeros((1, LANES), F32))

    norm = 1.0 / (64.0 * GRID_Y * GRID_X)
    square = norm * norm
    lane_half = lax.broadcasted_iota(jnp.int32, (half, LANES), 1)
    row_half = lax.broadcasted_iota(jnp.int32, (half, 2 * LANES), 0)
    lane_wide = lax.broadcasted_iota(jnp.int32, (half, 2 * LANES), 1)
    near = (lane_half < 2) | (lane_half >= LANES - 2)
    inside = lane_wide < LANES

    def blur(plus, minus):
        def one(value, other):
            later = jnp.where(row_half == half - 1, value, pltpu.roll(value, half - 1, 0))
            sooner = jnp.where(row_half == 0, other, pltpu.roll(value, 1, 0))
            sides = pltpu.roll(value, 1, 1) + pltpu.roll(value, 2 * LANES - 1, 1)
            return value + DIFFUSE_RATE * (later + sooner + sides - 4.0 * value)
        return one(plus, minus), one(minus, plus)

    def fold(value):
        def back(amount):
            return pltpu.roll(value, LANES - amount, 1)
        value = value + back(48)
        value = value + back(24)
        value = value + back(12)
        return value + back(4) + back(8)

    def unfold(value):
        value = jnp.where(near, value, 0.0)
        value = value + pltpu.roll(value, 4, 1) + pltpu.roll(value, 8, 1)
        value = value + pltpu.roll(value, 12, 1)
        value = value + pltpu.roll(value, 24, 1)
        return value + pltpu.roll(value, 48, 1)

    error = jnp.float32(0.0)
    for slot in range(2):
        live = (slot < count).astype(F32)
        rim_parts = waves(to_image(rim_lanes[slot]))
        for part in range(4):
            rim_field[part] = rim_parts[part]
        weights = jnp.broadcast_to(lane_weight, (half, LANES))
        rim_plus = weights * (rim_parts[0] * rim_parts[0] + rim_parts[1] * rim_parts[1])
        rim_minus = weights * (rim_parts[2] * rim_parts[2] + rim_parts[3] * rim_parts[3])
        plus = jnp.concatenate([sums[slot][0], jnp.where(near, fold(rim_plus), 0.0)], axis=1) * square
        minus = jnp.concatenate([sums[slot][1], jnp.where(near, fold(rim_minus), 0.0)], axis=1) * square
        plus, minus = blur(*blur(plus, minus))
        target = targets_ref[slots[slot]]
        t_top = target[:half]
        one = t_top.astype(BF16)
        t_top = t_top - one.astype(F32)
        two = t_top.astype(BF16)
        three = (t_top - two.astype(F32)).astype(BF16)
        turned = mm(turn_ref[...], one) + mm(turn_ref[...], two) + mm(turn_ref[...], three)

        def slope_of(value, goal):
            resist = 1.0 / (1.0 + jnp.exp(-RESIST_SLOPE * (value[:, :LANES] - RESIST_LEVEL)))
            misfit = resist - goal
            slope = (2.0 * RESIST_SLOPE) * misfit * resist * (1.0 - resist)
            slope = jnp.concatenate([slope, jnp.zeros_like(slope)], axis=1)
            return slope, jnp.sum(misfit * misfit)

        slope_plus, err_plus = slope_of(plus, target[half:])
        slope_minus, err_minus = slope_of(minus, turned)
        error = error + live * (err_plus + err_minus)
        slope_plus, slope_minus = blur(*blur(slope_plus, slope_minus))
        factor = 2.0 * square
        scale_ref[slot, 0] = slope_plus[:, :LANES] * factor
        scale_ref[slot, 1] = slope_minus[:, :LANES] * factor
        rim_f_plus = unfold(slope_plus[:, LANES:] * factor) * weights
        rim_f_minus = unfold(slope_minus[:, LANES:] * factor) * weights
        rim_slope[slot] = from_image(
            unwaves(
                rim_f_plus * rim_field[0],
                rim_f_plus * rim_field[1],
                rim_f_minus * rim_field[2],
                rim_f_minus * rim_field[3],
            )
        )
    error_ref[0] = error * (1.0 / (GRID_Y * CORE_X))

    slope_acc[...] = jnp.zeros_like(slope_acc)
    rim_lane = (lane < 2) | (lane >= LANES - 2)

    def backward(k, carry):
        kern_re, kern_im = kern_at(k)
        weight = weight_ref[k]
        for slot in range(2):
            plus = scale_ref[slot, 0] * weight
            minus = scale_ref[slot, 1] * weight
            cols = from_image(
                unwaves(
                    plus * field[slot, k, 0],
                    plus * field[slot, k, 1],
                    minus * field[slot, k, 2],
                    minus * field[slot, k, 3],
                )
            )
            top, rest = halves(cols)
            wave = thrice(top, rest, core_t_ref)
            edge = jnp.concatenate(
                [
                    pltpu.roll(rim_slope[slot, :, :LANES], LANES - 4 * k, 1),
                    pltpu.roll(rim_slope[slot, :, LANES:], LANES - 4 * k, 1),
                ],
                axis=1,
            )
            top, rest = halves(edge)
            wave = wave + thrice(top, rest, rim_t_ref)
            wave_re, wave_im = wave[:, :LANES], wave[:, LANES:]
            slope_acc[slot, :freq_y] += wave_re * kern_re + wave_im * kern_im
            slope_acc[slot, freq_y:] += wave_im * kern_re - wave_re * kern_im
        return carry

    lax.fori_loop(0, kern_count, backward, 0)

    for slot in (1, 0):
        top, rest = halves(slope_acc[slot])
        tall = mm(pick_t_ref[...], top) + mm(pick_t_ref[...], rest)
        wide = jnp.concatenate([tall[:ROWS], tall[ROWS:]], axis=1)
        both = mm(pair(wide), lanes_t_ref[...])
        slopes_ref[slots[slot]] = both[:ROWS] + both[ROWS:]


def owner_imaging(me, owner_list, kern_weight, packets, targets, kernels):
    kern_count, freq_y, freq_x = kernels.shape[2:]
    tiles = packets.shape[0]
    core, rim, rows = image_tables(freq_y, freq_x)
    lanes, picks = pick_tables(freq_y, freq_x)

    def tall(table):
        return np.concatenate(halves_np(table), axis=0)

    def three(table):
        top, rest = halves_np(table)
        return np.concatenate([top, top, rest], axis=1)

    tables = [
        tall(core),
        tall(core.T),
        tall(rim),
        tall(rim.T),
        three(rows),
        three(rows.T),
        lanes.astype(BF16),
        lanes.T.astype(BF16),
        picks.astype(BF16),
        picks.T.astype(BF16),
        np.eye(GRID_Y // 2)[::-1].astype(BF16),
    ]
    half = GRID_Y // 2
    smem = pl.BlockSpec(memory_space=pltpu.SMEM)
    vmem = pl.BlockSpec(memory_space=pltpu.VMEM)
    return pl.pallas_call(
        imaging_kernel,
        in_specs=[smem, smem, smem] + [vmem] * (3 + len(tables)),
        out_specs=(vmem, smem),
        out_shape=(
            jax.ShapeDtypeStruct((tiles, ROWS, LANES), F32),
            jax.ShapeDtypeStruct((1,), F32),
        ),
        scratch_shapes=[
            pltpu.VMEM((2, 2 * freq_y, LANES), F32),
            pltpu.VMEM((2, kern_count, 4, half, LANES), F32),
            pltpu.VMEM((4, half, LANES), F32),
            pltpu.VMEM((2, freq_y, 2 * LANES), F32),
            pltpu.VMEM((2, freq_y, 2 * LANES), F32),
            pltpu.VMEM((2, 2 * freq_y, LANES), F32),
            pltpu.VMEM((2, 2, half, LANES), F32),
        ],
        compiler_params=pltpu.CompilerParams(vmem_limit_bytes=40 * 2**20),
        name="owner_imaging",
    )(me, owner_list, kern_weight, packets, targets, kernels, *[jnp.asarray(t) for t in tables])


def on_device(mask_tiles, target_grid, kernels, kern_weight, owner_list):
    tile_px = mask_tiles.shape[1]
    freq_y, freq_x = kernels.shape[3:]
    count = lax.axis_size("tile")
    cols, rows = mask_tables(tile_px, freq_y, freq_x)
    me = lax.axis_index("tile").astype(jnp.int32)
    up = [(i, i + 1) for i in range(count - 1)]
    down = [(i + 1, i) for i in range(count - 1)]

    def spread(packet):
        wide = jnp.broadcast_to(packet[None], (count,) + packet.shape)
        return lax.all_to_all(wide, "tile", 0, 0, tiled=True)

    targets = spread(target_grid.reshape(GRID_Y, CORE_X))
    parts = mask_spectrum(mask_tiles, cols, rows)
    from_next = lax.ppermute(parts[1], "tile", down)
    from_last = lax.ppermute(parts[2], "tile", up)
    packets = spread(parts[0] + from_next + from_last)
    slopes, owner_error = owner_imaging(
        me.reshape(1), owner_list, kern_weight, packets, targets, kernels
    )
    returned = lax.all_to_all(slopes, "tile", 0, 0, tiled=True)
    my_owner = lax.dynamic_index_in_dim(owner_list[:, 0], me, 0, keepdims=False)
    own = lax.dynamic_index_in_dim(returned, my_owner, 0, keepdims=True)
    last = lax.ppermute(own, "tile", up)
    following = lax.ppermute(own, "tile", down)
    current = mask_update(mask_tiles, own, last, following, cols, rows)
    return (current, owner_error)


def solution(mesh):
    placed = (
        P(("stripe", "tile"), None, None),
        P(("stripe", "tile"), None),
        P("tile", None, None, None, None),
        P(),
        P("stripe", None),
    )
    return jax.shard_map(
        on_device,
        mesh=mesh,
        in_specs=placed,
        out_specs=(P(("stripe", "tile"), None, None), P(("stripe", "tile"))),
        check_vma=False,
    )
```

```python
import functools

import jax
import jax.numpy as jnp
import numpy as np
from jax import lax
from jax.experimental import pallas as pl
from jax.experimental.pallas import tpu as pltpu
from jax.sharding import PartitionSpec as P

AMBIT = 256
GRID_X = 192
GRID_Y = 128
CORE_X = 128
RESIST_SLOPE = 3.0
RESIST_LEVEL = 1.2
DIFFUSE_RATE = 0.2
STEP_SIZE = 1.0

LANES = 128
MOST = 2
BLOCKS = 4
BATCH = 6
ROWS = 72
ROWS_PAD = 80
F32 = jnp.float32
BF16 = jnp.bfloat16


def halves_np(table):
    table = np.asarray(table, np.float32)
    top = table.astype(BF16)
    rest = (table - top.astype(np.float32)).astype(BF16)
    return top, rest


def halves(value):
    top = value.astype(BF16)
    rest = (value - top.astype(F32)).astype(BF16)
    return top, rest


def mm(left, right):
    return jnp.dot(left, right, preferred_element_type=F32)


def in_hbm(value):
    return pltpu.with_memory_space_constraint(jnp.asarray(value), pltpu.HBM)


def real_waves(places, period, most, width):
    angles = 2.0 * np.pi * np.outer(places, np.arange(most + 1)) / period
    waves = np.concatenate([np.cos(angles), np.sin(angles[:, 1:])], axis=1)
    return np.pad(waves, ((0, 0), (0, width - waves.shape[1])))


def signed_picks(count, width):
    freqs = np.arange(count) - count // 2
    most = count // 2
    even = np.zeros((count, width))
    odd = np.zeros((count, width))
    for at, freq in enumerate(freqs):
        even[at, abs(freq)] = 1.0
        if freq != 0:
            odd[at, most + abs(freq)] = np.sign(freq)
    return even, odd


def mask_tables(tile_px, freq_y, freq_x):
    win = tile_px + 2 * AMBIT
    mid_x = (GRID_X - 1) / 2 * (win // GRID_X)
    mid_y = (GRID_Y - 1) / 2 * (tile_px // GRID_Y)
    cols = real_waves(np.arange(win) - mid_x, win, freq_x // 2, LANES)
    rows = real_waves(np.arange(tile_px) - mid_y, tile_px, freq_y // 2, ROWS_PAD)
    return cols, rows


def rim_marks(packet):
    row = lax.broadcasted_iota(jnp.int32, packet.shape, 0)
    lane = lax.broadcasted_iota(jnp.int32, packet.shape, 1)
    return lane, lax.rem(lane - row + LANES, packet.shape[0]) == 0


def packed(tall, used):
    body, line = tall[:-8], tall[-8:-7]
    rows = body.shape[0]
    lane, marked = rim_marks(body)
    line = jnp.where(marked & (lane < used), jnp.broadcast_to(line, body.shape), 0.0)
    one = jnp.sum(jnp.where(lane < rows, line, 0.0), axis=1, keepdims=True)
    two = jnp.sum(jnp.where(lane >= rows, line, 0.0), axis=1, keepdims=True)
    body = jnp.where(lane < used, body, 0.0)
    return jnp.where(lane == used, one, jnp.where(lane == used + 1, two, body))


def unpacked(packet, used):
    rows = packet.shape[0]
    lane, marked = rim_marks(packet)
    line = jnp.where(lane < rows, packet[:, used : used + 1], packet[:, used + 1 : used + 2])
    line = jnp.sum(jnp.where(marked & (lane < used), line, 0.0), axis=0, keepdims=True)
    body = jnp.where(lane < used, packet, 0.0)
    return jnp.concatenate([body, line, jnp.zeros((7, LANES), F32)], axis=0)


def fetch(pairs, sems):
    copies = [pltpu.make_async_copy(src, dst, sems.at[at]) for at, (src, dst) in enumerate(pairs)]
    for copy in copies:
        copy.start()
    return copies


def spectrum_kernel(used, me_ref, mask_hbm, cols_hbm, rows_hbm, out_ref, mask, cols, rows, total, sems):
    tile_px = mask.shape[0]
    block = tile_px // BLOCKS
    pairs = [(cols_hbm, cols), (rows_hbm, rows)]
    for at in range(BLOCKS):
        place = pl.ds(at * block, block)
        pairs.append((mask_hbm.at[0, place], mask.at[place]))
    copies = fetch(pairs, sems)
    copies[0].wait()
    copies[1].wait()

    def columns(top_part, rest_part, table):
        both = mm(top_part, table)
        return both[:, :LANES] + both[:, LANES:] + mm(rest_part, table[:, :LANES])

    for at in range(BLOCKS):
        copies[2 + at].wait()
        top, rest = halves(mask[at * block : (at + 1) * block])
        row_table = rows[:, at * block : (at + 1) * block]
        parts = (
            columns(top, rest, cols[AMBIT : AMBIT + tile_px]),
            columns(top[:, :AMBIT], rest[:, :AMBIT], cols[AMBIT + tile_px :]),
            columns(top[:, tile_px - AMBIT :], rest[:, tile_px - AMBIT :], cols[:AMBIT]),
        )
        for part, terms in enumerate(parts):
            piece = mm(row_table, jnp.concatenate(halves(terms), axis=1))
            if at == 0:
                total[part] = piece
            else:
                total[part] += piece

    def summed(part):
        whole = total[part]
        return packed(
            whole[:ROWS, :LANES] + whole[:ROWS, LANES:] + whole[ROWS_PAD : ROWS_PAD + ROWS, :LANES], used
        )

    odd = lax.rem(me_ref[0], 2) == 1
    low, high = summed(1), summed(2)
    out_ref[0] = summed(0)
    out_ref[1] = jnp.where(odd, high, low)
    out_ref[2] = jnp.where(odd, low, high)


def mask_spectrum(me, mask_tiles, cols, rows, freq_y, freq_x):
    tile_px = mask_tiles.shape[1]
    col_stack = np.concatenate(halves_np(cols), axis=1)
    row_stack = np.concatenate(halves_np(rows.T), axis=0)
    hbm = pl.BlockSpec(memory_space=pltpu.HBM)
    return pl.pallas_call(
        functools.partial(spectrum_kernel, freq_x + 1),
        in_specs=[pl.BlockSpec(memory_space=pltpu.SMEM), hbm, hbm, hbm],
        out_specs=pl.BlockSpec(memory_space=pltpu.VMEM),
        out_shape=jax.ShapeDtypeStruct((3, freq_y, LANES), F32),
        scratch_shapes=[
            pltpu.VMEM((tile_px, tile_px), F32),
            pltpu.VMEM(col_stack.shape, BF16),
            pltpu.VMEM(row_stack.shape, BF16),
            pltpu.VMEM((3, 2 * ROWS_PAD, 2 * LANES), F32),
            pltpu.SemaphoreType.DMA((2 + BLOCKS,)),
        ],
        compiler_params=pltpu.CompilerParams(vmem_limit_bytes=20 * 2**20),
        name="mask_spectrum",
    )(me, in_hbm(mask_tiles), in_hbm(col_stack), in_hbm(row_stack))


def slot_of(owner_ref, tile):
    owner = owner_ref[tile]

    def count(other, before):
        return before + ((owner_ref[other] == owner) & (other < tile)).astype(jnp.int32)

    return owner, lax.fori_loop(0, owner_ref.shape[0], count, jnp.int32(0))


def tiles_of(owner_ref, owner):
    def find(tile, carry):
        count, first, second = carry
        mine = owner_ref[tile] == owner
        first = jnp.where(mine & (count == 0), tile, first)
        second = jnp.where(mine & (count == 1), tile, second)
        return count + mine.astype(jnp.int32), first, second

    zero = jnp.int32(0)
    return lax.fori_loop(0, owner_ref.shape[0], find, (zero, zero, zero))


def mate_of(me):
    return me + 1 - 2 * lax.rem(me, 2)


def owner_pick_kernel(me_ref, owner_ref, packets_hbm, targets_hbm, out_ref, sems):
    _, first, second = tiles_of(owner_ref, mate_of(me_ref[0]))
    rows = packets_hbm.shape[1]
    pairs = []
    for slot, tile in enumerate((first, second)):
        pairs.append((packets_hbm.at[tile], out_ref.at[slot, pl.ds(0, rows)]))
        pairs.append((targets_hbm.at[tile], out_ref.at[slot, pl.ds(rows, targets_hbm.shape[1])]))
    for copy in fetch(pairs, sems):
        copy.wait()


def owner_pick(me, owner_list, packets, targets):
    smem = pl.BlockSpec(memory_space=pltpu.SMEM)
    vmem = pl.BlockSpec(memory_space=pltpu.VMEM)
    hbm = pl.BlockSpec(memory_space=pltpu.HBM)
    rows = packets.shape[1] + targets.shape[1]
    return pl.pallas_call(
        owner_pick_kernel,
        in_specs=[smem, smem, hbm, hbm],
        out_specs=vmem,
        out_shape=jax.ShapeDtypeStruct((MOST, rows, LANES), F32),
        scratch_shapes=[pltpu.SemaphoreType.DMA((2 * MOST,))],
        compiler_params=pltpu.CompilerParams(vmem_limit_bytes=2**20),
        name="owner_pick",
    )(me, owner_list, in_hbm(packets), in_hbm(targets))


def around(tile, tiles):
    return [
        (tile, None),
        (jnp.maximum(tile - 1, 0), tile > 0),
        (jnp.minimum(tile + 1, tiles - 1), tile < tiles - 1),
    ]


def tile_pick_kernel(me_ref, owner_ref, slopes_hbm, out_ref, sems):
    pairs = []
    for at, (tile, _) in enumerate(around(mate_of(me_ref[0]), owner_ref.shape[0])):
        owner, slot = slot_of(owner_ref, tile)
        pairs.append((slopes_hbm.at[owner, slot], out_ref.at[at]))
    for copy in fetch(pairs, sems):
        copy.wait()


def tile_pick(me, owner_list, slopes):
    smem = pl.BlockSpec(memory_space=pltpu.SMEM)
    vmem = pl.BlockSpec(memory_space=pltpu.VMEM)
    return pl.pallas_call(
        tile_pick_kernel,
        in_specs=[smem, smem, pl.BlockSpec(memory_space=pltpu.HBM)],
        out_specs=vmem,
        out_shape=jax.ShapeDtypeStruct((3,) + slopes.shape[2:], F32),
        scratch_shapes=[pltpu.SemaphoreType.DMA((3,))],
        compiler_params=pltpu.CompilerParams(vmem_limit_bytes=2**20),
        name="tile_pick",
    )(me, owner_list, in_hbm(slopes))


def joined(me, mine, other):
    odd = lax.rem(me, 2) == 1
    return jnp.concatenate([jnp.where(odd, other, mine), jnp.where(odd, mine, other)], axis=0)


def update_kernel(
    used, me_ref, owner_ref, slopes_hbm, other_ref, mask_hbm, cols_hbm, rows_hbm, out_hbm,
    mask, cols, rows, held, slopes, sems, out_sems, slope_sems,
):
    tile_px = mask.shape[0]
    block = tile_px // BLOCKS
    places = [pl.ds(at * block, block) for at in range(BLOCKS)]
    me = me_ref[0]
    near = around(me, owner_ref.shape[0])
    pairs = []
    for at, (tile, _) in enumerate(near):
        owner, slot = slot_of(owner_ref, tile)
        pairs.append((slopes_hbm.at[owner, slot], slopes.at[at]))
    slope_copies = fetch(pairs, slope_sems)
    copies = fetch(
        [(cols_hbm, cols), (rows_hbm, rows)]
        + [(mask_hbm.at[0, place], mask.at[place]) for place in places],
        sems,
    )
    packets = []
    for at, (_, there) in enumerate(near):
        slope_copies[at].wait()
        packet = unpacked(joined(me, slopes[at], other_ref[at]), used)
        packets.append(packet if there is None else jnp.where(there, packet, 0.0))
    copies[0].wait()

    def spread(packet, table):
        top, rest = halves(packet)
        return mm(
            jnp.concatenate([top, rest, top], axis=1),
            jnp.concatenate([table[:LANES], table[:LANES], table[LANES:]], axis=0),
        )

    wide = spread(packets[0], cols[:, AMBIT : AMBIT + tile_px])
    left = spread(packets[1], cols[:, AMBIT + tile_px :])
    right = spread(packets[2], cols[:, :AMBIT])
    wide = jnp.concatenate(
        [
            wide[:, :AMBIT] + left,
            wide[:, AMBIT : tile_px - AMBIT],
            wide[:, tile_px - AMBIT :] + right,
        ],
        axis=1,
    )
    wide = jnp.concatenate([wide, jnp.zeros((ROWS_PAD - ROWS, tile_px), F32)], axis=0)
    top, rest = halves(wide)
    held[:ROWS_PAD] = top
    held[ROWS_PAD : 2 * ROWS_PAD] = rest
    held[2 * ROWS_PAD :] = top
    copies[1].wait()
    sent = []
    for at, place in enumerate(places):
        copies[2 + at].wait()
        here = slice(at * block, (at + 1) * block)
        mask[here] = mask[here] - STEP_SIZE * mm(rows[here], held[...])
        copy = pltpu.make_async_copy(mask.at[place], out_hbm.at[0, place], out_sems.at[at])
        copy.start()
        sent.append(copy)
    for copy in sent:
        copy.wait()


def mask_update(me, owner_list, slopes, other, mask_tiles, cols, rows, freq_x):
    tile_px = mask_tiles.shape[1]
    col_stack = np.concatenate(halves_np(cols.T), axis=0)
    top, rest = halves_np(rows)
    row_stack = np.concatenate([top, top, rest], axis=1)
    smem = pl.BlockSpec(memory_space=pltpu.SMEM)
    vmem = pl.BlockSpec(memory_space=pltpu.VMEM)
    hbm = pl.BlockSpec(memory_space=pltpu.HBM)
    return pl.pallas_call(
        functools.partial(update_kernel, freq_x + 1),
        in_specs=[smem, smem, hbm, vmem, hbm, hbm, hbm],
        out_specs=hbm,
        out_shape=jax.ShapeDtypeStruct(mask_tiles.shape, F32),
        scratch_shapes=[
            pltpu.VMEM((tile_px, tile_px), F32),
            pltpu.VMEM(col_stack.shape, BF16),
            pltpu.VMEM(row_stack.shape, BF16),
            pltpu.VMEM((3 * ROWS_PAD, tile_px), BF16),
            pltpu.VMEM((3,) + slopes.shape[2:], F32),
            pltpu.SemaphoreType.DMA((2 + BLOCKS,)),
            pltpu.SemaphoreType.DMA((BLOCKS,)),
            pltpu.SemaphoreType.DMA((3,)),
        ],
        compiler_params=pltpu.CompilerParams(vmem_limit_bytes=20 * 2**20),
        name="mask_update",
    )(
        me, owner_list, in_hbm(slopes), other, in_hbm(mask_tiles), in_hbm(col_stack), in_hbm(row_stack)
    )


def image_tables(freq_y, freq_x):
    places_v = np.arange(GRID_X) - (GRID_X - 1) / 2
    freqs_b = np.arange(freq_x) - (freq_x - 1) / 2
    beta = 2.0 * np.pi * np.outer(freqs_b, places_v) / GRID_X
    first = (GRID_X - CORE_X) // 2

    def block(lane_of):
        table = np.zeros((2 * LANES, 2 * LANES))
        for place, lane in lane_of:
            table[:freq_x, lane] = np.cos(beta[:, place])
            table[:freq_x, LANES + lane] = np.sin(beta[:, place])
            table[LANES : LANES + freq_x, lane] = -np.sin(beta[:, place])
            table[LANES : LANES + freq_x, LANES + lane] = np.cos(beta[:, place])
        return table

    core = block([(first + lane, lane) for lane in range(CORE_X)])
    last = first + CORE_X
    rim = block(
        [(first - 2, LANES - 2), (first - 1, LANES - 1), (last, 0), (last + 1, 1)]
    )
    places_u = np.arange(GRID_Y // 2) + 0.5
    freqs_a = np.arange(freq_y) - (freq_y - 1) / 2
    alpha = 2.0 * np.pi * np.outer(places_u, freqs_a) / GRID_Y
    rows = np.concatenate([np.cos(alpha), np.sin(alpha)], axis=0)
    return core, rim, rows


def pick_tables(freq_y, freq_x):
    col_even, col_odd = signed_picks(freq_x, LANES)
    row_even, row_odd = signed_picks(freq_y, ROWS)
    lanes = np.zeros((LANES, 2 * LANES))
    lanes[:, :freq_x] = col_even.T
    lanes[:, LANES : LANES + freq_x] = col_odd.T
    rows = np.block([[row_even, -row_odd], [-row_odd, -row_even]])
    return lanes, rows


def imaging_kernel(
    places, used, me_ref, owner_ref, weight_ref, packets_hbm, targets_hbm, other_ref, kern_ref, table_ref,
    slopes_hbm, error_ref,
    spec, field, rim_field, rim_lanes, rim_slope, slope_acc, scale_ref, ready, packets, targets, sems, slot_sems,
):
    me = me_ref[0]
    kern_count, freq_y, freq_x = kern_ref.shape[2:]
    batch = max(size for size in range(1, BATCH + 1) if kern_count % size == 0)
    count, first, second = tiles_of(owner_ref, me)
    slots = (first, second)
    split = packets_hbm.shape[1]
    arrivals = fetch(
        [(packets_hbm.at[slots[slot]], packets.at[slot]) for slot in range(MOST)]
        + [(targets_hbm.at[slots[slot]], targets.at[slot]) for slot in range(MOST)],
        slot_sems,
    )
    for copy in arrivals:
        copy.wait()

    def table(name):
        start, height, width = places[name]
        return table_ref[start : start + height, :width]

    def pair(value):
        top, rest = halves(value)
        return jnp.concatenate([top, rest], axis=0)

    for slot in range(MOST):
        packet = joined(me, packets[slot], other_ref[slot, :split])
        packet = jnp.where(slot < count, unpacked(packet, used), 0.0)
        both = mm(pair(packet), table("lanes"))
        both = both[:ROWS] + both[ROWS:]
        tall = jnp.concatenate([both[:, :LANES], both[:, LANES:]], axis=0)
        top, rest = halves(tall)
        spec[slot] = mm(table("picks"), top) + mm(table("picks"), rest)

    half = GRID_Y // 2
    lane = lax.broadcasted_iota(jnp.int32, (freq_y, LANES), 1)
    live_lane = lane < freq_x

    def kern_at(k):
        def one(part):
            raw = kern_ref[0, part, k]
            wide = jnp.concatenate([raw, jnp.zeros((freq_y, LANES - freq_x), F32)], axis=1)
            return wide
        return one(0), one(1)

    def to_image(stack):
        top, rest = halves(stack)
        return mm(table("rows"), jnp.concatenate([top, rest, top], axis=0))

    def from_image(stack):
        top, rest = halves(stack)
        both = mm(table("rows_t"), jnp.concatenate([top, rest], axis=0))
        return both[:freq_y] + both[freq_y:]

    def thrice(top, rest, name):
        both = table(name)
        height = both.shape[0] // 2
        return mm(
            jnp.concatenate([top, rest, top], axis=1),
            jnp.concatenate([both[:height], both[:height], both[height:]], axis=0),
        )

    def waves(stack):
        even_re, even_im = stack[:half, :LANES], stack[:half, LANES:]
        odd_re, odd_im = stack[half:, :LANES], stack[half:, LANES:]
        return even_re - odd_im, even_im + odd_re, even_re + odd_im, even_im - odd_re

    def unwaves(plus_re, plus_im, minus_re, minus_im):
        above = jnp.concatenate([plus_re + minus_re, plus_im + minus_im], axis=1)
        below = jnp.concatenate([plus_im - minus_im, minus_re - plus_re], axis=1)
        return jnp.concatenate([above, below], axis=0)

    rim_lanes[...] = jnp.zeros_like(rim_lanes)

    def forward(group, sums):
        tops, rests = [], []
        for step in range(batch):
            kern_re, kern_im = kern_at(group * batch + step)
            for slot in range(2):
                spec_re, spec_im = spec[slot, :freq_y], spec[slot, freq_y:]
                wave = jnp.concatenate(
                    [kern_re * spec_re - kern_im * spec_im, kern_re * spec_im + kern_im * spec_re], axis=1
                )
                top, rest = halves(wave)
                tops.append(top)
                rests.append(rest)
        top, rest = jnp.concatenate(tops, axis=0), jnp.concatenate(rests, axis=0)
        cols = thrice(top, rest, "core")
        edges = thrice(top, rest, "rim")
        new = list(sums)
        for step in range(batch):
            k = group * batch + step
            weight = weight_ref[k]
            for slot in range(2):
                at = (2 * step + slot) * freq_y
                edge = edges[at : at + freq_y]
                rim_lanes[slot, :, :LANES] += pltpu.roll(edge[:, :LANES], 4 * k, 1)
                rim_lanes[slot, :, LANES:] += pltpu.roll(edge[:, LANES:], 4 * k, 1)
                parts = waves(to_image(cols[at : at + freq_y]))
                for part in range(4):
                    field[slot, k, part] = parts[part]
                plus, minus = new[slot]
                plus = plus + weight * (parts[0] * parts[0] + parts[1] * parts[1])
                minus = minus + weight * (parts[2] * parts[2] + parts[3] * parts[3])
                new[slot] = (plus, minus)
        return tuple(new)

    blank = jnp.zeros((half, LANES), F32)
    sums = lax.fori_loop(0, kern_count // batch, forward, ((blank, blank), (blank, blank)))

    def set_scale(k, carry):
        lane_row = lax.broadcasted_iota(jnp.int32, (1, LANES), 1)
        group = lax.rem(lane_row + 2, LANES) // 4
        return jnp.where(group == k, weight_ref[k], carry)

    lane_weight = lax.fori_loop(0, kern_count, set_scale, jnp.zeros((1, LANES), F32))

    norm = 1.0 / (64.0 * GRID_Y * GRID_X)
    square = norm * norm
    lane_half = lax.broadcasted_iota(jnp.int32, (half, LANES), 1)
    row_half = lax.broadcasted_iota(jnp.int32, (half, 2 * LANES), 0)
    lane_wide = lax.broadcasted_iota(jnp.int32, (half, 2 * LANES), 1)
    near = (lane_half < 2) | (lane_half >= LANES - 2)
    inside = lane_wide < LANES

    def blur(plus, minus):
        def one(value, other):
            later = jnp.where(row_half == half - 1, value, pltpu.roll(value, half - 1, 0))
            sooner = jnp.where(row_half == 0, other, pltpu.roll(value, 1, 0))
            sides = pltpu.roll(value, 1, 1) + pltpu.roll(value, 2 * LANES - 1, 1)
            return value + DIFFUSE_RATE * (later + sooner + sides - 4.0 * value)
        return one(plus, minus), one(minus, plus)

    def fold(value):
        def back(amount):
            return pltpu.roll(value, LANES - amount, 1)
        value = value + back(48)
        value = value + back(24)
        value = value + back(12)
        return value + back(4) + back(8)

    def unfold(value):
        value = jnp.where(near, value, 0.0)
        value = value + pltpu.roll(value, 4, 1) + pltpu.roll(value, 8, 1)
        value = value + pltpu.roll(value, 12, 1)
        value = value + pltpu.roll(value, 24, 1)
        return value + pltpu.roll(value, 48, 1)

    error = jnp.float32(0.0)
    for slot in range(2):
        live = (slot < count).astype(F32)
        rim_parts = waves(to_image(rim_lanes[slot]))
        for part in range(4):
            rim_field[part] = rim_parts[part]
        weights = jnp.broadcast_to(lane_weight, (half, LANES))
        rim_plus = weights * (rim_parts[0] * rim_parts[0] + rim_parts[1] * rim_parts[1])
        rim_minus = weights * (rim_parts[2] * rim_parts[2] + rim_parts[3] * rim_parts[3])
        plus = jnp.concatenate([sums[slot][0], jnp.where(near, fold(rim_plus), 0.0)], axis=1) * square
        minus = jnp.concatenate([sums[slot][1], jnp.where(near, fold(rim_minus), 0.0)], axis=1) * square
        plus, minus = blur(*blur(plus, minus))
        target = joined(me, targets[slot], other_ref[slot, split:])
        t_top = target[:half]
        one = t_top.astype(BF16)
        t_top = t_top - one.astype(F32)
        two = t_top.astype(BF16)
        three = (t_top - two.astype(F32)).astype(BF16)
        turned = mm(table("turn"), one) + mm(table("turn"), two) + mm(table("turn"), three)

        def slope_of(value, goal):
            resist = 1.0 / (1.0 + jnp.exp(-RESIST_SLOPE * (value[:, :LANES] - RESIST_LEVEL)))
            misfit = resist - goal
            slope = (2.0 * RESIST_SLOPE) * misfit * resist * (1.0 - resist)
            slope = jnp.concatenate([slope, jnp.zeros_like(slope)], axis=1)
            return slope, jnp.sum(misfit * misfit)

        slope_plus, err_plus = slope_of(plus, target[half:])
        slope_minus, err_minus = slope_of(minus, turned)
        error = error + live * (err_plus + err_minus)
        slope_plus, slope_minus = blur(*blur(slope_plus, slope_minus))
        factor = 2.0 * square
        scale_ref[slot, 0] = slope_plus[:, :LANES] * factor
        scale_ref[slot, 1] = slope_minus[:, :LANES] * factor
        rim_f_plus = unfold(slope_plus[:, LANES:] * factor) * weights
        rim_f_minus = unfold(slope_minus[:, LANES:] * factor) * weights
        rim_slope[slot] = from_image(
            unwaves(
                rim_f_plus * rim_field[0],
                rim_f_plus * rim_field[1],
                rim_f_minus * rim_field[2],
                rim_f_minus * rim_field[3],
            )
        )
    error_ref[0] = error * (1.0 / (GRID_Y * CORE_X))

    slope_acc[...] = jnp.zeros_like(slope_acc)
    rim_lane = (lane < 2) | (lane >= LANES - 2)

    def backward(group, carry):
        tops, rests, rim_tops, rim_rests = [], [], [], []
        for step in range(batch):
            k = group * batch + step
            weight = weight_ref[k]
            for slot in range(2):
                plus = scale_ref[slot, 0] * weight
                minus = scale_ref[slot, 1] * weight
                cols = from_image(
                    unwaves(
                        plus * field[slot, k, 0],
                        plus * field[slot, k, 1],
                        minus * field[slot, k, 2],
                        minus * field[slot, k, 3],
                    )
                )
                top, rest = halves(cols)
                tops.append(top)
                rests.append(rest)
                edge = jnp.concatenate(
                    [
                        pltpu.roll(rim_slope[slot, :, :LANES], LANES - 4 * k, 1),
                        pltpu.roll(rim_slope[slot, :, LANES:], LANES - 4 * k, 1),
                    ],
                    axis=1,
                )
                top, rest = halves(edge)
                rim_tops.append(top)
                rim_rests.append(rest)
        def stack(pieces):
            return jnp.concatenate(pieces, axis=0)
        waves_all = thrice(stack(tops), stack(rests), "core_t") + thrice(
            stack(rim_tops), stack(rim_rests), "rim_t"
        )
        sums = [[slope_acc[slot, :freq_y], slope_acc[slot, freq_y:]] for slot in range(2)]
        for step in range(batch):
            kern_re, kern_im = kern_at(group * batch + step)
            for slot in range(2):
                at = (2 * step + slot) * freq_y
                wave_re, wave_im = waves_all[at : at + freq_y, :LANES], waves_all[at : at + freq_y, LANES:]
                sums[slot][0] += wave_re * kern_re + wave_im * kern_im
                sums[slot][1] += wave_im * kern_re - wave_re * kern_im
        for slot in range(2):
            slope_acc[slot, :freq_y] = sums[slot][0]
            slope_acc[slot, freq_y:] = sums[slot][1]
        return carry

    lax.fori_loop(0, kern_count // batch, backward, 0)

    for slot in range(MOST):
        top, rest = halves(slope_acc[slot])
        tall = mm(table("picks_t"), top) + mm(table("picks_t"), rest)
        wide = jnp.concatenate([tall[:ROWS], tall[ROWS:]], axis=1)
        both = mm(pair(wide), table("lanes_t"))
        packet = packed(both[:ROWS] + both[ROWS:], used)
        ready[0, slot] = packet[:split]
        ready[1, slot] = packet[split:]
    tiles = slopes_hbm.shape[0]
    copies = fetch([(ready.at[tile % 2], slopes_hbm.at[tile]) for tile in range(tiles)], sems)
    for copy in copies:
        copy.wait()


def owner_imaging(me, owner_list, kern_weight, packets, targets, other, kernels):
    kern_count, freq_y, freq_x = kernels.shape[2:]
    tiles, split = packets.shape[:2]
    core, rim, rows = image_tables(freq_y, freq_x)
    lanes, picks = pick_tables(freq_y, freq_x)

    def tall(table):
        return np.concatenate(halves_np(table), axis=0)

    def three(table):
        top, rest = halves_np(table)
        return np.concatenate([top, top, rest], axis=1)

    def square_up(table):
        top, rest = halves_np(table)
        return np.block([[top, top], [rest, np.zeros_like(rest)]])

    tables = {
        "core": tall(core),
        "core_t": tall(core.T),
        "rim": tall(rim),
        "rim_t": tall(rim.T),
        "rows": three(rows),
        "rows_t": square_up(rows.T),
        "lanes": lanes.astype(BF16),
        "lanes_t": lanes.T.astype(BF16),
        "picks": picks.astype(BF16),
        "picks_t": picks.T.astype(BF16),
        "turn": np.eye(GRID_Y // 2)[::-1].astype(BF16),
    }
    places, pieces, start = {}, [], 0
    for name, piece in tables.items():
        height, width = piece.shape
        places[name] = (start, height, width)
        pieces.append(np.pad(piece, ((0, 0), (0, 2 * LANES - width))))
        start += height
    half = GRID_Y // 2
    smem = pl.BlockSpec(memory_space=pltpu.SMEM)
    vmem = pl.BlockSpec(memory_space=pltpu.VMEM)
    hbm = pl.BlockSpec(memory_space=pltpu.HBM)
    return pl.pallas_call(
        functools.partial(imaging_kernel, places, freq_x + 1),
        in_specs=[smem, smem, smem, hbm, hbm] + [vmem] * 3,
        out_specs=(hbm, smem),
        out_shape=(
            jax.ShapeDtypeStruct((tiles, MOST, split, LANES), F32),
            jax.ShapeDtypeStruct((1,), F32),
        ),
        scratch_shapes=[
            pltpu.VMEM((MOST, 2 * freq_y, LANES), F32),
            pltpu.VMEM((MOST, kern_count, 4, half, LANES), F32),
            pltpu.VMEM((4, half, LANES), F32),
            pltpu.VMEM((MOST, freq_y, 2 * LANES), F32),
            pltpu.VMEM((MOST, freq_y, 2 * LANES), F32),
            pltpu.VMEM((MOST, 2 * freq_y, LANES), F32),
            pltpu.VMEM((MOST, 2, half, LANES), F32),
            pltpu.VMEM((2, MOST, split, LANES), F32),
            pltpu.VMEM((MOST,) + packets.shape[1:], F32),
            pltpu.VMEM((MOST,) + targets.shape[1:], F32),
            pltpu.SemaphoreType.DMA((tiles,)),
            pltpu.SemaphoreType.DMA((2 * MOST,)),
        ],
        compiler_params=pltpu.CompilerParams(vmem_limit_bytes=20 * 2**20),
        name="owner_imaging",
    )(
        me, owner_list, kern_weight, in_hbm(packets), in_hbm(targets), other, kernels,
        jnp.asarray(np.concatenate(pieces, axis=0)),
    )


def on_device(mask_tiles, target_grid, kernels, kern_weight, owner_list):
    tile_px = mask_tiles.shape[1]
    freq_y, freq_x = kernels.shape[3:]
    count = lax.axis_size("tile")
    cols, rows = mask_tables(tile_px, freq_y, freq_x)
    me = lax.axis_index("tile").astype(jnp.int32).reshape(1)
    mates = [(i, i + 1 - 2 * (i % 2)) for i in range(count)]
    seams = [(i, i - 1 + 2 * (i % 2)) for i in range(1, count - 1)]

    def spread(value):
        value = value.reshape(1, 2, -1, LANES)
        wide = jnp.broadcast_to(value, (count // 2,) + value.shape[1:])
        return lax.all_to_all(wide.reshape(count, -1, LANES), "tile", 0, 0, tiled=True)

    owner_list = owner_list.reshape(-1)
    targets = spread(target_grid)
    parts = mask_spectrum(me, mask_tiles, cols, rows, freq_y, freq_x)
    from_seam = lax.ppermute(parts[1], "tile", seams)
    from_mate = lax.ppermute(parts[2], "tile", mates)
    packet, targets = lax.optimization_barrier((parts[0] + from_seam + from_mate, targets))
    packets = spread(packet)
    other = lax.ppermute(owner_pick(me, owner_list, packets, targets), "tile", mates)
    slopes, owner_error = owner_imaging(me, owner_list, kern_weight, packets, targets, other, kernels)
    slopes = lax.all_to_all(slopes, "tile", 0, 0, tiled=True)
    other = lax.ppermute(tile_pick(me, owner_list, slopes), "tile", mates)
    current = mask_update(me, owner_list, slopes, other, mask_tiles, cols, rows, freq_x)
    return (current, owner_error)


def solution(mesh):
    placed = (
        P(("stripe", "tile"), None, None),
        P(("stripe", "tile"), None),
        P("tile", None, None, None, None),
        P(),
        P("stripe", None),
    )
    return jax.shard_map(
        on_device,
        mesh=mesh,
        in_specs=placed,
        out_specs=(P(("stripe", "tile"), None, None), P(("stripe", "tile"))),
        check_vma=False,
    )
```

```python
import functools

import jax
import jax.numpy as jnp
import numpy as np
from jax import lax
from jax.experimental import pallas as pl
from jax.experimental.pallas import tpu as pltpu
from jax.sharding import PartitionSpec as P

AMBIT = 256
GRID_X = 192
GRID_Y = 128
CORE_X = 128
RESIST_SLOPE = 3.0
RESIST_LEVEL = 1.2
DIFFUSE_RATE = 0.2
STEP_SIZE = 1.0

LANES = 128
MOST = 2
BLOCKS = 4
PIECES = 16
BATCH = 6
ROWS = 72
ROWS_PAD = 80
F32 = jnp.float32
BF16 = jnp.bfloat16


def halves_np(table):
    table = np.asarray(table, np.float32)
    top = table.astype(BF16)
    rest = (table - top.astype(np.float32)).astype(BF16)
    return top, rest


def halves(value):
    top = value.astype(BF16)
    rest = (value - top.astype(F32)).astype(BF16)
    return top, rest


def mm(left, right):
    return jnp.dot(left, right, preferred_element_type=F32)


def in_hbm(value):
    return pltpu.with_memory_space_constraint(jnp.asarray(value), pltpu.HBM)


def in_vmem(value):
    return pltpu.with_memory_space_constraint(jnp.asarray(value), pltpu.VMEM)


def real_waves(places, period, most, width):
    angles = 2.0 * np.pi * np.outer(places, np.arange(most + 1)) / period
    waves = np.concatenate([np.cos(angles), np.sin(angles[:, 1:])], axis=1)
    return np.pad(waves, ((0, 0), (0, width - waves.shape[1])))


def signed_picks(count, width):
    freqs = np.arange(count) - count // 2
    most = count // 2
    even = np.zeros((count, width))
    odd = np.zeros((count, width))
    for at, freq in enumerate(freqs):
        even[at, abs(freq)] = 1.0
        if freq != 0:
            odd[at, most + abs(freq)] = np.sign(freq)
    return even, odd


def mask_tables(tile_px, freq_y, freq_x):
    win = tile_px + 2 * AMBIT
    mid_x = (GRID_X - 1) / 2 * (win // GRID_X)
    mid_y = (GRID_Y - 1) / 2 * (tile_px // GRID_Y)
    cols = real_waves(np.arange(win) - mid_x, win, freq_x // 2, LANES)
    rows = real_waves(np.arange(tile_px) - mid_y, tile_px, freq_y // 2, ROWS_PAD)
    return cols, rows


def rim_marks(packet):
    row = lax.broadcasted_iota(jnp.int32, packet.shape, 0)
    lane = lax.broadcasted_iota(jnp.int32, packet.shape, 1)
    return lane, lax.rem(lane - row + LANES, packet.shape[0]) == 0


def packed(tall, used):
    body, line = tall[:-8], tall[-8:-7]
    rows = body.shape[0]
    lane, marked = rim_marks(body)
    line = jnp.where(marked & (lane < used), jnp.broadcast_to(line, body.shape), 0.0)
    one = jnp.sum(jnp.where(lane < rows, line, 0.0), axis=1, keepdims=True)
    two = jnp.sum(jnp.where(lane >= rows, line, 0.0), axis=1, keepdims=True)
    body = jnp.where(lane < used, body, 0.0)
    return jnp.where(lane == used, one, jnp.where(lane == used + 1, two, body))


def unpacked(packet, used):
    rows = packet.shape[0]
    lane, marked = rim_marks(packet)
    line = jnp.where(lane < rows, packet[:, used : used + 1], packet[:, used + 1 : used + 2])
    line = jnp.sum(jnp.where(marked & (lane < used), line, 0.0), axis=0, keepdims=True)
    body = jnp.where(lane < used, packet, 0.0)
    return jnp.concatenate([body, line, jnp.zeros((7, LANES), F32)], axis=0)


def fetch(pairs, sems):
    copies = [pltpu.make_async_copy(src, dst, sems.at[at]) for at, (src, dst) in enumerate(pairs)]
    for copy in copies:
        copy.start()
    return copies


def spectrum_kernel(used, mask_hbm, cols_hbm, rows_hbm, target_hbm, out_ref, mask, cols, rows, total, sems, target_sems):
    tile_px = mask.shape[0]
    block = tile_px // BLOCKS
    pairs = [(cols_hbm, cols), (rows_hbm, rows)]
    for at in range(BLOCKS):
        place = pl.ds(at * block, block)
        pairs.append((mask_hbm.at[0, place], mask.at[place]))
    copies = fetch(pairs, sems)
    size = target_hbm.shape[0] // PIECES
    goals = fetch(
        [(target_hbm.at[pl.ds(at * size, size)], out_ref.at[at, pl.ds(16, size)]) for at in range(PIECES)],
        target_sems,
    )
    copies[0].wait()
    copies[1].wait()

    def columns(top_part, rest_part, table):
        both = mm(top_part, table)
        return both[:, :LANES] + both[:, LANES:] + mm(rest_part, table[:, :LANES])

    for at in range(BLOCKS):
        copies[2 + at].wait()
        top, rest = halves(mask[at * block : (at + 1) * block])
        row_table = rows[:, at * block : (at + 1) * block]
        parts = (
            columns(top, rest, cols[AMBIT : AMBIT + tile_px]),
            columns(top[:, :AMBIT], rest[:, :AMBIT], cols[AMBIT + tile_px :]),
            columns(top[:, tile_px - AMBIT :], rest[:, tile_px - AMBIT :], cols[:AMBIT]),
        )
        for part, terms in enumerate(parts):
            piece = mm(row_table, jnp.concatenate(halves(terms), axis=1))
            if at == 0:
                total[part] = piece
            else:
                total[part] += piece

    def summed(part):
        whole = total[part]
        return packed(
            whole[:ROWS, :LANES] + whole[:ROWS, LANES:] + whole[ROWS_PAD : ROWS_PAD + ROWS, :LANES], used
        )

    for part in range(3):
        packet = summed(part)
        for at in range(PIECES):
            out_ref[at, 4 * part : 4 * part + 4] = packet[4 * at : 4 * at + 4]
    for copy in goals:
        copy.wait()


def mask_spectrum(mask_tiles, target, cols, rows, freq_x):
    tile_px = mask_tiles.shape[1]
    col_stack = np.concatenate(halves_np(cols), axis=1)
    row_stack = np.concatenate(halves_np(rows.T), axis=0)
    hbm = pl.BlockSpec(memory_space=pltpu.HBM)
    return pl.pallas_call(
        functools.partial(spectrum_kernel, freq_x + 1),
        in_specs=[hbm, hbm, hbm, hbm],
        out_specs=pl.BlockSpec(memory_space=pltpu.VMEM),
        out_shape=jax.ShapeDtypeStruct((PIECES, 24, LANES), F32),
        scratch_shapes=[
            pltpu.VMEM((tile_px, tile_px), F32),
            pltpu.VMEM(col_stack.shape, BF16),
            pltpu.VMEM(row_stack.shape, BF16),
            pltpu.VMEM((3, 2 * ROWS_PAD, 2 * LANES), F32),
            pltpu.SemaphoreType.DMA((2 + BLOCKS,)),
            pltpu.SemaphoreType.DMA((PIECES,)),
        ],
        compiler_params=pltpu.CompilerParams(vmem_limit_bytes=20 * 2**20),
        name="mask_spectrum",
    )(in_hbm(mask_tiles), in_hbm(col_stack), in_hbm(row_stack), in_hbm(target))


def slots_of(owner_ref, tiles):
    owners = [owner_ref[tile] for tile in tiles]

    def count(other, before):
        held = owner_ref[other]
        return tuple(
            seen + ((held == owner) & (other < tile)).astype(jnp.int32)
            for seen, owner, tile in zip(before, owners, tiles)
        )

    ranks = lax.fori_loop(0, owner_ref.shape[0], count, (jnp.int32(0),) * len(tiles))
    return list(zip(owners, ranks))


def tiles_of(owner_ref, owner):
    def find(tile, carry):
        count, first, second = carry
        mine = owner_ref[tile] == owner
        first = jnp.where(mine & (count == 0), tile, first)
        second = jnp.where(mine & (count == 1), tile, second)
        return count + mine.astype(jnp.int32), first, second

    zero = jnp.int32(0)
    return lax.fori_loop(0, owner_ref.shape[0], find, (zero, zero, zero))


def mate_of(me):
    return me + 1 - 2 * lax.rem(me, 2)


def route_kernel(me_ref, owner_ref, pieces_ref, *rest):
    edges_ref = rest[0] if len(rest) == 3 else None
    out_ref, seen = rest[-2:]
    tiles = owner_ref.shape[0]
    base = me_ref[0] // PIECES * PIECES

    def clear(at, carry):
        seen[at] = 0
        return carry

    lax.fori_loop(0, tiles, clear, 0)

    def send(tile, carry):
        owner = owner_ref[tile]
        slot = seen[owner]
        seen[owner] = slot + 1
        at = tile - base

        @pl.when((at >= 0) & (at < PIECES))
        def _():
            high = pieces_ref[jnp.maximum(at - 1, 0), 8:12]
            low = pieces_ref[jnp.minimum(at + 1, PIECES - 1), 4:8]
            if edges_ref is None:
                edge_high, edge_low = jnp.zeros_like(high), jnp.zeros_like(low)
            else:
                edge_high, edge_low = edges_ref[0, 8:12], edges_ref[1, 4:8]
            high = jnp.where(at > 0, high, edge_high)
            low = jnp.where(at < PIECES - 1, low, edge_low)
            packet = pieces_ref[at, :4] + high + low

            @pl.when(slot == 0)
            def _():
                out_ref[owner, :4] = packet
                out_ref[owner, 8:16] = pieces_ref[at, 16:]

            @pl.when(slot == 1)
            def _():
                out_ref[owner, 4:8] = packet
                out_ref[owner, 16:] = pieces_ref[at, 16:]

        return carry

    lax.fori_loop(0, tiles, send, 0)


def route(me, owner_list, pieces, edges):
    smem = pl.BlockSpec(memory_space=pltpu.SMEM)
    vmem = pl.BlockSpec(memory_space=pltpu.VMEM)
    tiles = owner_list.shape[0]
    extra = [] if edges is None else [edges]
    return pl.pallas_call(
        route_kernel,
        in_specs=[smem, smem, vmem] + [vmem] * len(extra),
        out_specs=vmem,
        out_shape=jax.ShapeDtypeStruct((tiles, 24, LANES), F32),
        scratch_shapes=[pltpu.SMEM((tiles,), jnp.int32)],
        compiler_params=pltpu.CompilerParams(vmem_limit_bytes=2**20),
        name="route",
    )(me, owner_list, in_vmem(pieces), *extra)


def around(tile, tiles):
    return [
        (tile, None),
        (jnp.maximum(tile - 1, 0), tile > 0),
        (jnp.minimum(tile + 1, tiles - 1), tile < tiles - 1),
    ]


def tile_pick_kernel(me_ref, owner_ref, slopes_ref, out_ref):
    tiles = [tile for tile, _ in around(mate_of(me_ref[0]), owner_ref.shape[0])]
    for at, (owner, slot) in enumerate(slots_of(owner_ref, tiles)):
        out_ref[at] = slopes_ref[owner, slot]


def tile_pick(me, owner_list, slopes):
    smem = pl.BlockSpec(memory_space=pltpu.SMEM)
    vmem = pl.BlockSpec(memory_space=pltpu.VMEM)
    return pl.pallas_call(
        tile_pick_kernel,
        in_specs=[smem, smem, vmem],
        out_specs=vmem,
        out_shape=jax.ShapeDtypeStruct((3,) + slopes.shape[2:], F32),
        compiler_params=pltpu.CompilerParams(vmem_limit_bytes=2**20),
        name="tile_pick",
    )(me, owner_list, in_vmem(slopes))


def joined(me, mine, other):
    odd = lax.rem(me, 2) == 1
    return jnp.concatenate([jnp.where(odd, other, mine), jnp.where(odd, mine, other)], axis=0)


def update_kernel(
    used, me_ref, owner_ref, slopes_ref, other_ref, mask_ref, cols, rows, out_hbm, out, held, out_sems
):
    tile_px = out.shape[0]
    block = tile_px // BLOCKS
    me = me_ref[0]
    near = around(me, owner_ref.shape[0])
    packets = []
    for at, (owner, slot) in enumerate(slots_of(owner_ref, [tile for tile, _ in near])):
        packet = unpacked(joined(me, slopes_ref[owner, slot], other_ref[at]), used)
        there = near[at][1]
        packets.append(packet if there is None else jnp.where(there, packet, 0.0))

    def spread(packet, table):
        top, rest = halves(packet)
        return mm(
            jnp.concatenate([top, rest, top], axis=1),
            jnp.concatenate([table[:LANES], table[:LANES], table[LANES:]], axis=0),
        )

    wide = spread(packets[0], cols[:, AMBIT : AMBIT + tile_px])
    left = spread(packets[1], cols[:, AMBIT + tile_px :])
    right = spread(packets[2], cols[:, :AMBIT])
    wide = jnp.concatenate(
        [
            wide[:, :AMBIT] + left,
            wide[:, AMBIT : tile_px - AMBIT],
            wide[:, tile_px - AMBIT :] + right,
        ],
        axis=1,
    )
    wide = jnp.concatenate([wide, jnp.zeros((ROWS_PAD - ROWS, tile_px), F32)], axis=0)
    top, rest = halves(wide)
    held[:ROWS_PAD] = top
    held[ROWS_PAD : 2 * ROWS_PAD] = rest
    held[2 * ROWS_PAD :] = top
    sent = []
    for at in range(BLOCKS):
        here = slice(at * block, (at + 1) * block)
        place = pl.ds(at * block, block)
        out[here] = mask_ref[0, here] - STEP_SIZE * mm(rows[here], held[...])
        copy = pltpu.make_async_copy(out.at[place], out_hbm.at[0, place], out_sems.at[at])
        copy.start()
        sent.append(copy)
    for copy in sent:
        copy.wait()


def mask_update(me, owner_list, slopes, other, mask_tiles, cols, rows, freq_x):
    tile_px = mask_tiles.shape[1]
    col_stack = np.concatenate(halves_np(cols.T), axis=0)
    top, rest = halves_np(rows)
    row_stack = np.concatenate([top, top, rest], axis=1)
    smem = pl.BlockSpec(memory_space=pltpu.SMEM)
    vmem = pl.BlockSpec(memory_space=pltpu.VMEM)
    hbm = pl.BlockSpec(memory_space=pltpu.HBM)
    return pl.pallas_call(
        functools.partial(update_kernel, freq_x + 1),
        in_specs=[smem, smem] + [vmem] * 5,
        out_specs=hbm,
        out_shape=jax.ShapeDtypeStruct(mask_tiles.shape, F32),
        scratch_shapes=[
            pltpu.VMEM((tile_px, tile_px), F32),
            pltpu.VMEM((3 * ROWS_PAD, tile_px), BF16),
            pltpu.SemaphoreType.DMA((BLOCKS,)),
        ],
        compiler_params=pltpu.CompilerParams(vmem_limit_bytes=16 * 2**20),
        name="mask_update",
    )(
        me, owner_list, in_vmem(slopes), other, in_vmem(mask_tiles), in_vmem(col_stack), in_vmem(row_stack)
    )


def image_tables(freq_y, freq_x):
    places_v = np.arange(GRID_X) - (GRID_X - 1) / 2
    freqs_b = np.arange(freq_x) - (freq_x - 1) / 2
    beta = 2.0 * np.pi * np.outer(freqs_b, places_v) / GRID_X
    first = (GRID_X - CORE_X) // 2

    def block(lane_of):
        table = np.zeros((2 * LANES, 2 * LANES))
        for place, lane in lane_of:
            table[:freq_x, lane] = np.cos(beta[:, place])
            table[:freq_x, LANES + lane] = np.sin(beta[:, place])
            table[LANES : LANES + freq_x, lane] = -np.sin(beta[:, place])
            table[LANES : LANES + freq_x, LANES + lane] = np.cos(beta[:, place])
        return table

    core = block([(first + lane, lane) for lane in range(CORE_X)])
    last = first + CORE_X
    rim = block(
        [(first - 2, LANES - 2), (first - 1, LANES - 1), (last, 0), (last + 1, 1)]
    )
    places_u = np.arange(GRID_Y // 2) + 0.5
    freqs_a = np.arange(freq_y) - (freq_y - 1) / 2
    alpha = 2.0 * np.pi * np.outer(places_u, freqs_a) / GRID_Y
    rows = np.concatenate([np.cos(alpha), np.sin(alpha)], axis=0)
    return core, rim, rows


def pick_tables(freq_y, freq_x):
    col_even, col_odd = signed_picks(freq_x, LANES)
    row_even, row_odd = signed_picks(freq_y, ROWS)
    lanes = np.zeros((LANES, 2 * LANES))
    lanes[:, :freq_x] = col_even.T
    lanes[:, LANES : LANES + freq_x] = col_odd.T
    rows = np.block([[row_even, -row_odd], [-row_odd, -row_even]])
    return lanes, rows


def imaging_kernel(
    places, used, me_ref, owner_ref, weight_ref, pieces_ref, kern_ref, table_ref,
    slopes_hbm, error_ref,
    spec, field, rim_field, rim_lanes, rim_slope, slope_acc, scale_ref, ready, sems,
):
    me = me_ref[0]
    kern_count, freq_y, freq_x = kern_ref.shape[2:]
    batch = max(size for size in range(1, BATCH + 1) if kern_count % size == 0)
    count, first, second = tiles_of(owner_ref, me)
    slots = (first, second)
    split = freq_y // 2
    firsts = [slot // PIECES * PIECES for slot in slots]

    def table(name):
        start, height, width = places[name]
        return table_ref[start : start + height, :width]

    def pair(value):
        top, rest = halves(value)
        return jnp.concatenate([top, rest], axis=0)

    for slot in range(MOST):
        packet = jnp.concatenate(
            [pieces_ref[firsts[slot] + at, 4 * slot : 4 * slot + 4] for at in range(PIECES)], axis=0
        )
        packet = jnp.where(slot < count, unpacked(packet, used), 0.0)
        both = mm(pair(packet), table("lanes"))
        both = both[:ROWS] + both[ROWS:]
        tall = jnp.concatenate([both[:, :LANES], both[:, LANES:]], axis=0)
        top, rest = halves(tall)
        spec[slot] = mm(table("picks"), top) + mm(table("picks"), rest)

    half = GRID_Y // 2
    lane = lax.broadcasted_iota(jnp.int32, (freq_y, LANES), 1)
    live_lane = lane < freq_x

    def kern_at(k):
        def one(part):
            raw = kern_ref[0, part, k]
            wide = jnp.concatenate([raw, jnp.zeros((freq_y, LANES - freq_x), F32)], axis=1)
            return wide
        return one(0), one(1)

    def to_image(stack):
        top, rest = halves(stack)
        return mm(table("rows"), jnp.concatenate([top, rest, top], axis=0))

    def from_image(stack):
        top, rest = halves(stack)
        both = mm(table("rows_t"), jnp.concatenate([top, rest], axis=0))
        return both[:freq_y] + both[freq_y:]

    def thrice(top, rest, name):
        both = table(name)
        height = both.shape[0] // 2
        return mm(
            jnp.concatenate([top, rest, top], axis=1),
            jnp.concatenate([both[:height], both[:height], both[height:]], axis=0),
        )

    def waves(stack):
        even_re, even_im = stack[:half, :LANES], stack[:half, LANES:]
        odd_re, odd_im = stack[half:, :LANES], stack[half:, LANES:]
        return even_re - odd_im, even_im + odd_re, even_re + odd_im, even_im - odd_re

    def unwaves(plus_re, plus_im, minus_re, minus_im):
        above = jnp.concatenate([plus_re + minus_re, plus_im + minus_im], axis=1)
        below = jnp.concatenate([plus_im - minus_im, minus_re - plus_re], axis=1)
        return jnp.concatenate([above, below], axis=0)

    rim_lanes[...] = jnp.zeros_like(rim_lanes)

    def forward(group, sums):
        tops, rests = [], []
        for step in range(batch):
            kern_re, kern_im = kern_at(group * batch + step)
            for slot in range(2):
                spec_re, spec_im = spec[slot, :freq_y], spec[slot, freq_y:]
                wave = jnp.concatenate(
                    [kern_re * spec_re - kern_im * spec_im, kern_re * spec_im + kern_im * spec_re], axis=1
                )
                top, rest = halves(wave)
                tops.append(top)
                rests.append(rest)
        top, rest = jnp.concatenate(tops, axis=0), jnp.concatenate(rests, axis=0)
        cols = thrice(top, rest, "core")
        edges = thrice(top, rest, "rim")
        new = list(sums)
        for step in range(batch):
            k = group * batch + step
            weight = weight_ref[k]
            for slot in range(2):
                at = (2 * step + slot) * freq_y
                edge = edges[at : at + freq_y]
                rim_lanes[slot, :, :LANES] += pltpu.roll(edge[:, :LANES], 4 * k, 1)
                rim_lanes[slot, :, LANES:] += pltpu.roll(edge[:, LANES:], 4 * k, 1)
                parts = waves(to_image(cols[at : at + freq_y]))
                for part in range(4):
                    field[slot, k, part] = parts[part]
                plus, minus = new[slot]
                plus = plus + weight * (parts[0] * parts[0] + parts[1] * parts[1])
                minus = minus + weight * (parts[2] * parts[2] + parts[3] * parts[3])
                new[slot] = (plus, minus)
        return tuple(new)

    blank = jnp.zeros((half, LANES), F32)
    sums = lax.fori_loop(0, kern_count // batch, forward, ((blank, blank), (blank, blank)))

    def set_scale(k, carry):
        lane_row = lax.broadcasted_iota(jnp.int32, (1, LANES), 1)
        group = lax.rem(lane_row + 2, LANES) // 4
        return jnp.where(group == k, weight_ref[k], carry)

    lane_weight = lax.fori_loop(0, kern_count, set_scale, jnp.zeros((1, LANES), F32))

    norm = 1.0 / (64.0 * GRID_Y * GRID_X)
    square = norm * norm
    lane_half = lax.broadcasted_iota(jnp.int32, (half, LANES), 1)
    row_half = lax.broadcasted_iota(jnp.int32, (half, 2 * LANES), 0)
    lane_wide = lax.broadcasted_iota(jnp.int32, (half, 2 * LANES), 1)
    near = (lane_half < 2) | (lane_half >= LANES - 2)
    inside = lane_wide < LANES

    def blur(plus, minus):
        def one(value, other):
            later = jnp.where(row_half == half - 1, value, pltpu.roll(value, half - 1, 0))
            sooner = jnp.where(row_half == 0, other, pltpu.roll(value, 1, 0))
            sides = pltpu.roll(value, 1, 1) + pltpu.roll(value, 2 * LANES - 1, 1)
            return value + DIFFUSE_RATE * (later + sooner + sides - 4.0 * value)
        return one(plus, minus), one(minus, plus)

    def fold(value):
        def back(amount):
            return pltpu.roll(value, LANES - amount, 1)
        value = value + back(48)
        value = value + back(24)
        value = value + back(12)
        return value + back(4) + back(8)

    def unfold(value):
        value = jnp.where(near, value, 0.0)
        value = value + pltpu.roll(value, 4, 1) + pltpu.roll(value, 8, 1)
        value = value + pltpu.roll(value, 12, 1)
        value = value + pltpu.roll(value, 24, 1)
        return value + pltpu.roll(value, 48, 1)

    error = jnp.float32(0.0)
    for slot in range(2):
        live = (slot < count).astype(F32)
        rim_parts = waves(to_image(rim_lanes[slot]))
        for part in range(4):
            rim_field[part] = rim_parts[part]
        weights = jnp.broadcast_to(lane_weight, (half, LANES))
        rim_plus = weights * (rim_parts[0] * rim_parts[0] + rim_parts[1] * rim_parts[1])
        rim_minus = weights * (rim_parts[2] * rim_parts[2] + rim_parts[3] * rim_parts[3])
        plus = jnp.concatenate([sums[slot][0], jnp.where(near, fold(rim_plus), 0.0)], axis=1) * square
        minus = jnp.concatenate([sums[slot][1], jnp.where(near, fold(rim_minus), 0.0)], axis=1) * square
        plus, minus = blur(*blur(plus, minus))
        target = jnp.concatenate(
            [pieces_ref[firsts[slot] + at, 8 + 8 * slot : 16 + 8 * slot] for at in range(PIECES)], axis=0
        )
        target = jnp.where(slot < count, target, 0.0)
        t_top = target[:half]
        one = t_top.astype(BF16)
        t_top = t_top - one.astype(F32)
        two = t_top.astype(BF16)
        three = (t_top - two.astype(F32)).astype(BF16)
        turned = mm(table("turn"), one) + mm(table("turn"), two) + mm(table("turn"), three)

        def slope_of(value, goal):
            resist = 1.0 / (1.0 + jnp.exp(-RESIST_SLOPE * (value[:, :LANES] - RESIST_LEVEL)))
            misfit = resist - goal
            slope = (2.0 * RESIST_SLOPE) * misfit * resist * (1.0 - resist)
            slope = jnp.concatenate([slope, jnp.zeros_like(slope)], axis=1)
            return slope, jnp.sum(misfit * misfit)

        slope_plus, err_plus = slope_of(plus, target[half:])
        slope_minus, err_minus = slope_of(minus, turned)
        error = error + live * (err_plus + err_minus)
        slope_plus, slope_minus = blur(*blur(slope_plus, slope_minus))
        factor = 2.0 * square
        scale_ref[slot, 0] = slope_plus[:, :LANES] * factor
        scale_ref[slot, 1] = slope_minus[:, :LANES] * factor
        rim_f_plus = unfold(slope_plus[:, LANES:] * factor) * weights
        rim_f_minus = unfold(slope_minus[:, LANES:] * factor) * weights
        rim_slope[slot] = from_image(
            unwaves(
                rim_f_plus * rim_field[0],
                rim_f_plus * rim_field[1],
                rim_f_minus * rim_field[2],
                rim_f_minus * rim_field[3],
            )
        )
    error_ref[0] = error * (1.0 / (GRID_Y * CORE_X))

    slope_acc[...] = jnp.zeros_like(slope_acc)
    rim_lane = (lane < 2) | (lane >= LANES - 2)

    def backward(group, carry):
        tops, rests, rim_tops, rim_rests = [], [], [], []
        for step in range(batch):
            k = group * batch + step
            weight = weight_ref[k]
            for slot in range(2):
                plus = scale_ref[slot, 0] * weight
                minus = scale_ref[slot, 1] * weight
                cols = from_image(
                    unwaves(
                        plus * field[slot, k, 0],
                        plus * field[slot, k, 1],
                        minus * field[slot, k, 2],
                        minus * field[slot, k, 3],
                    )
                )
                top, rest = halves(cols)
                tops.append(top)
                rests.append(rest)
                edge = jnp.concatenate(
                    [
                        pltpu.roll(rim_slope[slot, :, :LANES], LANES - 4 * k, 1),
                        pltpu.roll(rim_slope[slot, :, LANES:], LANES - 4 * k, 1),
                    ],
                    axis=1,
                )
                top, rest = halves(edge)
                rim_tops.append(top)
                rim_rests.append(rest)
        def stack(pieces):
            return jnp.concatenate(pieces, axis=0)
        waves_all = thrice(stack(tops), stack(rests), "core_t") + thrice(
            stack(rim_tops), stack(rim_rests), "rim_t"
        )
        sums = [[slope_acc[slot, :freq_y], slope_acc[slot, freq_y:]] for slot in range(2)]
        for step in range(batch):
            kern_re, kern_im = kern_at(group * batch + step)
            for slot in range(2):
                at = (2 * step + slot) * freq_y
                wave_re, wave_im = waves_all[at : at + freq_y, :LANES], waves_all[at : at + freq_y, LANES:]
                sums[slot][0] += wave_re * kern_re + wave_im * kern_im
                sums[slot][1] += wave_im * kern_re - wave_re * kern_im
        for slot in range(2):
            slope_acc[slot, :freq_y] = sums[slot][0]
            slope_acc[slot, freq_y:] = sums[slot][1]
        return carry

    lax.fori_loop(0, kern_count // batch, backward, 0)

    for slot in range(MOST):
        top, rest = halves(slope_acc[slot])
        tall = mm(table("picks_t"), top) + mm(table("picks_t"), rest)
        wide = jnp.concatenate([tall[:ROWS], tall[ROWS:]], axis=1)
        both = mm(pair(wide), table("lanes_t"))
        packet = packed(both[:ROWS] + both[ROWS:], used)
        ready[0, slot] = packet[:split]
        ready[1, slot] = packet[split:]
    tiles = slopes_hbm.shape[0]
    copies = fetch([(ready.at[tile % 2], slopes_hbm.at[tile]) for tile in range(tiles)], sems)
    for copy in copies:
        copy.wait()


def owner_imaging(me, owner_list, kern_weight, pieces, kernels):
    kern_count, freq_y, freq_x = kernels.shape[2:]
    tiles, split = owner_list.shape[0], freq_y // 2
    core, rim, rows = image_tables(freq_y, freq_x)
    lanes, picks = pick_tables(freq_y, freq_x)

    def tall(table):
        return np.concatenate(halves_np(table), axis=0)

    def three(table):
        top, rest = halves_np(table)
        return np.concatenate([top, top, rest], axis=1)

    def square_up(table):
        top, rest = halves_np(table)
        return np.block([[top, top], [rest, np.zeros_like(rest)]])

    tables = {
        "core": tall(core),
        "core_t": tall(core.T),
        "rim": tall(rim),
        "rim_t": tall(rim.T),
        "rows": three(rows),
        "rows_t": square_up(rows.T),
        "lanes": lanes.astype(BF16),
        "lanes_t": lanes.T.astype(BF16),
        "picks": picks.astype(BF16),
        "picks_t": picks.T.astype(BF16),
        "turn": np.eye(GRID_Y // 2)[::-1].astype(BF16),
    }
    places, stacked, start = {}, [], 0
    for name, piece in tables.items():
        height, width = piece.shape
        places[name] = (start, height, width)
        stacked.append(np.pad(piece, ((0, 0), (0, 2 * LANES - width))))
        start += height
    half = GRID_Y // 2
    smem = pl.BlockSpec(memory_space=pltpu.SMEM)
    vmem = pl.BlockSpec(memory_space=pltpu.VMEM)
    hbm = pl.BlockSpec(memory_space=pltpu.HBM)
    return pl.pallas_call(
        functools.partial(imaging_kernel, places, freq_x + 1),
        in_specs=[smem, smem, smem] + [vmem] * 3,
        out_specs=(hbm, smem),
        out_shape=(
            jax.ShapeDtypeStruct((tiles, MOST, split, LANES), F32),
            jax.ShapeDtypeStruct((1,), F32),
        ),
        scratch_shapes=[
            pltpu.VMEM((MOST, 2 * freq_y, LANES), F32),
            pltpu.VMEM((MOST, kern_count, 4, half, LANES), F32),
            pltpu.VMEM((4, half, LANES), F32),
            pltpu.VMEM((MOST, freq_y, 2 * LANES), F32),
            pltpu.VMEM((MOST, freq_y, 2 * LANES), F32),
            pltpu.VMEM((MOST, 2 * freq_y, LANES), F32),
            pltpu.VMEM((MOST, 2, half, LANES), F32),
            pltpu.VMEM((2, MOST, split, LANES), F32),
            pltpu.SemaphoreType.DMA((tiles,)),
        ],
        compiler_params=pltpu.CompilerParams(vmem_limit_bytes=20 * 2**20),
        name="owner_imaging",
    )(
        me, owner_list, kern_weight, in_vmem(pieces), in_vmem(kernels),
        in_vmem(np.concatenate(stacked, axis=0)),
    )


def on_device(mask_tiles, target_grid, kernels, kern_weight, owner_list):
    tile_px = mask_tiles.shape[1]
    freq_y, freq_x = kernels.shape[3:]
    count = lax.axis_size("tile")
    cols, rows = mask_tables(tile_px, freq_y, freq_x)
    me = lax.axis_index("tile").astype(jnp.int32).reshape(1)
    owner_list = owner_list.reshape(-1)
    mates = [(i, i + 1 - 2 * (i % 2)) for i in range(count)]

    pieces = mask_spectrum(mask_tiles, target_grid.reshape(GRID_Y, CORE_X), cols, rows, freq_x)
    if count == PIECES:
        pieces, edges = lax.all_to_all(pieces, "tile", 0, 0, tiled=True), None
    else:
        groups = [list(range(at, at + PIECES)) for at in range(0, count, PIECES)]
        pieces = lax.all_to_all(pieces, "tile", 0, 0, axis_index_groups=groups, tiled=True)
        later = [(i, i + PIECES) for i in range(count - PIECES)]
        sooner = [(i + PIECES, i) for i in range(count - PIECES)]
        edges = jnp.stack(
            [lax.ppermute(pieces[PIECES - 1], "tile", later), lax.ppermute(pieces[0], "tile", sooner)]
        )
    pieces = lax.all_to_all(route(me, owner_list, pieces, edges), "tile", 0, 0, tiled=True)
    slopes, owner_error = owner_imaging(me, owner_list, kern_weight, pieces, kernels)
    slopes = lax.all_to_all(slopes, "tile", 0, 0, tiled=True)
    other = lax.ppermute(tile_pick(me, owner_list, slopes), "tile", mates)
    current = mask_update(me, owner_list, slopes, other, mask_tiles, cols, rows, freq_x)
    return (current, owner_error)


def solution(mesh):
    placed = (
        P(("stripe", "tile"), None, None),
        P(("stripe", "tile"), None),
        P("tile", None, None, None, None),
        P(),
        P("stripe", None),
    )
    return jax.shard_map(
        on_device,
        mesh=mesh,
        in_specs=placed,
        out_specs=(P(("stripe", "tile"), None, None), P(("stripe", "tile"))),
        check_vma=False,
    )
```

```python
import functools

import jax
import jax.numpy as jnp
import numpy as np
from jax import lax
from jax.experimental import pallas as pl
from jax.experimental.pallas import tpu as pltpu
from jax.sharding import PartitionSpec as P

AMBIT = 256
GRID_X = 192
GRID_Y = 128
CORE_X = 128
RESIST_SLOPE = 3.0
RESIST_LEVEL = 1.2
DIFFUSE_RATE = 0.2
STEP_SIZE = 1.0

LANES = 128
MOST = 2
BLOCKS = 4
PIECES = 16
BATCH = 12
WIDE = 8
RIM_WIDTH = 16
RIM_KERNS = LANES // RIM_WIDTH
ROWS = 72
ROWS_PAD = 80
F32 = jnp.float32
BF16 = jnp.bfloat16


def halves_np(table):
    table = np.asarray(table, np.float32)
    top = table.astype(BF16)
    rest = (table - top.astype(np.float32)).astype(BF16)
    return top, rest


def halves(value):
    top = value.astype(BF16)
    rest = (value - top.astype(F32)).astype(BF16)
    return top, rest


def mm(left, right):
    return jnp.dot(left, right, preferred_element_type=F32)


def in_hbm(value):
    return pltpu.with_memory_space_constraint(jnp.asarray(value), pltpu.HBM)


def in_vmem(value):
    return pltpu.with_memory_space_constraint(jnp.asarray(value), pltpu.VMEM)


def real_waves(places, period, most, width):
    angles = 2.0 * np.pi * np.outer(places, np.arange(most + 1)) / period
    waves = np.concatenate([np.cos(angles), np.sin(angles[:, 1:])], axis=1)
    return np.pad(waves, ((0, 0), (0, width - waves.shape[1])))


def signed_picks(count, width):
    freqs = np.arange(count) - count // 2
    most = count // 2
    even = np.zeros((count, width))
    odd = np.zeros((count, width))
    for at, freq in enumerate(freqs):
        even[at, abs(freq)] = 1.0
        if freq != 0:
            odd[at, most + abs(freq)] = np.sign(freq)
    return even, odd


def mask_tables(tile_px, freq_y, freq_x):
    win = tile_px + 2 * AMBIT
    mid_x = (GRID_X - 1) / 2 * (win // GRID_X)
    mid_y = (GRID_Y - 1) / 2 * (tile_px // GRID_Y)
    most = freq_x // 2
    cols = real_waves(np.arange(AMBIT), win, most, LANES)
    rows = real_waves(np.arange(tile_px) - mid_y, tile_px, freq_y // 2, ROWS_PAD)
    blocks = win // AMBIT
    angles = 2.0 * np.pi * np.outer(AMBIT * np.arange(blocks) - mid_x, np.arange(most + 1)) / win
    turns = np.zeros((2, blocks, LANES))
    turns[0, :, : most + 1] = np.cos(angles)
    turns[0, :, most + 1 : 2 * most + 1] = np.cos(angles[:, 1:])
    turns[1, :, : most + 1] = -np.sin(angles)
    turns[1, :, most + 1 : 2 * most + 1] = np.sin(angles[:, 1:])
    return cols, turns.astype(np.float32).reshape(2 * blocks, 1, LANES), rows


def swapped(value, used):
    lane = lax.broadcasted_iota(jnp.int32, value.shape, 1)
    most = (used - 1) // 2
    return jnp.where(lane <= most, pltpu.roll(value, LANES - most, 1), pltpu.roll(value, most, 1))


def packed(tall, used):
    rows = tall.shape[0] - 8
    body, line = tall[:rows], jnp.broadcast_to(tall[rows : rows + 1], (8, LANES))
    lane = lax.broadcasted_iota(jnp.int32, (8, LANES), 1)
    row = lax.broadcasted_iota(jnp.int32, (8, LANES), 0)
    spare = LANES - used
    first = jnp.where(lane < used, body[:8], 0.0)
    for at in range(-(-used // spare)):
        moved = pltpu.roll(line, (used - spare * at) % LANES, 1)
        first = jnp.where((row == at) & (lane >= used), moved, first)
    return jnp.concatenate([first, body[8:]], axis=0)


def unpacked(packet, used):
    lane = lax.broadcasted_iota(jnp.int32, packet.shape, 1)
    first = packet[:8]
    lane8 = lane[:8]
    row = lax.broadcasted_iota(jnp.int32, (8, LANES), 0)
    spare = LANES - used
    line = jnp.zeros((8, LANES), F32)
    for at in range(-(-used // spare)):
        moved = pltpu.roll(first, (spare * at - used) % LANES, 1)
        here = (row == at) & (lane8 >= spare * at) & (lane8 < min(spare * at + spare, used))
        line = line + jnp.where(here, moved, 0.0)
    line = jnp.where(row == 0, jnp.sum(line, axis=0, keepdims=True), 0.0)
    return jnp.concatenate([jnp.where(lane < used, packet, 0.0), line], axis=0)


def own_place():
    return lax.axis_index("tile").astype(jnp.int32)


def fetch(pairs, sems):
    copies = [pltpu.make_async_copy(src, dst, sems.at[at]) for at, (src, dst) in enumerate(pairs)]
    for copy in copies:
        copy.start()
    return copies


def spectrum_kernel(
    used, mask_hbm, cols_hbm, turns_hbm, rows_hbm, target_hbm, out_ref, mask, cols, turns, rows, sems, target_sems
):
    tile_px = mask.shape[0]
    width = AMBIT
    count = tile_px // width
    pairs = [(rows_hbm, rows)]
    for at in range(count):
        place = pl.ds(at * width, width)
        pairs.append((mask_hbm.at[0, :, place], mask.at[:, place]))
    pairs[2:2] = [(cols_hbm, cols), (turns_hbm, turns)]
    copies = fetch(pairs, sems)
    table_copies = [copies.pop(2), copies.pop(2)]
    size = target_hbm.shape[0] // PIECES
    goals = fetch(
        [(target_hbm.at[pl.ds(at * size, size)], out_ref.at[at, pl.ds(16, size)]) for at in range(PIECES)],
        target_sems,
    )

    def turned(both, block):
        return turns[block] * both[0] + turns[block + turns.shape[0] // 2] * both[1]

    copies[0].wait()
    own = None
    for at in range(count):
        copies[1 + at].wait()
        top, rest = halves(mask[:, at * width : (at + 1) * width])
        both = mm(rows[...], top)
        top, rest = halves(both[:ROWS_PAD] + both[ROWS_PAD:] + mm(rows[:ROWS_PAD], rest))
        if at == 0:
            for copy in table_copies:
                copy.wait()
        waves = mm(
            jnp.concatenate([top, rest, top], axis=1),
            jnp.concatenate([cols[:, :LANES], cols[:, :LANES], cols[:, LANES:]], axis=0),
        )
        both = (waves, swapped(waves, used))
        if at == 0:
            low = turned(both, count + 1)
        if at == count - 1:
            high = turned(both, 0)
        piece = turned(both, at + 1)
        own = piece if own is None else own + piece

    own, low, high = [packed(part[:ROWS], used) for part in (own, low, high)]
    groups = own.shape[0] // 8
    low = pltpu.roll(low.reshape(groups, 8, LANES), 4, 1)
    upper = lax.broadcasted_iota(jnp.int32, (8, LANES), 0) < 4
    for at in range(groups):
        mine, other = own[8 * at : 8 * at + 8], low[at]
        out_ref[2 * at, :8] = jnp.where(upper, mine, other)
        out_ref[2 * at + 1, :8] = jnp.where(upper, other, mine)
        out_ref[2 * at, 8:16] = high[8 * at : 8 * at + 8]
        out_ref[2 * at + 1, 8:16] = high[8 * at : 8 * at + 8]
    for copy in goals:
        copy.wait()


def mask_spectrum(mask_tiles, target, cols, turns, rows, freq_x):
    tile_px = mask_tiles.shape[1]
    col_stack = np.concatenate(halves_np(cols), axis=1)
    row_stack = np.concatenate(halves_np(rows.T), axis=0)
    hbm = pl.BlockSpec(memory_space=pltpu.HBM)
    return pl.pallas_call(
        functools.partial(spectrum_kernel, freq_x + 1),
        in_specs=[hbm] * 5,
        out_specs=pl.BlockSpec(memory_space=pltpu.VMEM),
        out_shape=jax.ShapeDtypeStruct((PIECES, 24, LANES), F32),
        scratch_shapes=[
            pltpu.VMEM((tile_px, tile_px), F32),
            pltpu.VMEM(col_stack.shape, BF16),
            pltpu.VMEM(turns.shape, F32),
            pltpu.VMEM(row_stack.shape, BF16),
            pltpu.SemaphoreType.DMA((3 + tile_px // AMBIT,)),
            pltpu.SemaphoreType.DMA((PIECES,)),
        ],
        compiler_params=pltpu.CompilerParams(vmem_limit_bytes=20 * 2**20),
        name="mask_spectrum",
    )(in_hbm(mask_tiles), in_hbm(col_stack), in_hbm(turns), in_hbm(row_stack), in_hbm(target))


def slot_pair(first, second, used):
    spare = LANES - used
    lane = lax.broadcasted_iota(jnp.int32, (8, LANES), 1)
    groups = [part[at : at + 8] for part in (first, second) for at in range(0, part.shape[0], 8)]
    last = groups.pop()
    for at, host in enumerate((1, 2, 3, 5)):
        groups[host] = jnp.where(lane < used, groups[host], pltpu.roll(last, (used - spare * at) % LANES, 1))
    return jnp.concatenate(groups, axis=0)


def slot_half(pair, slot, used):
    spare = LANES - used
    lane = lax.broadcasted_iota(jnp.int32, (8, LANES), 1)
    last = jnp.zeros((8, LANES), F32)
    for at, host in enumerate((1, 2, 3, 5)):
        moved = pltpu.roll(pair[8 * host : 8 * host + 8], (spare * at - used) % LANES, 1)
        last = jnp.where((lane >= spare * at) & (lane < min(spare * at + spare, used)), moved, last)
    return jnp.where(slot == 0, pair[:32], jnp.concatenate([pair[32:], last], axis=0))


def slots_of(owner_ref, tiles):
    owners = [owner_ref[tile] for tile in tiles]

    def count(other, before):
        held = owner_ref[other]
        return tuple(
            seen + ((held == owner) & (other < tile)).astype(jnp.int32)
            for seen, owner, tile in zip(before, owners, tiles)
        )

    ranks = lax.fori_loop(0, owner_ref.shape[0], count, (jnp.int32(0),) * len(tiles))
    return list(zip(owners, ranks))


def tiles_of(owner_ref, owner):
    def find(tile, carry):
        count, first, second = carry
        mine = owner_ref[tile] == owner
        first = jnp.where(mine & (count == 0), tile, first)
        second = jnp.where(mine & (count == 1), tile, second)
        return count + mine.astype(jnp.int32), first, second

    zero = jnp.int32(0)
    return lax.fori_loop(0, owner_ref.shape[0], find, (zero, zero, zero))


def mate_of(me):
    return me + 1 - 2 * lax.rem(me, 2)


def route_kernel(owner_ref, pieces_ref, *rest):
    edges_ref = rest[0] if len(rest) == 3 else None
    out_ref, seen = rest[-2:]
    tiles = owner_ref.shape[0]
    me = own_place()
    base = me // PIECES * PIECES
    row = lax.broadcasted_iota(jnp.int32, (8, LANES), 0)
    mine = row // 4 == lax.rem(me, 2)

    def clear(at, carry):
        seen[at] = 0
        return carry

    lax.fori_loop(0, tiles, clear, 0)

    def send(tile, carry):
        owner = owner_ref[tile]
        slot = seen[owner]
        seen[owner] = slot + 1
        at = tile - base

        @pl.when((at >= 0) & (at < PIECES))
        def _():
            high = pieces_ref[jnp.maximum(at - 1, 0), 8:16]
            low = pieces_ref[jnp.minimum(at + 1, PIECES - 1), :8]
            if edges_ref is None:
                edge_high, edge_low = jnp.zeros_like(high), jnp.zeros_like(low)
            else:
                edge_high, edge_low = edges_ref[0, 8:16], edges_ref[1, :8]
            high = jnp.where(at > 0, high, edge_high)
            low = jnp.where(at < PIECES - 1, low, edge_low)
            packet = pieces_ref[at, :8] + high + pltpu.roll(low, 4, 0)
            beside = jnp.where(mine, out_ref[owner, :8], pltpu.roll(packet, 4, 0))
            out_ref[owner, :8] = jnp.where(slot == 0, packet, beside)
            out_ref[owner, pl.ds(pl.multiple_of(8 + 8 * slot, 8), 8)] = pieces_ref[at, 16:]

        return carry

    lax.fori_loop(0, tiles, send, 0)


def route(owner_list, pieces, edges):
    smem = pl.BlockSpec(memory_space=pltpu.SMEM)
    vmem = pl.BlockSpec(memory_space=pltpu.VMEM)
    tiles = owner_list.shape[0]
    extra = [] if edges is None else [edges]
    return pl.pallas_call(
        route_kernel,
        in_specs=[smem, vmem] + [vmem] * len(extra),
        out_specs=vmem,
        out_shape=jax.ShapeDtypeStruct((tiles, 24, LANES), F32),
        scratch_shapes=[pltpu.SMEM((tiles,), jnp.int32)],
        compiler_params=pltpu.CompilerParams(vmem_limit_bytes=2**20),
        name="route",
    )(owner_list, in_vmem(pieces), *extra)


def around(tile, tiles):
    return [
        (tile, None),
        (jnp.maximum(tile - 1, 0), tile > 0),
        (jnp.minimum(tile + 1, tiles - 1), tile < tiles - 1),
    ]


def tile_pick_kernel(used, owner_ref, slopes_ref, out_ref):
    tiles = [tile for tile, _ in around(mate_of(own_place()), owner_ref.shape[0])]
    for at, (owner, slot) in enumerate(slots_of(owner_ref, tiles)):
        out_ref[at] = slot_half(slopes_ref[owner], slot, used)


def tile_pick(owner_list, slopes, freq_x):
    smem = pl.BlockSpec(memory_space=pltpu.SMEM)
    vmem = pl.BlockSpec(memory_space=pltpu.VMEM)
    return pl.pallas_call(
        functools.partial(tile_pick_kernel, freq_x + 1),
        in_specs=[smem, vmem],
        out_specs=vmem,
        out_shape=jax.ShapeDtypeStruct((3, 32, LANES), F32),
        compiler_params=pltpu.CompilerParams(vmem_limit_bytes=2**20),
        name="tile_pick",
    )(owner_list, in_vmem(slopes))


def joined(me, mine, other):
    odd = lax.rem(me, 2) == 1
    return jnp.concatenate([jnp.where(odd, other, mine), jnp.where(odd, mine, other)], axis=0)


def update_kernel(
    used, owner_ref, slopes_ref, other_ref, mask_ref, cols, turns, rows, out_hbm, out, held, out_sems
):
    tile_px = out.shape[0]
    block = tile_px // BLOCKS
    me = own_place()
    near = around(me, owner_ref.shape[0])
    packets = []
    for at, (owner, slot) in enumerate(slots_of(owner_ref, [tile for tile, _ in near])):
        packet = unpacked(joined(me, slot_half(slopes_ref[owner], slot, used), other_ref[at]), used)
        there = near[at][1]
        packets.append(packet if there is None else jnp.where(there, packet, 0.0))

    own, last, following = [(packet, swapped(packet, used)) for packet in packets]

    def turned_back(both, block):
        return turns[block] * both[0] - turns[block + turns.shape[0] // 2] * both[1]

    count = tile_px // AMBIT
    waves = [turned_back(own, at + 1) for at in range(count)]
    waves[0] = waves[0] + turned_back(last, count + 1)
    waves[-1] = waves[-1] + turned_back(following, 0)
    blank = jnp.zeros((ROWS_PAD - ROWS, LANES), F32)
    top, rest = halves(jnp.concatenate([part for wave in waves for part in (wave, blank)], axis=0))
    wide = mm(
        jnp.concatenate([top, rest, top], axis=1),
        jnp.concatenate([cols[:LANES], cols[:LANES], cols[LANES:]], axis=0),
    )
    for at in range(count):
        top, rest = halves(wide[at * ROWS_PAD : (at + 1) * ROWS_PAD])
        held[:, at * AMBIT : (at + 1) * AMBIT] = jnp.concatenate([top, rest, top], axis=0)
    sent = []
    for at in range(BLOCKS):
        here = slice(at * block, (at + 1) * block)
        place = pl.ds(at * block, block)
        out[here] = mask_ref[0, here] - STEP_SIZE * mm(rows[here], held[...])
        copy = pltpu.make_async_copy(out.at[place], out_hbm.at[0, place], out_sems.at[at])
        copy.start()
        sent.append(copy)
    for copy in sent:
        copy.wait()


def update_tables(cols, turns, rows):
    top, rest = halves_np(rows)
    return (
        np.concatenate(halves_np(cols.T), axis=0),
        turns,
        np.concatenate([top, top, rest], axis=1),
    )


def mask_update(owner_list, slopes, other, mask_tiles, cols, turns, rows, freq_x):
    tile_px = mask_tiles.shape[1]
    smem = pl.BlockSpec(memory_space=pltpu.SMEM)
    vmem = pl.BlockSpec(memory_space=pltpu.VMEM)
    hbm = pl.BlockSpec(memory_space=pltpu.HBM)
    return pl.pallas_call(
        functools.partial(update_kernel, freq_x + 1),
        in_specs=[smem] + [vmem] * 6,
        out_specs=hbm,
        out_shape=jax.ShapeDtypeStruct(mask_tiles.shape, F32),
        scratch_shapes=[
            pltpu.VMEM((tile_px, tile_px), F32),
            pltpu.VMEM((3 * ROWS_PAD, tile_px), BF16),
            pltpu.SemaphoreType.DMA((BLOCKS,)),
        ],
        compiler_params=pltpu.CompilerParams(vmem_limit_bytes=16 * 2**20),
        name="mask_update",
    )(
        owner_list, in_vmem(slopes), other, in_vmem(mask_tiles),
        in_vmem(cols), in_vmem(turns), in_vmem(rows),
    )


def half_order():
    return np.arange(GRID_Y // 2).reshape(8, -1).T.reshape(-1)


def image_tables(freq_y, freq_x):
    places_v = np.arange(GRID_X) - (GRID_X - 1) / 2
    freqs_b = np.arange(freq_x) - (freq_x - 1) / 2
    beta = 2.0 * np.pi * np.outer(freqs_b, places_v) / GRID_X
    first = (GRID_X - CORE_X) // 2

    def block(lane_of):
        table = np.zeros((2 * LANES, 2 * LANES))
        for place, lane in lane_of:
            table[:freq_x, lane] = np.cos(beta[:, place])
            table[:freq_x, LANES + lane] = np.sin(beta[:, place])
            table[LANES : LANES + freq_x, lane] = -np.sin(beta[:, place])
            table[LANES : LANES + freq_x, LANES + lane] = np.cos(beta[:, place])
        return table

    core = block([(first + lane, lane) for lane in range(CORE_X)])
    last = first + CORE_X
    rim = block(
        [(first - 2, LANES - 2), (first - 1, LANES - 1), (last, 0), (last + 1, 1)]
    )
    places_u = half_order() + 0.5
    freqs_a = np.arange(freq_y) - (freq_y - 1) / 2
    alpha = 2.0 * np.pi * np.outer(places_u, freqs_a) / GRID_Y
    rows = np.concatenate([np.cos(alpha), np.sin(alpha)], axis=0)
    return core, rim, rows


def rim_tables(rim, kern_count):
    seats = [(LANES - 2 + at) % LANES for at in range(4)]
    seats = seats + [LANES + seat for seat in seats]
    top, rest = halves_np(rim.T[seats])
    blank = np.zeros((LANES - 8, 2 * LANES), BF16)
    rim_out = np.concatenate([top, top, blank[8:], rest, blank], axis=0)
    width = -(-kern_count * RIM_WIDTH // LANES) * LANES
    scatter = np.zeros((4 * LANES, width))
    for kern in range(kern_count):
        for at in range(8):
            lane = (4 * kern - 2 + at % 4) % LANES + at // 4 * LANES
            scatter[lane, kern * RIM_WIDTH + at] = 1.0
            scatter[2 * LANES + lane, kern * RIM_WIDTH + 8 + at] = 1.0
    return rim_out, scatter.astype(BF16)


def pick_tables(freq_y, freq_x):
    col_even, col_odd = signed_picks(freq_x, LANES)
    row_even, row_odd = signed_picks(freq_y, ROWS)
    lanes = np.zeros((LANES, 2 * LANES))
    lanes[:, :freq_x] = col_even.T
    lanes[:, LANES : LANES + freq_x] = col_odd.T
    rows = np.block([[row_even, -row_odd], [-row_odd, -row_even]])
    return lanes, rows


def imaging_kernel(places, used, extra, *refs):
    owner_ref, weight_ref, pieces_ref, kern_ref, table_ref = refs[:5]
    later_hbm, refs = refs[5 : 5 + extra], refs[5 + extra :]
    slopes_ref, error_ref, later_ref, refs = refs[0], refs[1], refs[2 : 2 + extra], refs[2 + extra :]
    spec, field, rim_field, rim_lanes, rim_slope, slope_acc, scale_ref, ready, goal_ref, sems = refs
    kern_count, freq_y, freq_x = kern_ref.shape[2:]
    later = fetch(list(zip(later_hbm, later_ref)), sems)
    batch = max(size for size in range(1, BATCH + 1) if kern_count % size == 0)
    count, first, second = tiles_of(owner_ref, own_place())
    slots = (first, second)
    split = freq_y // 2
    firsts = [slot // PIECES * PIECES for slot in slots]

    def table(name):
        start, height, width = places[name]
        return table_ref[start : start + height, :width]

    def pair(value):
        top, rest = halves(value)
        return jnp.concatenate([top, rest], axis=0)

    upper = lax.broadcasted_iota(jnp.int32, (8, LANES), 0) < 4
    for slot in range(MOST):
        target = jnp.concatenate(
            [pieces_ref[firsts[slot] + at, 8 + 8 * slot : 16 + 8 * slot] for at in range(PIECES)], axis=0
        )
        target = jnp.where(slot < count, target, 0.0)
        one = target.astype(BF16)
        target = target - one.astype(F32)
        two = target.astype(BF16)
        three = (target - two.astype(F32)).astype(BF16)
        goal_ref[slot] = mm(table("turn"), one) + mm(table("turn"), two) + mm(table("turn"), three)
        pieces = []
        for at in range(0, PIECES, 2):
            even, odd = pieces_ref[firsts[slot] + at, :8], pieces_ref[firsts[slot] + at + 1, :8]
            if slot == 0:
                pieces.append(jnp.where(upper, even, odd))
            else:
                pieces.append(pltpu.roll(jnp.where(upper, odd, even), 4, 0))
        packet = jnp.concatenate(pieces, axis=0)
        packet = jnp.where(slot < count, unpacked(packet, used), 0.0)
        both = mm(pair(packet), table("lanes"))
        both = both[:ROWS] + both[ROWS:]
        tall = jnp.concatenate([both[:, :LANES], both[:, LANES:]], axis=0)
        top, rest = halves(tall)
        spec[slot] = mm(table("picks"), top) + mm(table("picks"), rest)

    half = GRID_Y // 2
    lane = lax.broadcasted_iota(jnp.int32, (freq_y, LANES), 1)
    live_lane = lane < freq_x

    def kern_at(k):
        def one(part):
            raw = kern_ref[0, part, k]
            wide = jnp.concatenate([raw, jnp.zeros((freq_y, LANES - freq_x), F32)], axis=1)
            return wide
        return one(0), one(1)

    def side_by_side(pieces):
        return pieces[0] if len(pieces) == 1 else jnp.concatenate(pieces, axis=1)

    def apart(wide):
        size = 2 * LANES
        return [wide[:, at : at + size] for at in range(0, wide.shape[1], size)]

    def to_image(stacks):
        pieces = []
        for stack in stacks:
            top, rest = halves(stack)
            pieces.append(jnp.concatenate([top, rest, top], axis=0))
        return apart(mm(table("rows"), side_by_side(pieces)))

    def from_image(stacks):
        pieces = [jnp.concatenate(halves(stack), axis=0) for stack in stacks]
        both = mm(table("rows_t"), side_by_side(pieces))
        return apart(both[:freq_y] + both[freq_y:])

    def thrice(top, rest, name):
        both = table(name)
        height = both.shape[0] // 2
        return mm(
            jnp.concatenate([top, rest, top], axis=1),
            jnp.concatenate([both[:height], both[:height], both[height:]], axis=0),
        )

    def waves(stack):
        even_re, even_im = stack[:half, :LANES], stack[:half, LANES:]
        odd_re, odd_im = stack[half:, :LANES], stack[half:, LANES:]
        return even_re - odd_im, even_im + odd_re, even_re + odd_im, even_im - odd_re

    def unwaves(plus_re, plus_im, minus_re, minus_im):
        above = jnp.concatenate([plus_re + minus_re, plus_im + minus_im], axis=1)
        below = jnp.concatenate([plus_im - minus_im, minus_re - plus_re], axis=1)
        return jnp.concatenate([above, below], axis=0)

    rim_lanes[...] = jnp.zeros_like(rim_lanes)

    def forward(group, sums):
        tops, rests = [], []
        for step in range(batch):
            kern_re, kern_im = kern_at(group * batch + step)
            for slot in range(2):
                spec_re, spec_im = spec[slot, :freq_y], spec[slot, freq_y:]
                wave = jnp.concatenate(
                    [kern_re * spec_re - kern_im * spec_im, kern_re * spec_im + kern_im * spec_re], axis=1
                )
                top, rest = halves(wave)
                tops.append(top)
                rests.append(rest)
        top, rest = jnp.concatenate(tops, axis=0), jnp.concatenate(rests, axis=0)
        cols = thrice(top, rest, "core")
        edges = thrice(top, rest, "rim")
        new = list(sums)
        for step in range(batch):
            k = group * batch + step
            weight = weight_ref[k]
            new[2] = jnp.where(group_of == k, weight, new[2])
            for slot in range(2):
                at = (2 * step + slot) * freq_y
                edge = edges[at : at + freq_y]
                rim_lanes[slot, :, :LANES] += pltpu.roll(edge[:, :LANES], 4 * k, 1)
                rim_lanes[slot, :, LANES:] += pltpu.roll(edge[:, LANES:], 4 * k, 1)
                if at // freq_y % WIDE == 0:
                    images = to_image([cols[at + near * freq_y : at + (near + 1) * freq_y] for near in range(WIDE)])
                parts = waves(images[at // freq_y % WIDE])
                for part in range(4):
                    field[slot, k, part] = parts[part]
                plus, minus = new[slot]
                plus = plus + weight * (parts[0] * parts[0] + parts[1] * parts[1])
                minus = minus + weight * (parts[2] * parts[2] + parts[3] * parts[3])
                new[slot] = (plus, minus)
        return tuple(new)

    blank = jnp.zeros((half, LANES), F32)
    group_of = lax.rem(lax.broadcasted_iota(jnp.int32, (8, LANES), 1) + 2, LANES) // 4
    *sums, lane_weight = lax.fori_loop(
        0, kern_count // batch, forward, ((blank, blank), (blank, blank), jnp.zeros((8, LANES), F32))
    )

    norm = 1.0 / (64.0 * GRID_Y * GRID_X)
    square = norm * norm
    lane_half = lax.broadcasted_iota(jnp.int32, (half, LANES), 1)
    near = (lane_half < 2) | (lane_half >= LANES - 2)
    row_8 = lax.broadcasted_iota(jnp.int32, (8, LANES), 0)

    def rows_beside(value, other):
        first, last = value[:8], value[half - 8 :]
        later = jnp.where(row_8 == 7, last, pltpu.roll(first, 7, 0))
        sooner = jnp.where(row_8 == 0, other[:8], pltpu.roll(last, 1, 0))
        return jnp.concatenate([value[8:], later], axis=0) + jnp.concatenate([sooner, value[:-8]], axis=0)

    at_first, at_last = lane_half == 0, lane_half == LANES - 1

    def spread_out(value, rows, left, right):
        return value + DIFFUSE_RATE * (rows + left + right - 4.0 * value)

    def sides(value):
        return pltpu.roll(value, 1, 1), pltpu.roll(value, LANES - 1, 1)

    def beside(core, rim):
        return jnp.where(at_first, rim[0], core[0]), jnp.where(at_last, rim[1], core[1])

    def blur(core, rim):
        core_sides = [sides(value) for value in core]
        rim_sides = [sides(value) for value in rim]
        rim_one = [
            spread_out(rim[at], rows_beside(rim[at], rim[1 - at]), *beside(rim_sides[at], core_sides[at]))
            for at in range(2)
        ]
        core_one = [
            spread_out(core[at], rows_beside(core[at], core[1 - at]), *beside(core_sides[at], rim_sides[at]))
            for at in range(2)
        ]
        return [
            spread_out(
                core_one[at],
                rows_beside(core_one[at], core_one[1 - at]),
                *beside(sides(core_one[at]), sides(rim_one[at])),
            )
            for at in range(2)
        ]

    def blur_back(core):
        core_sides = [sides(value) for value in core]
        none = jnp.zeros((half, LANES), F32)
        rim_one = [DIFFUSE_RATE * sum(beside((none, none), core_sides[at])) for at in range(2)]
        core_one = [
            spread_out(core[at], rows_beside(core[at], core[1 - at]), *beside(core_sides[at], (none, none)))
            for at in range(2)
        ]
        core_sides = [sides(value) for value in core_one]
        rim_sides = [sides(value) for value in rim_one]
        rim_two = [
            spread_out(rim_one[at], rows_beside(rim_one[at], rim_one[1 - at]), *beside(rim_sides[at], core_sides[at]))
            for at in range(2)
        ]
        core_two = [
            spread_out(core_one[at], rows_beside(core_one[at], core_one[1 - at]), *beside(core_sides[at], rim_sides[at]))
            for at in range(2)
        ]
        return core_two, rim_two

    def fold(value):
        def back(amount):
            return pltpu.roll(value, LANES - amount, 1)
        value = value + back(48)
        value = value + back(24)
        value = value + back(12)
        return value + back(4) + back(8)

    def unfold(value):
        value = jnp.where(near, value, 0.0)
        value = value + pltpu.roll(value, 4, 1) + pltpu.roll(value, 8, 1)
        value = value + pltpu.roll(value, 12, 1)
        value = value + pltpu.roll(value, 24, 1)
        return value + pltpu.roll(value, 48, 1)

    error = jnp.float32(0.0)
    rim_halves = []
    for slot in range(2):
        live = (slot < count).astype(F32)
        rim_parts = waves(to_image([rim_lanes[slot]])[0])
        for part in range(4):
            rim_field[part] = rim_parts[part]
        weights = jnp.concatenate([lane_weight] * (half // 8), axis=0)
        rim_plus = weights * (rim_parts[0] * rim_parts[0] + rim_parts[1] * rim_parts[1])
        rim_minus = weights * (rim_parts[2] * rim_parts[2] + rim_parts[3] * rim_parts[3])
        core = [part * square for part in sums[slot]]
        rim = [jnp.where(near, fold(part), 0.0) * square for part in (rim_plus, rim_minus)]
        core = blur(core, rim)

        def slope_of(value, goal):
            resist = 1.0 / (1.0 + jnp.exp(-RESIST_SLOPE * (value - RESIST_LEVEL)))
            misfit = resist - goal
            return (2.0 * RESIST_SLOPE) * misfit * resist * (1.0 - resist), jnp.sum(misfit * misfit)

        slope_plus, err_plus = slope_of(core[0], goal_ref[slot, :half])
        slope_minus, err_minus = slope_of(core[1], goal_ref[slot, half:])
        error = error + live * (err_plus + err_minus)
        core, rim = blur_back([slope_plus, slope_minus])
        factor = 2.0 * square
        for at in range(2):
            scale_ref[slot, at] = core[at] * factor
        rim_f_plus = unfold(rim[0] * factor) * weights
        rim_f_minus = unfold(rim[1] * factor) * weights
        edge = from_image(
            [
                unwaves(
                    rim_f_plus * rim_field[0],
                    rim_f_plus * rim_field[1],
                    rim_f_minus * rim_field[2],
                    rim_f_minus * rim_field[3],
                )
            ]
        )[0]
        rim_halves.append(jnp.concatenate(halves(edge), axis=1))
    rim_stack = jnp.concatenate(rim_halves, axis=0)
    for part in range(0, rim_slope.shape[2], 2 * LANES):
        moved = mm(rim_stack, table(f"scatter{part}"))
        for slot in range(MOST):
            rim_slope[slot, :, part : part + moved.shape[1]] = moved[slot * freq_y : (slot + 1) * freq_y]
    error_ref[0] = error * (1.0 / (GRID_Y * CORE_X))

    slope_acc[...] = jnp.zeros_like(slope_acc)

    def backward(group, carry):
        tops, rests, edges, images = [], [], [], []
        for step in range(batch):
            k = group * batch + step
            weight = weight_ref[k]
            for slot in range(2):
                plus = scale_ref[slot, 0] * weight
                minus = scale_ref[slot, 1] * weight
                images.append(
                    unwaves(
                        plus * field[slot, k, 0],
                        plus * field[slot, k, 1],
                        minus * field[slot, k, 2],
                        minus * field[slot, k, 3],
                    )
                )
                if len(images) == WIDE:
                    for cols in from_image(images):
                        top, rest = halves(cols)
                        tops.append(top)
                        rests.append(rest)
                    images = []
                edge = rim_slope[slot, :, pl.ds(pl.multiple_of(k // RIM_KERNS * LANES, LANES), LANES)]
                edge = pltpu.roll(edge, LANES - k % RIM_KERNS * RIM_WIDTH, 1).astype(BF16)
                edges.append(jnp.concatenate([edge, edge], axis=1))

        def stack(pieces):
            return jnp.concatenate(pieces, axis=0)
        waves_all = thrice(stack(tops), stack(rests), "core_t") + mm(stack(edges), table("rim_t"))
        sums = [[slope_acc[slot, :freq_y], slope_acc[slot, freq_y:]] for slot in range(2)]
        for step in range(batch):
            kern_re, kern_im = kern_at(group * batch + step)
            for slot in range(2):
                at = (2 * step + slot) * freq_y
                wave_re, wave_im = waves_all[at : at + freq_y, :LANES], waves_all[at : at + freq_y, LANES:]
                sums[slot][0] += wave_re * kern_re + wave_im * kern_im
                sums[slot][1] += wave_im * kern_re - wave_re * kern_im
        for slot in range(2):
            slope_acc[slot, :freq_y] = sums[slot][0]
            slope_acc[slot, freq_y:] = sums[slot][1]
        return carry

    lax.fori_loop(0, kern_count // batch, backward, 0)

    packets = []
    for slot in range(MOST):
        top, rest = halves(slope_acc[slot])
        tall = mm(table("picks_t"), top) + mm(table("picks_t"), rest)
        wide = jnp.concatenate([tall[:ROWS], tall[ROWS:]], axis=1)
        both = mm(pair(wide), table("lanes_t"))
        packets.append(packed(both[:ROWS] + both[ROWS:], used))
    for at in range(2):
        here = slice(at * split, (at + 1) * split)
        ready[at] = slot_pair(packets[0][here], packets[1][here], used)

    def give(pair_at, carry):
        slopes_ref[2 * pair_at] = ready[0]
        slopes_ref[2 * pair_at + 1] = ready[1]
        return carry

    lax.fori_loop(0, slopes_ref.shape[0] // 2, give, 0)
    for copy in later:
        copy.wait()


def imaging_table(kern_count, freq_y, freq_x):
    core, rim, rows = image_tables(freq_y, freq_x)
    lanes, picks = pick_tables(freq_y, freq_x)

    def tall(table):
        return np.concatenate(halves_np(table), axis=0)

    def three(table):
        top, rest = halves_np(table)
        return np.concatenate([top, top, rest], axis=1)

    def square_up(table):
        top, rest = halves_np(table)
        return np.block([[top, top], [rest, np.zeros_like(rest)]])

    rim_out, scatter = rim_tables(rim, kern_count)
    tables = {
        "core": tall(core),
        "core_t": tall(core.T),
        "rim": tall(rim),
        "rim_t": rim_out,
        "rows": three(rows),
        "rows_t": square_up(rows.T),
        "lanes": lanes.astype(BF16),
        "lanes_t": lanes.T.astype(BF16),
        "picks": picks.astype(BF16),
        "picks_t": picks.T.astype(BF16),
        "turn": np.eye(GRID_Y)[
            np.concatenate([GRID_Y // 2 + half_order(), GRID_Y // 2 - 1 - half_order()])
        ].astype(BF16),
    }
    for part in range(0, scatter.shape[1], 2 * LANES):
        tables[f"scatter{part}"] = scatter[:, part : part + 2 * LANES]
    places, stacked, start = {}, [], 0
    for name, piece in tables.items():
        height, width = piece.shape
        places[name] = (start, height, width)
        stacked.append(np.pad(piece, ((0, 0), (0, 2 * LANES - width))))
        start += height
    return places, np.concatenate(stacked, axis=0)


def owner_imaging(owner_list, kern_weight, pieces, kernels, places, table, later):
    kern_count, freq_y, freq_x = kernels.shape[2:]
    tiles, split = owner_list.shape[0], freq_y // 2
    half = GRID_Y // 2
    smem = pl.BlockSpec(memory_space=pltpu.SMEM)
    vmem = pl.BlockSpec(memory_space=pltpu.VMEM)
    hbm = pl.BlockSpec(memory_space=pltpu.HBM)
    return pl.pallas_call(
        functools.partial(imaging_kernel, places, freq_x + 1, len(later)),
        in_specs=[smem, smem, vmem, vmem, vmem] + [hbm] * len(later),
        out_specs=(vmem, smem) + (vmem,) * len(later),
        out_shape=(
            jax.ShapeDtypeStruct((tiles, 2 * split - 8, LANES), F32),
            jax.ShapeDtypeStruct((1,), F32),
        )
        + tuple(jax.ShapeDtypeStruct(part.shape, part.dtype) for part in later),
        scratch_shapes=[
            pltpu.VMEM((MOST, 2 * freq_y, LANES), F32),
            pltpu.VMEM((MOST, kern_count, 4, half, LANES), F32),
            pltpu.VMEM((4, half, LANES), F32),
            pltpu.VMEM((MOST, freq_y, 2 * LANES), F32),
            pltpu.VMEM((MOST, freq_y, -(-kern_count * RIM_WIDTH // LANES) * LANES), F32),
            pltpu.VMEM((MOST, 2 * freq_y, LANES), F32),
            pltpu.VMEM((MOST, 2, half, LANES), F32),
            pltpu.VMEM((2, 2 * split - 8, LANES), F32),
            pltpu.VMEM((MOST, 2 * half, LANES), F32),
            pltpu.SemaphoreType.DMA((len(later),)),
        ],
        compiler_params=pltpu.CompilerParams(vmem_limit_bytes=20 * 2**20),
        name="owner_imaging",
    )(
        owner_list, kern_weight, in_vmem(pieces), in_vmem(kernels),
        in_vmem(table), *[in_hbm(part) for part in later],
    )


def on_device(mask_tiles, target_grid, kernels, kern_weight, owner_list):
    tile_px = mask_tiles.shape[1]
    freq_y, freq_x = kernels.shape[3:]
    count = lax.axis_size("tile")
    cols, turns, rows = mask_tables(tile_px, freq_y, freq_x)
    owner_list = owner_list.reshape(-1)
    mates = [(i, i + 1 - 2 * (i % 2)) for i in range(count)]

    pieces = mask_spectrum(mask_tiles, target_grid.reshape(GRID_Y, CORE_X), cols, turns, rows, freq_x)
    places, table = imaging_table(kernels.shape[2], freq_y, freq_x)
    pieces, table = lax.optimization_barrier((pieces, jnp.asarray(table)))
    if count == PIECES:
        pieces, edges = lax.all_to_all(pieces, "tile", 0, 0, tiled=True), None
    else:
        groups = [list(range(at, at + PIECES)) for at in range(0, count, PIECES)]
        pieces = lax.all_to_all(pieces, "tile", 0, 0, axis_index_groups=groups, tiled=True)
        later = [(i, i + PIECES) for i in range(count - PIECES)]
        sooner = [(i + PIECES, i) for i in range(count - PIECES)]
        edges = jnp.stack(
            [lax.ppermute(pieces[PIECES - 1], "tile", later), lax.ppermute(pieces[0], "tile", sooner)]
        )
    pieces = lax.all_to_all(route(owner_list, pieces, edges), "tile", 0, 0, tiled=True)
    slopes, owner_error, *held = owner_imaging(
        owner_list, kern_weight, pieces, kernels, places, table,
        (mask_tiles,) + update_tables(cols, turns, rows),
    )
    slopes = lax.all_to_all(slopes, "tile", 0, 0, tiled=True)
    other = lax.ppermute(tile_pick(owner_list, slopes, freq_x), "tile", mates)
    current = mask_update(owner_list, slopes, other, *held, freq_x)
    return (current, owner_error)


def solution(mesh):
    placed = (
        P(("stripe", "tile"), None, None),
        P(("stripe", "tile"), None),
        P("tile", None, None, None, None),
        P(),
        P("stripe", None),
    )
    return jax.shard_map(
        on_device,
        mesh=mesh,
        in_specs=placed,
        out_specs=(P(("stripe", "tile"), None, None), P(("stripe", "tile"))),
        check_vma=False,
    )
```

```python
import functools

import jax
import jax.numpy as jnp
import numpy as np
from jax import lax
from jax.experimental import pallas as pl
from jax.experimental.pallas import tpu as pltpu
from jax.sharding import PartitionSpec as P

AMBIT = 256
GRID_X = 192
GRID_Y = 128
CORE_X = 128
RESIST_SLOPE = 3.0
RESIST_LEVEL = 1.2
DIFFUSE_RATE = 0.2
STEP_SIZE = 1.0

LANES = 128
MOST = 2
BLOCKS = 4
PIECES = 16
CHUNK = 6
RIM_WIDTH = 16
RIM_KERNS = LANES // RIM_WIDTH
ROWS = 72
ROWS_PAD = 80
F32 = jnp.float32
BF16 = jnp.bfloat16


def halves_np(table):
    table = np.asarray(table, np.float32)
    top = table.astype(BF16)
    rest = (table - top.astype(np.float32)).astype(BF16)
    return top, rest


def halves(value):
    top = value.astype(BF16)
    rest = (value - top.astype(F32)).astype(BF16)
    return top, rest


def mm(left, right):
    return jnp.dot(left, right, preferred_element_type=F32)


def in_hbm(value):
    return pltpu.with_memory_space_constraint(jnp.asarray(value), pltpu.HBM)


def in_vmem(value):
    return pltpu.with_memory_space_constraint(jnp.asarray(value), pltpu.VMEM)


def real_waves(places, period, most, width):
    angles = 2.0 * np.pi * np.outer(places, np.arange(most + 1)) / period
    waves = np.concatenate([np.cos(angles), np.sin(angles[:, 1:])], axis=1)
    return np.pad(waves, ((0, 0), (0, width - waves.shape[1])))


def signed_picks(count, width):
    freqs = np.arange(count) - count // 2
    most = count // 2
    even = np.zeros((count, width))
    odd = np.zeros((count, width))
    for at, freq in enumerate(freqs):
        even[at, abs(freq)] = 1.0
        if freq != 0:
            odd[at, most + abs(freq)] = np.sign(freq)
    return even, odd


def mask_tables(tile_px, freq_y, freq_x):
    win = tile_px + 2 * AMBIT
    mid_x = (GRID_X - 1) / 2 * (win // GRID_X)
    mid_y = (GRID_Y - 1) / 2 * (tile_px // GRID_Y)
    most = freq_x // 2
    cols = real_waves(np.arange(AMBIT), win, most, LANES)
    rows = real_waves(np.arange(tile_px) - mid_y, tile_px, freq_y // 2, ROWS_PAD)
    blocks = win // AMBIT
    angles = 2.0 * np.pi * np.outer(AMBIT * np.arange(blocks) - mid_x, np.arange(most + 1)) / win
    turns = np.zeros((2, blocks, LANES))
    turns[0, :, : most + 1] = np.cos(angles)
    turns[0, :, most + 1 : 2 * most + 1] = np.cos(angles[:, 1:])
    turns[1, :, : most + 1] = -np.sin(angles)
    turns[1, :, most + 1 : 2 * most + 1] = np.sin(angles[:, 1:])
    return cols, turns.astype(np.float32).reshape(2 * blocks, 1, LANES), rows


def swapped(value, used):
    lane = lax.broadcasted_iota(jnp.int32, value.shape, 1)
    most = (used - 1) // 2
    return jnp.where(lane <= most, pltpu.roll(value, LANES - most, 1), pltpu.roll(value, most, 1))


def packed(tall, used):
    rows = tall.shape[0] - 8
    body, line = tall[:rows], jnp.broadcast_to(tall[rows : rows + 1], (8, LANES))
    lane = lax.broadcasted_iota(jnp.int32, (8, LANES), 1)
    row = lax.broadcasted_iota(jnp.int32, (8, LANES), 0)
    spare = LANES - used
    first = jnp.where(lane < used, body[:8], 0.0)
    for at in range(-(-used // spare)):
        moved = pltpu.roll(line, (used - spare * at) % LANES, 1)
        first = jnp.where((row == at) & (lane >= used), moved, first)
    return jnp.concatenate([first, body[8:]], axis=0)


def unpacked(packet, used):
    lane = lax.broadcasted_iota(jnp.int32, packet.shape, 1)
    first = packet[:8]
    lane8 = lane[:8]
    row = lax.broadcasted_iota(jnp.int32, (8, LANES), 0)
    spare = LANES - used
    line = jnp.zeros((8, LANES), F32)
    for at in range(-(-used // spare)):
        moved = pltpu.roll(first, (spare * at - used) % LANES, 1)
        here = (row == at) & (lane8 >= spare * at) & (lane8 < min(spare * at + spare, used))
        line = line + jnp.where(here, moved, 0.0)
    line = jnp.where(row == 0, jnp.sum(line, axis=0, keepdims=True), 0.0)
    return jnp.concatenate([jnp.where(lane < used, packet, 0.0), line], axis=0)


def own_place():
    return lax.axis_index("tile").astype(jnp.int32)


def fetch(pairs, sems):
    copies = [pltpu.make_async_copy(src, dst, sems.at[at]) for at, (src, dst) in enumerate(pairs)]
    for copy in copies:
        copy.start()
    return copies


def spectrum_kernel(
    used, mask_hbm, cols_hbm, turns_hbm, rows_hbm, target_hbm, out_ref, mask, cols, turns, rows, sems, target_sems
):
    tile_px = mask.shape[0]
    width = AMBIT
    count = tile_px // width
    pairs = [(rows_hbm, rows)]
    for at in range(count):
        place = pl.ds(at * width, width)
        pairs.append((mask_hbm.at[0, :, place], mask.at[:, place]))
    pairs[2:2] = [(cols_hbm, cols), (turns_hbm, turns)]
    copies = fetch(pairs, sems)
    table_copies = [copies.pop(2), copies.pop(2)]
    size = target_hbm.shape[0] // PIECES
    goals = fetch(
        [(target_hbm.at[pl.ds(at * size, size)], out_ref.at[at, pl.ds(16, size)]) for at in range(PIECES)],
        target_sems,
    )

    def turned(both, block):
        return turns[block] * both[0] + turns[block + turns.shape[0] // 2] * both[1]

    copies[0].wait()
    own = None
    for at in range(count):
        copies[1 + at].wait()
        top, rest = halves(mask[:, at * width : (at + 1) * width])
        both = mm(rows[...], top)
        top, rest = halves(both[:ROWS_PAD] + both[ROWS_PAD:] + mm(rows[:ROWS_PAD], rest))
        if at == 0:
            for copy in table_copies:
                copy.wait()
        waves = mm(
            jnp.concatenate([top, rest, top], axis=1),
            jnp.concatenate([cols[:, :LANES], cols[:, :LANES], cols[:, LANES:]], axis=0),
        )
        both = (waves, swapped(waves, used))
        if at == 0:
            low = turned(both, count + 1)
        if at == count - 1:
            high = turned(both, 0)
        piece = turned(both, at + 1)
        own = piece if own is None else own + piece

    own, low, high = [packed(part[:ROWS], used) for part in (own, low, high)]
    groups = own.shape[0] // 8
    low = pltpu.roll(low.reshape(groups, 8, LANES), 4, 1)
    upper = lax.broadcasted_iota(jnp.int32, (8, LANES), 0) < 4
    for at in range(groups):
        mine, other = own[8 * at : 8 * at + 8], low[at]
        out_ref[2 * at, :8] = jnp.where(upper, mine, other)
        out_ref[2 * at + 1, :8] = jnp.where(upper, other, mine)
        out_ref[2 * at, 8:16] = high[8 * at : 8 * at + 8]
        out_ref[2 * at + 1, 8:16] = high[8 * at : 8 * at + 8]
    for copy in goals:
        copy.wait()


def mask_spectrum(mask_tiles, target, cols, turns, rows, freq_x):
    tile_px = mask_tiles.shape[1]
    col_stack = np.concatenate(halves_np(cols), axis=1)
    row_stack = np.concatenate(halves_np(rows.T), axis=0)
    hbm = pl.BlockSpec(memory_space=pltpu.HBM)
    return pl.pallas_call(
        functools.partial(spectrum_kernel, freq_x + 1),
        in_specs=[hbm] * 5,
        out_specs=pl.BlockSpec(memory_space=pltpu.VMEM),
        out_shape=jax.ShapeDtypeStruct((PIECES, 24, LANES), F32),
        scratch_shapes=[
            pltpu.VMEM((tile_px, tile_px), F32),
            pltpu.VMEM(col_stack.shape, BF16),
            pltpu.VMEM(turns.shape, F32),
            pltpu.VMEM(row_stack.shape, BF16),
            pltpu.SemaphoreType.DMA((3 + tile_px // AMBIT,)),
            pltpu.SemaphoreType.DMA((PIECES,)),
        ],
        compiler_params=pltpu.CompilerParams(vmem_limit_bytes=20 * 2**20),
        name="mask_spectrum",
    )(in_hbm(mask_tiles), in_hbm(col_stack), in_hbm(turns), in_hbm(row_stack), in_hbm(target))


def slot_pair(first, second, used):
    spare = LANES - used
    lane = lax.broadcasted_iota(jnp.int32, (8, LANES), 1)
    groups = [part[at : at + 8] for part in (first, second) for at in range(0, part.shape[0], 8)]
    last = groups.pop()
    for at, host in enumerate((1, 2, 3, 5)):
        groups[host] = jnp.where(lane < used, groups[host], pltpu.roll(last, (used - spare * at) % LANES, 1))
    return jnp.concatenate(groups, axis=0)


def slot_half(pair, slot, used):
    spare = LANES - used
    lane = lax.broadcasted_iota(jnp.int32, (8, LANES), 1)
    last = jnp.zeros((8, LANES), F32)
    for at, host in enumerate((1, 2, 3, 5)):
        moved = pltpu.roll(pair[8 * host : 8 * host + 8], (spare * at - used) % LANES, 1)
        last = jnp.where((lane >= spare * at) & (lane < min(spare * at + spare, used)), moved, last)
    return jnp.where(slot == 0, pair[:32], jnp.concatenate([pair[32:], last], axis=0))


def slots_of(owner_ref, tiles):
    owners = [owner_ref[tile] for tile in tiles]

    def count(other, before):
        held = owner_ref[other]
        return tuple(
            seen + ((held == owner) & (other < tile)).astype(jnp.int32)
            for seen, owner, tile in zip(before, owners, tiles)
        )

    ranks = lax.fori_loop(0, owner_ref.shape[0], count, (jnp.int32(0),) * len(tiles))
    return list(zip(owners, ranks))


def tiles_of(owner_ref, owner):
    def find(tile, carry):
        count, first, second = carry
        mine = owner_ref[tile] == owner
        first = jnp.where(mine & (count == 0), tile, first)
        second = jnp.where(mine & (count == 1), tile, second)
        return count + mine.astype(jnp.int32), first, second

    zero = jnp.int32(0)
    return lax.fori_loop(0, owner_ref.shape[0], find, (zero, zero, zero))


def mate_of(me):
    return me + 1 - 2 * lax.rem(me, 2)


def route_kernel(owner_ref, pieces_ref, *rest):
    edges_ref = rest[0] if len(rest) == 3 else None
    out_ref, seen = rest[-2:]
    tiles = owner_ref.shape[0]
    me = own_place()
    base = me // PIECES * PIECES
    row = lax.broadcasted_iota(jnp.int32, (8, LANES), 0)
    mine = row // 4 == lax.rem(me, 2)

    def clear(at, carry):
        seen[at] = 0
        return carry

    lax.fori_loop(0, tiles, clear, 0)

    def send(tile, carry):
        owner = owner_ref[tile]
        slot = seen[owner]
        seen[owner] = slot + 1
        at = tile - base

        @pl.when((at >= 0) & (at < PIECES))
        def _():
            high = pieces_ref[jnp.maximum(at - 1, 0), 8:16]
            low = pieces_ref[jnp.minimum(at + 1, PIECES - 1), :8]
            if edges_ref is None:
                edge_high, edge_low = jnp.zeros_like(high), jnp.zeros_like(low)
            else:
                edge_high, edge_low = edges_ref[0, 8:16], edges_ref[1, :8]
            high = jnp.where(at > 0, high, edge_high)
            low = jnp.where(at < PIECES - 1, low, edge_low)
            packet = pieces_ref[at, :8] + high + pltpu.roll(low, 4, 0)
            beside = jnp.where(mine, out_ref[owner, :8], pltpu.roll(packet, 4, 0))
            out_ref[owner, :8] = jnp.where(slot == 0, packet, beside)
            out_ref[owner, pl.ds(pl.multiple_of(8 + 8 * slot, 8), 8)] = pieces_ref[at, 16:]

        return carry

    lax.fori_loop(0, tiles, send, 0)


def route(owner_list, pieces, edges):
    smem = pl.BlockSpec(memory_space=pltpu.SMEM)
    vmem = pl.BlockSpec(memory_space=pltpu.VMEM)
    tiles = owner_list.shape[0]
    extra = [] if edges is None else [edges]
    return pl.pallas_call(
        route_kernel,
        in_specs=[smem, vmem] + [vmem] * len(extra),
        out_specs=vmem,
        out_shape=jax.ShapeDtypeStruct((tiles, 24, LANES), F32),
        scratch_shapes=[pltpu.SMEM((tiles,), jnp.int32)],
        compiler_params=pltpu.CompilerParams(vmem_limit_bytes=2**20),
        name="route",
    )(owner_list, in_vmem(pieces), *extra)


def around(tile, tiles):
    return [
        (tile, None),
        (jnp.maximum(tile - 1, 0), tile > 0),
        (jnp.minimum(tile + 1, tiles - 1), tile < tiles - 1),
    ]


def tile_pick_kernel(used, owner_ref, slopes_ref, out_ref):
    tiles = [tile for tile, _ in around(mate_of(own_place()), owner_ref.shape[0])]
    for at, (owner, slot) in enumerate(slots_of(owner_ref, tiles)):
        out_ref[at] = slot_half(slopes_ref[owner], slot, used)


def tile_pick(owner_list, slopes, freq_x):
    smem = pl.BlockSpec(memory_space=pltpu.SMEM)
    vmem = pl.BlockSpec(memory_space=pltpu.VMEM)
    return pl.pallas_call(
        functools.partial(tile_pick_kernel, freq_x + 1),
        in_specs=[smem, vmem],
        out_specs=vmem,
        out_shape=jax.ShapeDtypeStruct((3, 32, LANES), F32),
        compiler_params=pltpu.CompilerParams(vmem_limit_bytes=2**20),
        name="tile_pick",
    )(owner_list, in_vmem(slopes))


def joined(me, mine, other):
    odd = lax.rem(me, 2) == 1
    return jnp.concatenate([jnp.where(odd, other, mine), jnp.where(odd, mine, other)], axis=0)


def update_kernel(
    used, owner_ref, slopes_ref, other_ref, mask_ref, cols, turns, rows, out_hbm, out, held, out_sems
):
    tile_px = out.shape[0]
    block = tile_px // BLOCKS
    me = own_place()
    near = around(me, owner_ref.shape[0])
    packets = []
    for at, (owner, slot) in enumerate(slots_of(owner_ref, [tile for tile, _ in near])):
        packet = unpacked(joined(me, slot_half(slopes_ref[owner], slot, used), other_ref[at]), used)
        there = near[at][1]
        packets.append(packet if there is None else jnp.where(there, packet, 0.0))

    own, last, following = [(packet, swapped(packet, used)) for packet in packets]

    def turned_back(both, block):
        return turns[block] * both[0] - turns[block + turns.shape[0] // 2] * both[1]

    count = tile_px // AMBIT
    waves = [turned_back(own, at + 1) for at in range(count)]
    waves[0] = waves[0] + turned_back(last, count + 1)
    waves[-1] = waves[-1] + turned_back(following, 0)
    blank = jnp.zeros((ROWS_PAD - ROWS, LANES), F32)
    top, rest = halves(jnp.concatenate([part for wave in waves for part in (wave, blank)], axis=0))
    wide = mm(
        jnp.concatenate([top, rest, top], axis=1),
        jnp.concatenate([cols[:LANES], cols[:LANES], cols[LANES:]], axis=0),
    )
    for at in range(count):
        top, rest = halves(wide[at * ROWS_PAD : (at + 1) * ROWS_PAD])
        held[:, at * AMBIT : (at + 1) * AMBIT] = jnp.concatenate([top, rest, top], axis=0)
    sent = []
    for at in range(BLOCKS):
        here = slice(at * block, (at + 1) * block)
        place = pl.ds(at * block, block)
        out[here] = mask_ref[0, here] - STEP_SIZE * mm(rows[here], held[...])
        copy = pltpu.make_async_copy(out.at[place], out_hbm.at[0, place], out_sems.at[at])
        copy.start()
        sent.append(copy)
    for copy in sent:
        copy.wait()


def update_tables(cols, turns, rows):
    top, rest = halves_np(rows)
    return (
        np.concatenate(halves_np(cols.T), axis=0),
        turns,
        np.concatenate([top, top, rest], axis=1),
    )


def mask_update(owner_list, slopes, other, mask_tiles, cols, turns, rows, freq_x):
    tile_px = mask_tiles.shape[1]
    smem = pl.BlockSpec(memory_space=pltpu.SMEM)
    vmem = pl.BlockSpec(memory_space=pltpu.VMEM)
    hbm = pl.BlockSpec(memory_space=pltpu.HBM)
    return pl.pallas_call(
        functools.partial(update_kernel, freq_x + 1),
        in_specs=[smem] + [vmem] * 6,
        out_specs=hbm,
        out_shape=jax.ShapeDtypeStruct(mask_tiles.shape, F32),
        scratch_shapes=[
            pltpu.VMEM((tile_px, tile_px), F32),
            pltpu.VMEM((3 * ROWS_PAD, tile_px), BF16),
            pltpu.SemaphoreType.DMA((BLOCKS,)),
        ],
        compiler_params=pltpu.CompilerParams(vmem_limit_bytes=16 * 2**20),
        name="mask_update",
    )(
        owner_list, in_vmem(slopes), other, in_vmem(mask_tiles),
        in_vmem(cols), in_vmem(turns), in_vmem(rows),
    )


def half_order():
    return np.arange(GRID_Y // 2).reshape(8, -1).T.reshape(-1)


def image_tables(freq_y, freq_x):
    places_v = np.arange(GRID_X) - (GRID_X - 1) / 2
    freqs_b = np.arange(freq_x) - (freq_x - 1) / 2
    beta = 2.0 * np.pi * np.outer(freqs_b, places_v) / GRID_X
    first = (GRID_X - CORE_X) // 2

    def block(lane_of):
        table = np.zeros((2 * LANES, 2 * LANES))
        for place, lane in lane_of:
            table[:freq_x, lane] = np.cos(beta[:, place])
            table[:freq_x, LANES + lane] = np.sin(beta[:, place])
            table[LANES : LANES + freq_x, lane] = -np.sin(beta[:, place])
            table[LANES : LANES + freq_x, LANES + lane] = np.cos(beta[:, place])
        return table

    core = block([(first + lane, lane) for lane in range(CORE_X)])
    last = first + CORE_X
    rim = block(
        [(first - 2, LANES - 2), (first - 1, LANES - 1), (last, 0), (last + 1, 1)]
    )
    places_u = half_order() + 0.5
    freqs_a = np.arange(freq_y) - (freq_y - 1) / 2
    alpha = 2.0 * np.pi * np.outer(places_u, freqs_a) / GRID_Y
    rows = np.concatenate([np.cos(alpha), np.sin(alpha)], axis=0)
    return core, rim, rows


def rim_tables(rim, kern_count):
    seats = [(LANES - 2 + at) % LANES for at in range(4)]
    seats = seats + [LANES + seat for seat in seats]
    top, rest = halves_np(rim.T[seats])
    blank = np.zeros((LANES - 8, 2 * LANES), BF16)
    rim_out = np.concatenate([top, top, blank[8:], rest, blank], axis=0)
    width = -(-kern_count * RIM_WIDTH // LANES) * LANES
    scatter = np.zeros((4 * LANES, width))
    for kern in range(kern_count):
        for at in range(8):
            lane = (4 * kern - 2 + at % 4) % LANES + at // 4 * LANES
            scatter[lane, kern * RIM_WIDTH + at] = 1.0
            scatter[2 * LANES + lane, kern * RIM_WIDTH + 8 + at] = 1.0
    return rim_out, scatter.astype(BF16)


def pick_tables(freq_y, freq_x):
    col_even, col_odd = signed_picks(freq_x, LANES)
    row_even, row_odd = signed_picks(freq_y, ROWS)
    lanes = np.zeros((LANES, 2 * LANES))
    lanes[:, :freq_x] = col_even.T
    lanes[:, LANES : LANES + freq_x] = col_odd.T
    rows = np.block([[row_even, -row_odd], [-row_odd, -row_even]])
    return lanes, rows


def imaging_kernel(places, used, extra, *refs):
    owner_ref, weight_ref, pieces_ref, kern_ref, table_ref = refs[:5]
    later_hbm, refs = refs[5 : 5 + extra], refs[5 + extra :]
    slopes_ref, error_ref, later_ref, refs = refs[0], refs[1], refs[2 : 2 + extra], refs[2 + extra :]
    spec, field, rim_field, rim_lanes, rim_slope, scale_ref, ready, goal_ref, sems = refs
    kern_count, freq_y, freq_x = kern_ref.shape[2:]
    later = fetch(list(zip(later_hbm, later_ref)), sems)
    chunk = max(size for size in range(1, CHUNK + 1) if kern_count % size == 0)
    count, first, second = tiles_of(owner_ref, own_place())
    slots = (first, second)
    split = freq_y // 2
    firsts = [slot // PIECES * PIECES for slot in slots]

    def table(name):
        start, height, width = places[name]
        return table_ref[start : start + height, :width]

    def pair(value):
        top, rest = halves(value)
        return jnp.concatenate([top, rest], axis=0)

    upper = lax.broadcasted_iota(jnp.int32, (8, LANES), 0) < 4
    for slot in range(MOST):
        target = jnp.concatenate(
            [pieces_ref[firsts[slot] + at, 8 + 8 * slot : 16 + 8 * slot] for at in range(PIECES)], axis=0
        )
        target = jnp.where(slot < count, target, 0.0)
        one = target.astype(BF16)
        target = target - one.astype(F32)
        two = target.astype(BF16)
        three = (target - two.astype(F32)).astype(BF16)
        goal_ref[slot] = mm(table("turn"), one) + mm(table("turn"), two) + mm(table("turn"), three)
        pieces = []
        for at in range(0, PIECES, 2):
            even, odd = pieces_ref[firsts[slot] + at, :8], pieces_ref[firsts[slot] + at + 1, :8]
            if slot == 0:
                pieces.append(jnp.where(upper, even, odd))
            else:
                pieces.append(pltpu.roll(jnp.where(upper, odd, even), 4, 0))
        packet = jnp.concatenate(pieces, axis=0)
        packet = jnp.where(slot < count, unpacked(packet, used), 0.0)
        both = mm(pair(packet), table("lanes"))
        both = both[:ROWS] + both[ROWS:]
        tall = jnp.concatenate([both[:, :LANES], both[:, LANES:]], axis=0)
        top, rest = halves(tall)
        spec[slot] = mm(table("picks"), top) + mm(table("picks"), rest)

    half = GRID_Y // 2
    lane = lax.broadcasted_iota(jnp.int32, (freq_y, LANES), 1)
    live_lane = lane < freq_x

    def kern_at(k):
        def one(part):
            raw = kern_ref[0, part, k]
            wide = jnp.concatenate([raw, jnp.zeros((freq_y, LANES - freq_x), F32)], axis=1)
            return wide
        return one(0), one(1)

    def side_by_side(pieces):
        return pieces[0] if len(pieces) == 1 else jnp.concatenate(pieces, axis=1)

    def apart(wide):
        size = 2 * LANES
        return [wide[:, at : at + size] for at in range(0, wide.shape[1], size)]

    def to_image(stacks):
        pieces = []
        for stack in stacks:
            top, rest = halves(stack)
            pieces.append(jnp.concatenate([top, rest, top], axis=0))
        return apart(mm(table("rows"), side_by_side(pieces)))

    def from_image(stacks):
        pieces = [jnp.concatenate(halves(stack), axis=0) for stack in stacks]
        both = mm(table("rows_t"), side_by_side(pieces))
        return apart(both[:freq_y] + both[freq_y:])

    def thrice(top, rest, name):
        both = table(name)
        height = both.shape[0] // 2
        return mm(
            jnp.concatenate([top, rest, top], axis=1),
            jnp.concatenate([both[:height], both[:height], both[height:]], axis=0),
        )

    def waves(stack):
        even_re, even_im = stack[:half, :LANES], stack[:half, LANES:]
        odd_re, odd_im = stack[half:, :LANES], stack[half:, LANES:]
        return even_re - odd_im, even_im + odd_re, even_re + odd_im, even_im - odd_re

    def unwaves(plus_re, plus_im, minus_re, minus_im):
        above = jnp.concatenate([plus_re + minus_re, plus_im + minus_im], axis=1)
        below = jnp.concatenate([plus_im - minus_im, minus_re - plus_re], axis=1)
        return jnp.concatenate([above, below], axis=0)


    def forward_chunk(start, new):
        tops, rests = [], []
        for step in range(chunk):
            kern_re, kern_im = kern_at(start + step)
            for slot in range(MOST):
                spec_re, spec_im = spec[slot, :freq_y], spec[slot, freq_y:]
                wave = jnp.concatenate(
                    [kern_re * spec_re - kern_im * spec_im, kern_re * spec_im + kern_im * spec_re], axis=1
                )
                top, rest = halves(wave)
                tops.append(top)
                rests.append(rest)
        top, rest = jnp.concatenate(tops, axis=0), jnp.concatenate(rests, axis=0)
        cols = thrice(top, rest, "core")
        edges = thrice(top, rest, "rim")
        places = [(step, slot) for step in range(chunk) for slot in range(MOST)]
        images = to_image([cols[at * freq_y : (at + 1) * freq_y] for at in range(len(places))])
        for at, (step, slot) in enumerate(places):
            k = start + step
            weight = weight_ref[k]
            new[2] = jnp.where(group_of == k, weight, new[2])
            edge = edges[at * freq_y : (at + 1) * freq_y]
            for part in range(2):
                here = slice(part * LANES, (part + 1) * LANES)
                if k == 0:
                    rim_lanes[slot, :, here] = edge[:, here]
                else:
                    rim_lanes[slot, :, here] += pltpu.roll(edge[:, here], 4 * k, 1)
            parts = waves(images[at])
            for part in range(4):
                field[slot, k, part] = parts[part]
            plus, minus = new[slot]
            plus = plus + weight * (parts[0] * parts[0] + parts[1] * parts[1])
            minus = minus + weight * (parts[2] * parts[2] + parts[3] * parts[3])
            new[slot] = (plus, minus)

    blank = jnp.zeros((half, LANES), F32)
    group_of = lax.rem(lax.broadcasted_iota(jnp.int32, (8, LANES), 1) + 2, LANES) // 4
    sums = [(blank, blank), (blank, blank), jnp.zeros((8, LANES), F32)]
    for start in range(0, kern_count, chunk):
        forward_chunk(start, sums)
    lane_weight = sums.pop()

    norm = 1.0 / (64.0 * GRID_Y * GRID_X)
    square = norm * norm
    lane_half = lax.broadcasted_iota(jnp.int32, (half, LANES), 1)
    near = (lane_half < 2) | (lane_half >= LANES - 2)
    row_8 = lax.broadcasted_iota(jnp.int32, (8, LANES), 0)

    def rows_beside(value, other):
        first, last = value[:8], value[half - 8 :]
        later = jnp.where(row_8 == 7, last, pltpu.roll(first, 7, 0))
        sooner = jnp.where(row_8 == 0, other[:8], pltpu.roll(last, 1, 0))
        return jnp.concatenate([value[8:], later], axis=0) + jnp.concatenate([sooner, value[:-8]], axis=0)

    at_first, at_last = lane_half == 0, lane_half == LANES - 1

    def spread_out(value, rows, left, right):
        return value + DIFFUSE_RATE * (rows + left + right - 4.0 * value)

    def sides(value):
        return pltpu.roll(value, 1, 1), pltpu.roll(value, LANES - 1, 1)

    def beside(core, rim):
        return jnp.where(at_first, rim[0], core[0]), jnp.where(at_last, rim[1], core[1])

    def blur(core, rim):
        core_sides = [sides(value) for value in core]
        rim_sides = [sides(value) for value in rim]
        rim_one = [
            spread_out(rim[at], rows_beside(rim[at], rim[1 - at]), *beside(rim_sides[at], core_sides[at]))
            for at in range(2)
        ]
        core_one = [
            spread_out(core[at], rows_beside(core[at], core[1 - at]), *beside(core_sides[at], rim_sides[at]))
            for at in range(2)
        ]
        return [
            spread_out(
                core_one[at],
                rows_beside(core_one[at], core_one[1 - at]),
                *beside(sides(core_one[at]), sides(rim_one[at])),
            )
            for at in range(2)
        ]

    def blur_back(core):
        core_sides = [sides(value) for value in core]
        none = jnp.zeros((half, LANES), F32)
        rim_one = [DIFFUSE_RATE * sum(beside((none, none), core_sides[at])) for at in range(2)]
        core_one = [
            spread_out(core[at], rows_beside(core[at], core[1 - at]), *beside(core_sides[at], (none, none)))
            for at in range(2)
        ]
        core_sides = [sides(value) for value in core_one]
        rim_sides = [sides(value) for value in rim_one]
        rim_two = [
            spread_out(rim_one[at], rows_beside(rim_one[at], rim_one[1 - at]), *beside(rim_sides[at], core_sides[at]))
            for at in range(2)
        ]
        core_two = [
            spread_out(core_one[at], rows_beside(core_one[at], core_one[1 - at]), *beside(core_sides[at], rim_sides[at]))
            for at in range(2)
        ]
        return core_two, rim_two

    def fold(value):
        def back(amount):
            return pltpu.roll(value, LANES - amount, 1)
        value = value + back(48)
        value = value + back(24)
        value = value + back(12)
        return value + back(4) + back(8)

    def unfold(value):
        value = jnp.where(near, value, 0.0)
        value = value + pltpu.roll(value, 4, 1) + pltpu.roll(value, 8, 1)
        value = value + pltpu.roll(value, 12, 1)
        value = value + pltpu.roll(value, 24, 1)
        return value + pltpu.roll(value, 48, 1)

    error = jnp.float32(0.0)
    rim_halves = []
    for slot in range(2):
        live = (slot < count).astype(F32)
        rim_parts = waves(to_image([rim_lanes[slot]])[0])
        for part in range(4):
            rim_field[slot, part] = rim_parts[part]
        weights = jnp.concatenate([lane_weight] * (half // 8), axis=0)
        rim_plus = weights * (rim_parts[0] * rim_parts[0] + rim_parts[1] * rim_parts[1])
        rim_minus = weights * (rim_parts[2] * rim_parts[2] + rim_parts[3] * rim_parts[3])
        core = [part * square for part in sums[slot]]
        rim = [jnp.where(near, fold(part), 0.0) * square for part in (rim_plus, rim_minus)]
        core = blur(core, rim)

        def slope_of(value, goal):
            resist = 1.0 / (1.0 + jnp.exp(-RESIST_SLOPE * (value - RESIST_LEVEL)))
            misfit = resist - goal
            return (2.0 * RESIST_SLOPE) * misfit * resist * (1.0 - resist), jnp.sum(misfit * misfit)

        slope_plus, err_plus = slope_of(core[0], goal_ref[slot, :half])
        slope_minus, err_minus = slope_of(core[1], goal_ref[slot, half:])
        error = error + live * (err_plus + err_minus)
        core, rim = blur_back([slope_plus, slope_minus])
        factor = 2.0 * square
        for at in range(2):
            scale_ref[slot, at] = core[at] * factor
        rim_f_plus = unfold(rim[0] * factor) * weights
        rim_f_minus = unfold(rim[1] * factor) * weights
        edge = from_image(
            [
                unwaves(
                    rim_f_plus * rim_field[slot, 0],
                    rim_f_plus * rim_field[slot, 1],
                    rim_f_minus * rim_field[slot, 2],
                    rim_f_minus * rim_field[slot, 3],
                )
            ]
        )[0]
        rim_halves.append(jnp.concatenate(halves(edge), axis=1))
    rim_stack = jnp.concatenate(rim_halves, axis=0)
    for part in range(0, rim_slope.shape[2], 2 * LANES):
        moved = mm(rim_stack, table(f"scatter{part}"))
        for slot in range(MOST):
            rim_slope[slot, :, part : part + moved.shape[1]] = moved[slot * freq_y : (slot + 1) * freq_y]
    error_ref[0] = error * (1.0 / (GRID_Y * CORE_X))


    def backward_chunk(start, sums):
        images, edges = [], []
        for step in range(chunk):
            k = start + step
            weight = weight_ref[k]
            for slot in range(MOST):
                plus = scale_ref[slot, 0] * weight
                minus = scale_ref[slot, 1] * weight
                images.append(
                    unwaves(
                        plus * field[slot, k, 0],
                        plus * field[slot, k, 1],
                        minus * field[slot, k, 2],
                        minus * field[slot, k, 3],
                    )
                )
                column = k // RIM_KERNS * LANES
                edge = rim_slope[slot, :, column : column + LANES]
                if k % RIM_KERNS != 0:
                    edge = pltpu.roll(edge, LANES - k % RIM_KERNS * RIM_WIDTH, 1)
                edge = edge.astype(BF16)
                edges.append(jnp.concatenate([edge, edge], axis=1))
        pairs = [halves(cols) for cols in from_image(images)]
        top, rest = [jnp.concatenate(part, axis=0) for part in zip(*pairs)]
        waves_all = thrice(top, rest, "core_t") + mm(jnp.concatenate(edges, axis=0), table("rim_t"))
        for step in range(chunk):
            kern_re, kern_im = kern_at(start + step)
            for slot in range(MOST):
                at = (MOST * step + slot) * freq_y
                wave_re, wave_im = waves_all[at : at + freq_y, :LANES], waves_all[at : at + freq_y, LANES:]
                sums[slot][0] += wave_re * kern_re + wave_im * kern_im
                sums[slot][1] += wave_im * kern_re - wave_re * kern_im

    slopes = [[jnp.zeros((freq_y, LANES), F32)] * 2 for _ in range(MOST)]
    for start in range(0, kern_count, chunk):
        backward_chunk(start, slopes)

    packets = []
    for slot in range(MOST):
        top, rest = halves(jnp.concatenate(slopes[slot], axis=0))
        tall = mm(table("picks_t"), top) + mm(table("picks_t"), rest)
        wide = jnp.concatenate([tall[:ROWS], tall[ROWS:]], axis=1)
        both = mm(pair(wide), table("lanes_t"))
        packets.append(packed(both[:ROWS] + both[ROWS:], used))
    for at in range(2):
        here = slice(at * split, (at + 1) * split)
        ready[at] = slot_pair(packets[0][here], packets[1][here], used)

    def give(pair_at, carry):
        slopes_ref[2 * pair_at] = ready[0]
        slopes_ref[2 * pair_at + 1] = ready[1]
        return carry

    lax.fori_loop(0, slopes_ref.shape[0] // 2, give, 0)
    for copy in later:
        copy.wait()


def imaging_table(kern_count, freq_y, freq_x):
    core, rim, rows = image_tables(freq_y, freq_x)
    lanes, picks = pick_tables(freq_y, freq_x)

    def tall(table):
        return np.concatenate(halves_np(table), axis=0)

    def three(table):
        top, rest = halves_np(table)
        return np.concatenate([top, top, rest], axis=1)

    def square_up(table):
        top, rest = halves_np(table)
        return np.block([[top, top], [rest, np.zeros_like(rest)]])

    rim_out, scatter = rim_tables(rim, kern_count)
    tables = {
        "core": tall(core),
        "core_t": tall(core.T),
        "rim": tall(rim),
        "rim_t": rim_out,
        "rows": three(rows),
        "rows_t": square_up(rows.T),
        "lanes": lanes.astype(BF16),
        "lanes_t": lanes.T.astype(BF16),
        "picks": picks.astype(BF16),
        "picks_t": picks.T.astype(BF16),
        "turn": np.eye(GRID_Y)[
            np.concatenate([GRID_Y // 2 + half_order(), GRID_Y // 2 - 1 - half_order()])
        ].astype(BF16),
    }
    for part in range(0, scatter.shape[1], 2 * LANES):
        tables[f"scatter{part}"] = scatter[:, part : part + 2 * LANES]
    places, stacked, start = {}, [], 0
    for name, piece in tables.items():
        height, width = piece.shape
        places[name] = (start, height, width)
        stacked.append(np.pad(piece, ((0, 0), (0, 2 * LANES - width))))
        start += height
    return places, np.concatenate(stacked, axis=0)


def owner_imaging(owner_list, kern_weight, pieces, kernels, places, table, later):
    kern_count, freq_y, freq_x = kernels.shape[2:]
    tiles, split = owner_list.shape[0], freq_y // 2
    half = GRID_Y // 2
    smem = pl.BlockSpec(memory_space=pltpu.SMEM)
    vmem = pl.BlockSpec(memory_space=pltpu.VMEM)
    hbm = pl.BlockSpec(memory_space=pltpu.HBM)
    return pl.pallas_call(
        functools.partial(imaging_kernel, places, freq_x + 1, len(later)),
        in_specs=[smem, smem, vmem, vmem, vmem] + [hbm] * len(later),
        out_specs=(vmem, smem) + (vmem,) * len(later),
        out_shape=(
            jax.ShapeDtypeStruct((tiles, 2 * split - 8, LANES), F32),
            jax.ShapeDtypeStruct((1,), F32),
        )
        + tuple(jax.ShapeDtypeStruct(part.shape, part.dtype) for part in later),
        scratch_shapes=[
            pltpu.VMEM((MOST, 2 * freq_y, LANES), F32),
            pltpu.VMEM((MOST, kern_count, 4, half, LANES), F32),
            pltpu.VMEM((MOST, 4, half, LANES), F32),
            pltpu.VMEM((MOST, freq_y, 2 * LANES), F32),
            pltpu.VMEM((MOST, freq_y, -(-kern_count * RIM_WIDTH // LANES) * LANES), F32),
            pltpu.VMEM((MOST, 2, half, LANES), F32),
            pltpu.VMEM((2, 2 * split - 8, LANES), F32),
            pltpu.VMEM((MOST, 2 * half, LANES), F32),
            pltpu.SemaphoreType.DMA((len(later),)),
        ],
        compiler_params=pltpu.CompilerParams(vmem_limit_bytes=20 * 2**20),
        name="owner_imaging",
    )(
        owner_list, kern_weight, in_vmem(pieces), in_vmem(kernels),
        in_vmem(table), *[in_hbm(part) for part in later],
    )


def on_device(mask_tiles, target_grid, kernels, kern_weight, owner_list):
    tile_px = mask_tiles.shape[1]
    freq_y, freq_x = kernels.shape[3:]
    count = lax.axis_size("tile")
    cols, turns, rows = mask_tables(tile_px, freq_y, freq_x)
    owner_list = owner_list.reshape(-1)
    mates = [(i, i + 1 - 2 * (i % 2)) for i in range(count)]

    pieces = mask_spectrum(mask_tiles, target_grid.reshape(GRID_Y, CORE_X), cols, turns, rows, freq_x)
    places, table = imaging_table(kernels.shape[2], freq_y, freq_x)
    pieces, table = lax.optimization_barrier((pieces, jnp.asarray(table)))
    if count == PIECES:
        pieces, edges = lax.all_to_all(pieces, "tile", 0, 0, tiled=True), None
    else:
        groups = [list(range(at, at + PIECES)) for at in range(0, count, PIECES)]
        pieces = lax.all_to_all(pieces, "tile", 0, 0, axis_index_groups=groups, tiled=True)
        later = [(i, i + PIECES) for i in range(count - PIECES)]
        sooner = [(i + PIECES, i) for i in range(count - PIECES)]
        edges = jnp.stack(
            [lax.ppermute(pieces[PIECES - 1], "tile", later), lax.ppermute(pieces[0], "tile", sooner)]
        )
    pieces = lax.all_to_all(route(owner_list, pieces, edges), "tile", 0, 0, tiled=True)
    slopes, owner_error, *held = owner_imaging(
        owner_list, kern_weight, pieces, kernels, places, table,
        (mask_tiles,) + update_tables(cols, turns, rows),
    )
    slopes = lax.all_to_all(slopes, "tile", 0, 0, tiled=True)
    other = lax.ppermute(tile_pick(owner_list, slopes, freq_x), "tile", mates)
    current = mask_update(owner_list, slopes, other, *held, freq_x)
    return (current, owner_error)


def solution(mesh):
    placed = (
        P(("stripe", "tile"), None, None),
        P(("stripe", "tile"), None),
        P("tile", None, None, None, None),
        P(),
        P("stripe", None),
    )
    return jax.shard_map(
        on_device,
        mesh=mesh,
        in_specs=placed,
        out_specs=(P(("stripe", "tile"), None, None), P(("stripe", "tile"))),
        check_vma=False,
    )
```

```python
import functools

import jax
import jax.numpy as jnp
import numpy as np
from jax import lax
from jax.experimental import pallas as pl
from jax.experimental.pallas import tpu as pltpu
from jax.sharding import PartitionSpec as P

AMBIT = 256
GRID_X = 192
GRID_Y = 128
CORE_X = 128
RESIST_SLOPE = 3.0
RESIST_LEVEL = 1.2
DIFFUSE_RATE = 0.2
STEP_SIZE = 1.0

LANES = 128
MOST = 2
BLOCKS = 4
PIECES = 16
CHUNK = 6
RIM_WIDTH = 16
RIM_KERNS = LANES // RIM_WIDTH
ROWS = 72
ROWS_PAD = 80
F32 = jnp.float32
BF16 = jnp.bfloat16


def halves_np(table):
    table = np.asarray(table, np.float32)
    top = table.astype(BF16)
    rest = (table - top.astype(np.float32)).astype(BF16)
    return top, rest


def halves(value):
    top = value.astype(BF16)
    rest = (value - top.astype(F32)).astype(BF16)
    return top, rest


def mm(left, right):
    return jnp.dot(left, right, preferred_element_type=F32)


def in_hbm(value):
    return pltpu.with_memory_space_constraint(jnp.asarray(value), pltpu.HBM)


def in_vmem(value):
    return pltpu.with_memory_space_constraint(jnp.asarray(value), pltpu.VMEM)


def real_waves(places, period, most, width):
    angles = 2.0 * np.pi * np.outer(places, np.arange(most + 1)) / period
    waves = np.concatenate([np.cos(angles), np.sin(angles[:, 1:])], axis=1)
    return np.pad(waves, ((0, 0), (0, width - waves.shape[1])))


def signed_picks(count, width):
    freqs = np.arange(count) - count // 2
    most = count // 2
    even = np.zeros((count, width))
    odd = np.zeros((count, width))
    for at, freq in enumerate(freqs):
        even[at, abs(freq)] = 1.0
        if freq != 0:
            odd[at, most + abs(freq)] = np.sign(freq)
    return even, odd


def mask_tables(tile_px, freq_y, freq_x):
    win = tile_px + 2 * AMBIT
    mid_x = (GRID_X - 1) / 2 * (win // GRID_X)
    mid_y = (GRID_Y - 1) / 2 * (tile_px // GRID_Y)
    most = freq_x // 2
    cols = real_waves(np.arange(AMBIT), win, most, LANES)
    rows = real_waves(np.arange(tile_px) - mid_y, tile_px, freq_y // 2, ROWS_PAD)
    blocks = win // AMBIT
    angles = 2.0 * np.pi * np.outer(AMBIT * np.arange(blocks) - mid_x, np.arange(most + 1)) / win
    turns = np.zeros((2, blocks, LANES))
    turns[0, :, : most + 1] = np.cos(angles)
    turns[0, :, most + 1 : 2 * most + 1] = np.cos(angles[:, 1:])
    turns[1, :, : most + 1] = -np.sin(angles)
    turns[1, :, most + 1 : 2 * most + 1] = np.sin(angles[:, 1:])
    return cols, turns.astype(np.float32).reshape(2 * blocks, 1, LANES), rows


def swapped(value, used):
    lane = lax.broadcasted_iota(jnp.int32, value.shape, 1)
    most = (used - 1) // 2
    return jnp.where(lane <= most, pltpu.roll(value, LANES - most, 1), pltpu.roll(value, most, 1))


def packed(tall, used):
    rows = tall.shape[0] - 8
    body, line = tall[:rows], jnp.broadcast_to(tall[rows : rows + 1], (8, LANES))
    lane = lax.broadcasted_iota(jnp.int32, (8, LANES), 1)
    row = lax.broadcasted_iota(jnp.int32, (8, LANES), 0)
    spare = LANES - used
    first = jnp.where(lane < used, body[:8], 0.0)
    for at in range(-(-used // spare)):
        moved = pltpu.roll(line, (used - spare * at) % LANES, 1)
        first = jnp.where((row == at) & (lane >= used), moved, first)
    return jnp.concatenate([first, body[8:]], axis=0)


def unpacked(packet, used):
    lane = lax.broadcasted_iota(jnp.int32, packet.shape, 1)
    first = packet[:8]
    lane8 = lane[:8]
    row = lax.broadcasted_iota(jnp.int32, (8, LANES), 0)
    spare = LANES - used
    line = jnp.zeros((8, LANES), F32)
    for at in range(-(-used // spare)):
        moved = pltpu.roll(first, (spare * at - used) % LANES, 1)
        here = (row == at) & (lane8 >= spare * at) & (lane8 < min(spare * at + spare, used))
        line = line + jnp.where(here, moved, 0.0)
    line = jnp.where(row == 0, jnp.sum(line, axis=0, keepdims=True), 0.0)
    return jnp.concatenate([jnp.where(lane < used, packet, 0.0), line], axis=0)


def own_place():
    return lax.axis_index("tile").astype(jnp.int32)


def fetch(pairs, sems):
    copies = [pltpu.make_async_copy(src, dst, sems.at[at]) for at, (src, dst) in enumerate(pairs)]
    for copy in copies:
        copy.start()
    return copies


def spectrum_kernel(
    used, mask_hbm, cols_hbm, turns_hbm, rows_hbm, target_hbm, out_ref, mask, cols, turns, rows, sems, target_sems
):
    tile_px = mask.shape[0]
    width = AMBIT
    count = tile_px // width
    pairs = [(rows_hbm, rows)]
    for at in range(count):
        place = pl.ds(at * width, width)
        pairs.append((mask_hbm.at[0, :, place], mask.at[:, place]))
    pairs[2:2] = [(cols_hbm, cols), (turns_hbm, turns)]
    copies = fetch(pairs, sems)
    table_copies = [copies.pop(2), copies.pop(2)]
    size = target_hbm.shape[0] // PIECES
    goals = fetch(
        [(target_hbm.at[pl.ds(at * size, size)], out_ref.at[at, pl.ds(16, size)]) for at in range(PIECES)],
        target_sems,
    )

    def turned(both, block):
        return turns[block] * both[0] + turns[block + turns.shape[0] // 2] * both[1]

    copies[0].wait()
    terms = []
    for at in range(count):
        copies[1 + at].wait()
        top, rest = halves(mask[:, at * width : (at + 1) * width])
        both = mm(rows[...], top)
        top, rest = halves(both[:ROWS_PAD] + both[ROWS_PAD:] + mm(rows[:ROWS_PAD], rest))
        terms.append(jnp.concatenate([top, rest, top], axis=1))

    for copy in table_copies:
        copy.wait()
    table = jnp.concatenate([cols[:, :LANES], cols[:, :LANES], cols[:, LANES:]], axis=0)
    waves = []
    for some in (terms,):
        wave = mm(jnp.concatenate(some, axis=0), table)
        waves += [wave[at * ROWS_PAD : (at + 1) * ROWS_PAD] for at in range(len(some))]
    waves = [(wave, swapped(wave, used)) for wave in waves]
    own = sum(turned(wave, at + 1) for at, wave in enumerate(waves))
    low, high = turned(waves[0], count + 1), turned(waves[-1], 0)

    own, low, high = [packed(part[:ROWS], used) for part in (own, low, high)]
    groups = own.shape[0] // 8
    low = pltpu.roll(low.reshape(groups, 8, LANES), 4, 1)
    upper = lax.broadcasted_iota(jnp.int32, (8, LANES), 0) < 4
    for at in range(groups):
        mine, other = own[8 * at : 8 * at + 8], low[at]
        out_ref[2 * at, :8] = jnp.where(upper, mine, other)
        out_ref[2 * at + 1, :8] = jnp.where(upper, other, mine)
        out_ref[2 * at, 8:16] = high[8 * at : 8 * at + 8]
        out_ref[2 * at + 1, 8:16] = high[8 * at : 8 * at + 8]
    for copy in goals:
        copy.wait()


def mask_spectrum(mask_tiles, target, cols, turns, rows, freq_x):
    tile_px = mask_tiles.shape[1]
    col_stack = np.concatenate(halves_np(cols), axis=1)
    row_stack = np.concatenate(halves_np(rows.T), axis=0)
    hbm = pl.BlockSpec(memory_space=pltpu.HBM)
    return pl.pallas_call(
        functools.partial(spectrum_kernel, freq_x + 1),
        in_specs=[hbm] * 5,
        out_specs=pl.BlockSpec(memory_space=pltpu.VMEM),
        out_shape=jax.ShapeDtypeStruct((PIECES, 24, LANES), F32),
        scratch_shapes=[
            pltpu.VMEM((tile_px, tile_px), F32),
            pltpu.VMEM(col_stack.shape, BF16),
            pltpu.VMEM(turns.shape, F32),
            pltpu.VMEM(row_stack.shape, BF16),
            pltpu.SemaphoreType.DMA((3 + tile_px // AMBIT,)),
            pltpu.SemaphoreType.DMA((PIECES,)),
        ],
        compiler_params=pltpu.CompilerParams(vmem_limit_bytes=20 * 2**20),
        name="mask_spectrum",
    )(in_hbm(mask_tiles), in_hbm(col_stack), in_hbm(turns), in_hbm(row_stack), in_hbm(target))


def slot_pair(first, second, used):
    spare = LANES - used
    lane = lax.broadcasted_iota(jnp.int32, (8, LANES), 1)
    groups = [part[at : at + 8] for part in (first, second) for at in range(0, part.shape[0], 8)]
    last = groups.pop()
    for at, host in enumerate((1, 2, 3, 5)):
        groups[host] = jnp.where(lane < used, groups[host], pltpu.roll(last, (used - spare * at) % LANES, 1))
    return jnp.concatenate(groups, axis=0)


def slot_half(pair, slot, used):
    spare = LANES - used
    lane = lax.broadcasted_iota(jnp.int32, (8, LANES), 1)
    last = jnp.zeros((8, LANES), F32)
    for at, host in enumerate((1, 2, 3, 5)):
        moved = pltpu.roll(pair[8 * host : 8 * host + 8], (spare * at - used) % LANES, 1)
        last = jnp.where((lane >= spare * at) & (lane < min(spare * at + spare, used)), moved, last)
    return jnp.where(slot == 0, pair[:32], jnp.concatenate([pair[32:], last], axis=0))


def each(count, body, carry):
    if count > PIECES:
        return lax.fori_loop(0, count, body, carry)
    for at in range(count):
        carry = body(jnp.int32(at), carry)
    return carry


def slots_of(owner_ref, tiles):
    owners = [owner_ref[tile] for tile in tiles]

    def count(other, before):
        held = owner_ref[other]
        return tuple(
            seen + ((held == owner) & (other < tile)).astype(jnp.int32)
            for seen, owner, tile in zip(before, owners, tiles)
        )

    ranks = each(owner_ref.shape[0], count, (jnp.int32(0),) * len(tiles))
    return list(zip(owners, ranks))


def tiles_of(owner_ref, owner):
    def find(tile, carry):
        count, first, second = carry
        mine = owner_ref[tile] == owner
        first = jnp.where(mine & (count == 0), tile, first)
        second = jnp.where(mine & (count == 1), tile, second)
        return count + mine.astype(jnp.int32), first, second

    zero = jnp.int32(0)
    return lax.fori_loop(0, owner_ref.shape[0], find, (zero, zero, zero))


def mate_of(me):
    return me + 1 - 2 * lax.rem(me, 2)


def route_kernel(owner_ref, pieces_ref, *rest):
    edges_ref = rest[0] if len(rest) == 3 else None
    out_ref, seen = rest[-2:]
    tiles = owner_ref.shape[0]
    me = own_place()
    base = me // PIECES * PIECES if tiles > PIECES else 0
    row = lax.broadcasted_iota(jnp.int32, (8, LANES), 0)
    mine = row // 4 == lax.rem(me, 2)

    def clear(at, carry):
        seen[at] = 0
        return carry

    each(tiles, clear, 0)

    def send(tile, carry):
        owner = owner_ref[tile]
        slot = seen[owner]
        seen[owner] = slot + 1
        at = tile - base

        def forward():
            high = pieces_ref[jnp.maximum(at - 1, 0), 8:16]
            low = pieces_ref[jnp.minimum(at + 1, PIECES - 1), :8]
            if edges_ref is None:
                edge_high, edge_low = jnp.zeros_like(high), jnp.zeros_like(low)
            else:
                edge_high, edge_low = edges_ref[0, 8:16], edges_ref[1, :8]
            high = jnp.where(at > 0, high, edge_high)
            low = jnp.where(at < PIECES - 1, low, edge_low)
            packet = pieces_ref[at, :8] + high + pltpu.roll(low, 4, 0)
            beside = jnp.where(mine, out_ref[owner, :8], pltpu.roll(packet, 4, 0))
            out_ref[owner, :8] = jnp.where(slot == 0, packet, beside)
            out_ref[owner, pl.ds(pl.multiple_of(8 + 8 * slot, 8), 8)] = pieces_ref[at, 16:]

        if tiles > PIECES:
            pl.when((at >= 0) & (at < PIECES))(forward)
        else:
            forward()
        return carry

    each(tiles, send, 0)


def route(owner_list, pieces, edges):
    smem = pl.BlockSpec(memory_space=pltpu.SMEM)
    vmem = pl.BlockSpec(memory_space=pltpu.VMEM)
    tiles = owner_list.shape[0]
    extra = [] if edges is None else [edges]
    return pl.pallas_call(
        route_kernel,
        in_specs=[smem, vmem] + [vmem] * len(extra),
        out_specs=vmem,
        out_shape=jax.ShapeDtypeStruct((tiles, 24, LANES), F32),
        scratch_shapes=[pltpu.SMEM((tiles,), jnp.int32)],
        compiler_params=pltpu.CompilerParams(vmem_limit_bytes=2**20),
        name="route",
    )(owner_list, in_vmem(pieces), *extra)


def around(tile, tiles):
    return [
        (tile, None),
        (jnp.maximum(tile - 1, 0), tile > 0),
        (jnp.minimum(tile + 1, tiles - 1), tile < tiles - 1),
    ]


def tile_pick_kernel(used, owner_ref, slopes_ref, out_ref):
    tiles = [tile for tile, _ in around(mate_of(own_place()), owner_ref.shape[0])]
    for at, (owner, slot) in enumerate(slots_of(owner_ref, tiles)):
        out_ref[at] = slot_half(slopes_ref[owner], slot, used)


def tile_pick(owner_list, slopes, freq_x):
    smem = pl.BlockSpec(memory_space=pltpu.SMEM)
    vmem = pl.BlockSpec(memory_space=pltpu.VMEM)
    return pl.pallas_call(
        functools.partial(tile_pick_kernel, freq_x + 1),
        in_specs=[smem, vmem],
        out_specs=vmem,
        out_shape=jax.ShapeDtypeStruct((3, 32, LANES), F32),
        compiler_params=pltpu.CompilerParams(vmem_limit_bytes=2**20),
        name="tile_pick",
    )(owner_list, in_vmem(slopes))


def joined(me, mine, other):
    odd = lax.rem(me, 2) == 1
    return jnp.concatenate([jnp.where(odd, other, mine), jnp.where(odd, mine, other)], axis=0)


def update_kernel(
    used, owner_ref, slopes_ref, other_ref, mask_ref, cols, turns, rows, out_hbm, out, held, out_sems
):
    tile_px = out.shape[0]
    block = tile_px // BLOCKS
    me = own_place()
    near = around(me, owner_ref.shape[0])
    packets = []
    for at, (owner, slot) in enumerate(slots_of(owner_ref, [tile for tile, _ in near])):
        packet = unpacked(joined(me, slot_half(slopes_ref[owner], slot, used), other_ref[at]), used)
        there = near[at][1]
        packets.append(packet if there is None else jnp.where(there, packet, 0.0))

    own, last, following = [(packet, swapped(packet, used)) for packet in packets]

    def turned_back(both, block):
        return turns[block] * both[0] - turns[block + turns.shape[0] // 2] * both[1]

    count = tile_px // AMBIT
    waves = [turned_back(own, at + 1) for at in range(count)]
    waves[0] = waves[0] + turned_back(last, count + 1)
    waves[-1] = waves[-1] + turned_back(following, 0)
    blank = jnp.zeros((ROWS_PAD - ROWS, LANES), F32)
    top, rest = halves(jnp.concatenate([part for wave in waves for part in (wave, blank)], axis=0))
    wide = mm(
        jnp.concatenate([top, rest, top], axis=1),
        jnp.concatenate([cols[:LANES], cols[:LANES], cols[LANES:]], axis=0),
    )
    for at in range(count):
        top, rest = halves(wide[at * ROWS_PAD : (at + 1) * ROWS_PAD])
        held[:, at * AMBIT : (at + 1) * AMBIT] = jnp.concatenate([top, rest, top], axis=0)
    sent = []
    for at in range(BLOCKS):
        here = slice(at * block, (at + 1) * block)
        place = pl.ds(at * block, block)
        out[here] = mask_ref[0, here] - STEP_SIZE * mm(rows[here], held[...])
        copy = pltpu.make_async_copy(out.at[place], out_hbm.at[0, place], out_sems.at[at])
        copy.start()
        sent.append(copy)
    for copy in sent:
        copy.wait()


def update_tables(cols, turns, rows):
    top, rest = halves_np(rows)
    return (
        np.concatenate(halves_np(cols.T), axis=0),
        turns,
        np.concatenate([top, top, rest], axis=1),
    )


def mask_update(owner_list, slopes, other, mask_tiles, cols, turns, rows, freq_x):
    tile_px = mask_tiles.shape[1]
    smem = pl.BlockSpec(memory_space=pltpu.SMEM)
    vmem = pl.BlockSpec(memory_space=pltpu.VMEM)
    hbm = pl.BlockSpec(memory_space=pltpu.HBM)
    return pl.pallas_call(
        functools.partial(update_kernel, freq_x + 1),
        in_specs=[smem] + [vmem] * 6,
        out_specs=hbm,
        out_shape=jax.ShapeDtypeStruct(mask_tiles.shape, F32),
        scratch_shapes=[
            pltpu.VMEM((tile_px, tile_px), F32),
            pltpu.VMEM((3 * ROWS_PAD, tile_px), BF16),
            pltpu.SemaphoreType.DMA((BLOCKS,)),
        ],
        compiler_params=pltpu.CompilerParams(vmem_limit_bytes=16 * 2**20),
        name="mask_update",
    )(
        owner_list, in_vmem(slopes), other, in_vmem(mask_tiles),
        in_vmem(cols), in_vmem(turns), in_vmem(rows),
    )


def half_order():
    return np.arange(GRID_Y // 2).reshape(8, -1).T.reshape(-1)


def image_tables(freq_y, freq_x):
    places_v = np.arange(GRID_X) - (GRID_X - 1) / 2
    freqs_b = np.arange(freq_x) - (freq_x - 1) / 2
    beta = 2.0 * np.pi * np.outer(freqs_b, places_v) / GRID_X
    first = (GRID_X - CORE_X) // 2

    def block(lane_of):
        table = np.zeros((2 * LANES, 2 * LANES))
        for place, lane in lane_of:
            table[:freq_x, lane] = np.cos(beta[:, place])
            table[:freq_x, LANES + lane] = np.sin(beta[:, place])
            table[LANES : LANES + freq_x, lane] = -np.sin(beta[:, place])
            table[LANES : LANES + freq_x, LANES + lane] = np.cos(beta[:, place])
        return table

    core = block([(first + lane, lane) for lane in range(CORE_X)])
    last = first + CORE_X
    rim = block(
        [(first - 2, LANES - 2), (first - 1, LANES - 1), (last, 0), (last + 1, 1)]
    )
    places_u = half_order() + 0.5
    freqs_a = np.arange(freq_y) - (freq_y - 1) / 2
    alpha = 2.0 * np.pi * np.outer(places_u, freqs_a) / GRID_Y
    rows = np.concatenate([np.cos(alpha), np.sin(alpha)], axis=0)
    return core, rim, rows


def rim_tables(rim, kern_count):
    seats = [(LANES - 2 + at) % LANES for at in range(4)]
    seats = seats + [LANES + seat for seat in seats]
    top, rest = halves_np(rim.T[seats])
    blank = np.zeros((LANES - 8, 2 * LANES), BF16)
    rim_out = np.concatenate([top, top, blank[8:], rest, blank], axis=0)
    width = -(-kern_count * RIM_WIDTH // LANES) * LANES
    scatter = np.zeros((4 * LANES, width))
    for kern in range(kern_count):
        for at in range(8):
            lane = (4 * kern - 2 + at % 4) % LANES + at // 4 * LANES
            scatter[lane, kern * RIM_WIDTH + at] = 1.0
            scatter[2 * LANES + lane, kern * RIM_WIDTH + 8 + at] = 1.0
    return rim_out, scatter.astype(BF16)


def pick_tables(freq_y, freq_x):
    col_even, col_odd = signed_picks(freq_x, LANES)
    row_even, row_odd = signed_picks(freq_y, ROWS)
    lanes = np.zeros((LANES, 2 * LANES))
    lanes[:, :freq_x] = col_even.T
    lanes[:, LANES : LANES + freq_x] = col_odd.T
    rows = np.block([[row_even, -row_odd], [-row_odd, -row_even]])
    return lanes, rows


def imaging_kernel(places, used, extra, *refs):
    owner_ref, weight_ref, pieces_ref, kern_ref, table_ref = refs[:5]
    later_hbm, refs = refs[5 : 5 + extra], refs[5 + extra :]
    slopes_ref, error_ref, later_ref, refs = refs[0], refs[1], refs[2 : 2 + extra], refs[2 + extra :]
    spec, field, rim_field, rim_lanes, rim_slope, scale_ref, ready, goal_ref, sems = refs
    kern_count, freq_y, freq_x = kern_ref.shape[2:]
    later = fetch(list(zip(later_hbm, later_ref)), sems)
    chunk = max(size for size in range(1, CHUNK + 1) if kern_count % size == 0)
    count, first, second = tiles_of(owner_ref, own_place())
    slots = (first, second)
    split = freq_y // 2
    firsts = [slot // PIECES * PIECES for slot in slots]

    def table(name):
        start, height, width = places[name]
        return table_ref[start : start + height, :width]

    upper = lax.broadcasted_iota(jnp.int32, (8, LANES), 0) < 4
    for slot in range(MOST):
        target = jnp.concatenate(
            [pieces_ref[firsts[slot] + at, 8 + 8 * slot : 16 + 8 * slot] for at in range(PIECES)], axis=0
        )
        target = jnp.where(slot < count, target, 0.0)
        one = target.astype(BF16)
        target = target - one.astype(F32)
        two = target.astype(BF16)
        three = (target - two.astype(F32)).astype(BF16)
        goal_ref[slot] = mm(table("turn"), one) + mm(table("turn"), two) + mm(table("turn"), three)
        pieces = []
        for at in range(0, PIECES, 2):
            even, odd = pieces_ref[firsts[slot] + at, :8], pieces_ref[firsts[slot] + at + 1, :8]
            if slot == 0:
                pieces.append(jnp.where(upper, even, odd))
            else:
                pieces.append(pltpu.roll(jnp.where(upper, odd, even), 4, 0))
        packet = jnp.concatenate(pieces, axis=0)
        packet = jnp.where(slot < count, unpacked(packet, used), 0.0)
        top, rest = halves(packet)
        both = mm(top, table("lanes")) + mm(rest, table("lanes"))
        tall = jnp.concatenate([both[:, :LANES], both[:, LANES:]], axis=0)
        top, rest = halves(tall)
        spec[slot] = mm(table("picks"), top) + mm(table("picks"), rest)

    half = GRID_Y // 2
    lane = lax.broadcasted_iota(jnp.int32, (freq_y, LANES), 1)
    live_lane = lane < freq_x

    def kern_at(k):
        def one(part):
            raw = kern_ref[0, part, k]
            wide = jnp.concatenate([raw, jnp.zeros((freq_y, LANES - freq_x), F32)], axis=1)
            return wide
        return one(0), one(1)

    def side_by_side(pieces):
        return pieces[0] if len(pieces) == 1 else jnp.concatenate(pieces, axis=1)

    def apart(wide):
        size = 2 * LANES
        return [wide[:, at : at + size] for at in range(0, wide.shape[1], size)]

    def to_image(stacks):
        pieces = []
        for stack in stacks:
            top, rest = halves(stack)
            pieces.append(jnp.concatenate([top, rest, top], axis=0))
        return apart(mm(table("rows"), side_by_side(pieces)))

    def from_image(stacks):
        pieces = [jnp.concatenate(halves(stack), axis=0) for stack in stacks]
        both = mm(table("rows_t"), side_by_side(pieces))
        return apart(both[:freq_y] + both[freq_y:])

    def thrice(top, rest, name):
        both = table(name)
        height = both.shape[0] // 2
        return mm(
            jnp.concatenate([top, rest, top], axis=1),
            jnp.concatenate([both[:height], both[:height], both[height:]], axis=0),
        )

    def waves(stack):
        even_re, even_im = stack[:half, :LANES], stack[:half, LANES:]
        odd_re, odd_im = stack[half:, :LANES], stack[half:, LANES:]
        return even_re - odd_im, even_im + odd_re, even_re + odd_im, even_im - odd_re

    def unwaves(plus_re, plus_im, minus_re, minus_im):
        above = jnp.concatenate([plus_re + minus_re, plus_im + minus_im], axis=1)
        below = jnp.concatenate([plus_im - minus_im, minus_re - plus_re], axis=1)
        return jnp.concatenate([above, below], axis=0)


    def forward_chunk(start, new):
        tops, rests = [], []
        for step in range(chunk):
            kern_re, kern_im = kern_at(start + step)
            for slot in range(MOST):
                spec_re, spec_im = spec[slot, :freq_y], spec[slot, freq_y:]
                wave = jnp.concatenate(
                    [kern_re * spec_re - kern_im * spec_im, kern_re * spec_im + kern_im * spec_re], axis=1
                )
                top, rest = halves(wave)
                tops.append(top)
                rests.append(rest)
        top, rest = jnp.concatenate(tops, axis=0), jnp.concatenate(rests, axis=0)
        cols = thrice(top, rest, "core")
        edges = thrice(top, rest, "rim")
        places = [(step, slot) for step in range(chunk) for slot in range(MOST)]
        images = to_image([cols[at * freq_y : (at + 1) * freq_y] for at in range(len(places))])
        for at, (step, slot) in enumerate(places):
            k = start + step
            weight = weight_ref[k]
            new[2] = jnp.where(group_of == k, weight, new[2])
            edge = edges[at * freq_y : (at + 1) * freq_y]
            for part in range(2):
                here = slice(part * LANES, (part + 1) * LANES)
                if k == 0:
                    rim_lanes[slot, :, here] = edge[:, here]
                else:
                    rim_lanes[slot, :, here] += pltpu.roll(edge[:, here], 4 * k, 1)
            parts = waves(images[at])
            for part in range(4):
                field[slot, k, part] = parts[part]
            plus, minus = new[slot]
            plus = plus + weight * (parts[0] * parts[0] + parts[1] * parts[1])
            minus = minus + weight * (parts[2] * parts[2] + parts[3] * parts[3])
            new[slot] = (plus, minus)

    blank = jnp.zeros((half, LANES), F32)
    group_of = lax.rem(lax.broadcasted_iota(jnp.int32, (8, LANES), 1) + 2, LANES) // 4
    sums = [(blank, blank), (blank, blank), jnp.zeros((8, LANES), F32)]
    for start in range(0, kern_count, chunk):
        forward_chunk(start, sums)
    lane_weight = sums.pop()

    norm = 1.0 / (64.0 * GRID_Y * GRID_X)
    square = norm * norm
    lane_half = lax.broadcasted_iota(jnp.int32, (half, LANES), 1)
    near = (lane_half < 2) | (lane_half >= LANES - 2)
    row_8 = lax.broadcasted_iota(jnp.int32, (8, LANES), 0)

    def rows_beside(value, other):
        first, last = value[:8], value[half - 8 :]
        later = jnp.where(row_8 == 7, last, pltpu.roll(first, 7, 0))
        sooner = jnp.where(row_8 == 0, other[:8], pltpu.roll(last, 1, 0))
        return jnp.concatenate([value[8:], later], axis=0) + jnp.concatenate([sooner, value[:-8]], axis=0)

    at_first, at_last = lane_half == 0, lane_half == LANES - 1

    def spread_out(value, rows, left, right):
        return value + DIFFUSE_RATE * (rows + left + right - 4.0 * value)

    def sides(value):
        return pltpu.roll(value, 1, 1), pltpu.roll(value, LANES - 1, 1)

    def beside(core, rim):
        return jnp.where(at_first, rim[0], core[0]), jnp.where(at_last, rim[1], core[1])

    def blur(core, rim):
        core_sides = [sides(value) for value in core]
        rim_sides = [sides(value) for value in rim]
        rim_one = [
            spread_out(rim[at], rows_beside(rim[at], rim[1 - at]), *beside(rim_sides[at], core_sides[at]))
            for at in range(2)
        ]
        core_one = [
            spread_out(core[at], rows_beside(core[at], core[1 - at]), *beside(core_sides[at], rim_sides[at]))
            for at in range(2)
        ]
        return [
            spread_out(
                core_one[at],
                rows_beside(core_one[at], core_one[1 - at]),
                *beside(sides(core_one[at]), sides(rim_one[at])),
            )
            for at in range(2)
        ]

    def blur_back(core):
        core_sides = [sides(value) for value in core]
        none = jnp.zeros((half, LANES), F32)
        rim_one = [DIFFUSE_RATE * sum(beside((none, none), core_sides[at])) for at in range(2)]
        core_one = [
            spread_out(core[at], rows_beside(core[at], core[1 - at]), *beside(core_sides[at], (none, none)))
            for at in range(2)
        ]
        core_sides = [sides(value) for value in core_one]
        rim_sides = [sides(value) for value in rim_one]
        rim_two = [
            spread_out(rim_one[at], rows_beside(rim_one[at], rim_one[1 - at]), *beside(rim_sides[at], core_sides[at]))
            for at in range(2)
        ]
        core_two = [
            spread_out(core_one[at], rows_beside(core_one[at], core_one[1 - at]), *beside(core_sides[at], rim_sides[at]))
            for at in range(2)
        ]
        return core_two, rim_two

    def fold(value):
        def back(amount):
            return pltpu.roll(value, LANES - amount, 1)
        value = value + back(48)
        value = value + back(24)
        value = value + back(12)
        return value + back(4) + back(8)

    def unfold(value):
        value = jnp.where(near, value, 0.0)
        value = value + pltpu.roll(value, 4, 1) + pltpu.roll(value, 8, 1)
        value = value + pltpu.roll(value, 12, 1)
        value = value + pltpu.roll(value, 24, 1)
        return value + pltpu.roll(value, 48, 1)

    error = jnp.float32(0.0)
    rim_halves = []
    for slot in range(2):
        live = (slot < count).astype(F32)
        rim_parts = waves(to_image([rim_lanes[slot]])[0])
        for part in range(4):
            rim_field[slot, part] = rim_parts[part]
        weights = jnp.concatenate([lane_weight] * (half // 8), axis=0)
        rim_plus = weights * (rim_parts[0] * rim_parts[0] + rim_parts[1] * rim_parts[1])
        rim_minus = weights * (rim_parts[2] * rim_parts[2] + rim_parts[3] * rim_parts[3])
        core = [part * square for part in sums[slot]]
        rim = [jnp.where(near, fold(part), 0.0) * square for part in (rim_plus, rim_minus)]
        core = blur(core, rim)

        def slope_of(value, goal):
            resist = 1.0 / (1.0 + jnp.exp(-RESIST_SLOPE * (value - RESIST_LEVEL)))
            misfit = resist - goal
            return (2.0 * RESIST_SLOPE) * misfit * resist * (1.0 - resist), jnp.sum(misfit * misfit)

        slope_plus, err_plus = slope_of(core[0], goal_ref[slot, :half])
        slope_minus, err_minus = slope_of(core[1], goal_ref[slot, half:])
        error = error + live * (err_plus + err_minus)
        core, rim = blur_back([slope_plus, slope_minus])
        factor = 2.0 * square
        for at in range(2):
            scale_ref[slot, at] = core[at] * factor
        rim_f_plus = unfold(rim[0] * factor) * weights
        rim_f_minus = unfold(rim[1] * factor) * weights
        edge = from_image(
            [
                unwaves(
                    rim_f_plus * rim_field[slot, 0],
                    rim_f_plus * rim_field[slot, 1],
                    rim_f_minus * rim_field[slot, 2],
                    rim_f_minus * rim_field[slot, 3],
                )
            ]
        )[0]
        rim_halves.append(jnp.concatenate(halves(edge), axis=1))
    rim_stack = jnp.concatenate(rim_halves, axis=0)
    for part in range(0, rim_slope.shape[2], 2 * LANES):
        moved = mm(rim_stack, table(f"scatter{part}"))
        for slot in range(MOST):
            rim_slope[slot, :, part : part + moved.shape[1]] = moved[slot * freq_y : (slot + 1) * freq_y]
    error_ref[0] = error * (1.0 / (GRID_Y * CORE_X))


    def backward_chunk(start, sums):
        images, edges = [], []
        for step in range(chunk):
            k = start + step
            weight = weight_ref[k]
            for slot in range(MOST):
                plus = scale_ref[slot, 0] * weight
                minus = scale_ref[slot, 1] * weight
                images.append(
                    unwaves(
                        plus * field[slot, k, 0],
                        plus * field[slot, k, 1],
                        minus * field[slot, k, 2],
                        minus * field[slot, k, 3],
                    )
                )
                column = k // RIM_KERNS * LANES
                edge = rim_slope[slot, :, column : column + LANES]
                if k % RIM_KERNS != 0:
                    edge = pltpu.roll(edge, LANES - k % RIM_KERNS * RIM_WIDTH, 1)
                edge = edge.astype(BF16)
                edges.append(jnp.concatenate([edge, edge], axis=1))
        pairs = [halves(cols) for cols in from_image(images)]
        top, rest = [jnp.concatenate(part, axis=0) for part in zip(*pairs)]
        waves_all = thrice(top, rest, "core_t") + mm(jnp.concatenate(edges, axis=0), table("rim_t"))
        for step in range(chunk):
            kern_re, kern_im = kern_at(start + step)
            for slot in range(MOST):
                at = (MOST * step + slot) * freq_y
                wave_re, wave_im = waves_all[at : at + freq_y, :LANES], waves_all[at : at + freq_y, LANES:]
                sums[slot][0] += wave_re * kern_re + wave_im * kern_im
                sums[slot][1] += wave_im * kern_re - wave_re * kern_im

    slopes = [[jnp.zeros((freq_y, LANES), F32)] * 2 for _ in range(MOST)]
    for start in range(0, kern_count, chunk):
        backward_chunk(start, slopes)

    packets = []
    for slot in range(MOST):
        top, rest = halves(jnp.concatenate(slopes[slot], axis=0))
        tall = mm(table("picks_t"), top) + mm(table("picks_t"), rest)
        wide = jnp.concatenate([tall[:ROWS], tall[ROWS:]], axis=1)
        top, rest = halves(wide)
        packets.append(packed(mm(top, table("lanes_t")) + mm(rest, table("lanes_t")), used))
    for at in range(2):
        here = slice(at * split, (at + 1) * split)
        ready[at] = slot_pair(packets[0][here], packets[1][here], used)

    def give(pair_at, carry):
        slopes_ref[2 * pair_at] = ready[0]
        slopes_ref[2 * pair_at + 1] = ready[1]
        return carry

    lax.fori_loop(0, slopes_ref.shape[0] // 2, give, 0)
    for copy in later:
        copy.wait()


def imaging_table(kern_count, freq_y, freq_x):
    core, rim, rows = image_tables(freq_y, freq_x)
    lanes, picks = pick_tables(freq_y, freq_x)

    def tall(table):
        return np.concatenate(halves_np(table), axis=0)

    def three(table):
        top, rest = halves_np(table)
        return np.concatenate([top, top, rest], axis=1)

    def square_up(table):
        top, rest = halves_np(table)
        return np.block([[top, top], [rest, np.zeros_like(rest)]])

    rim_out, scatter = rim_tables(rim, kern_count)
    tables = {
        "core": tall(core),
        "core_t": tall(core.T),
        "rim": tall(rim),
        "rim_t": rim_out,
        "rows": three(rows),
        "rows_t": square_up(rows.T),
        "lanes": lanes.astype(BF16),
        "lanes_t": lanes.T.astype(BF16),
        "picks": picks.astype(BF16),
        "picks_t": picks.T.astype(BF16),
        "turn": np.eye(GRID_Y)[
            np.concatenate([GRID_Y // 2 + half_order(), GRID_Y // 2 - 1 - half_order()])
        ].astype(BF16),
    }
    for part in range(0, scatter.shape[1], 2 * LANES):
        tables[f"scatter{part}"] = scatter[:, part : part + 2 * LANES]
    places, stacked, start = {}, [], 0
    for name, piece in tables.items():
        height, width = piece.shape
        places[name] = (start, height, width)
        stacked.append(np.pad(piece, ((0, 0), (0, 2 * LANES - width))))
        start += height
    return places, np.concatenate(stacked, axis=0)


def owner_imaging(owner_list, kern_weight, pieces, kernels, places, table, later):
    kern_count, freq_y, freq_x = kernels.shape[2:]
    tiles, split = owner_list.shape[0], freq_y // 2
    half = GRID_Y // 2
    smem = pl.BlockSpec(memory_space=pltpu.SMEM)
    vmem = pl.BlockSpec(memory_space=pltpu.VMEM)
    hbm = pl.BlockSpec(memory_space=pltpu.HBM)
    return pl.pallas_call(
        functools.partial(imaging_kernel, places, freq_x + 1, len(later)),
        in_specs=[smem, smem, vmem, vmem, vmem] + [hbm] * len(later),
        out_specs=(vmem, smem) + (vmem,) * len(later),
        out_shape=(
            jax.ShapeDtypeStruct((tiles, 2 * split - 8, LANES), F32),
            jax.ShapeDtypeStruct((1,), F32),
        )
        + tuple(jax.ShapeDtypeStruct(part.shape, part.dtype) for part in later),
        scratch_shapes=[
            pltpu.VMEM((MOST, 2 * freq_y, LANES), F32),
            pltpu.VMEM((MOST, kern_count, 4, half, LANES), F32),
            pltpu.VMEM((MOST, 4, half, LANES), F32),
            pltpu.VMEM((MOST, freq_y, 2 * LANES), F32),
            pltpu.VMEM((MOST, freq_y, -(-kern_count * RIM_WIDTH // LANES) * LANES), F32),
            pltpu.VMEM((MOST, 2, half, LANES), F32),
            pltpu.VMEM((2, 2 * split - 8, LANES), F32),
            pltpu.VMEM((MOST, 2 * half, LANES), F32),
            pltpu.SemaphoreType.DMA((len(later),)),
        ],
        compiler_params=pltpu.CompilerParams(vmem_limit_bytes=20 * 2**20),
        name="owner_imaging",
    )(
        owner_list, kern_weight, in_vmem(pieces), in_vmem(kernels),
        in_vmem(table), *[in_hbm(part) for part in later],
    )


def on_device(mask_tiles, target_grid, kernels, kern_weight, owner_list):
    tile_px = mask_tiles.shape[1]
    freq_y, freq_x = kernels.shape[3:]
    count = lax.axis_size("tile")
    cols, turns, rows = mask_tables(tile_px, freq_y, freq_x)
    owner_list = owner_list.reshape(-1)
    mates = [(i, i + 1 - 2 * (i % 2)) for i in range(count)]

    pieces = mask_spectrum(mask_tiles, target_grid.reshape(GRID_Y, CORE_X), cols, turns, rows, freq_x)
    places, table = imaging_table(kernels.shape[2], freq_y, freq_x)
    pieces, table = lax.optimization_barrier((pieces, jnp.asarray(table)))
    if count == PIECES:
        pieces, edges = lax.all_to_all(pieces, "tile", 0, 0, tiled=True), None
    else:
        groups = [list(range(at, at + PIECES)) for at in range(0, count, PIECES)]
        pieces = lax.all_to_all(pieces, "tile", 0, 0, axis_index_groups=groups, tiled=True)
        later = [(i, i + PIECES) for i in range(count - PIECES)]
        sooner = [(i + PIECES, i) for i in range(count - PIECES)]
        edges = jnp.stack(
            [lax.ppermute(pieces[PIECES - 1], "tile", later), lax.ppermute(pieces[0], "tile", sooner)]
        )
    pieces = lax.all_to_all(route(owner_list, pieces, edges), "tile", 0, 0, tiled=True)
    slopes, owner_error, *held = owner_imaging(
        owner_list, kern_weight, pieces, kernels, places, table,
        (mask_tiles,) + update_tables(cols, turns, rows),
    )
    slopes = lax.all_to_all(slopes, "tile", 0, 0, tiled=True)
    other = lax.ppermute(tile_pick(owner_list, slopes, freq_x), "tile", mates)
    current = mask_update(owner_list, slopes, other, *held, freq_x)
    return (current, owner_error)


def solution(mesh):
    placed = (
        P(("stripe", "tile"), None, None),
        P(("stripe", "tile"), None),
        P("tile", None, None, None, None),
        P(),
        P("stripe", None),
    )
    return jax.shard_map(
        on_device,
        mesh=mesh,
        in_specs=placed,
        out_specs=(P(("stripe", "tile"), None, None), P(("stripe", "tile"))),
        check_vma=False,
    )
```

```python
import functools

import jax
import jax.numpy as jnp
import numpy as np
from jax import lax
from jax.experimental import pallas as pl
from jax.experimental.pallas import tpu as pltpu
from jax.sharding import PartitionSpec as P

AMBIT = 256
GRID_X = 192
GRID_Y = 128
CORE_X = 128
RESIST_SLOPE = 3.0
RESIST_LEVEL = 1.2
DIFFUSE_RATE = 0.2
STEP_SIZE = 1.0

LANES = 128
MOST = 2
BLOCKS = 4
PIECES = 16
CHUNK = 6
QUARTER = 32
RIM_WIDTH = 16
RIM_KERNS = LANES // RIM_WIDTH
ROWS = 72
ROWS_PAD = 80
F32 = jnp.float32
BF16 = jnp.bfloat16


def halves_np(table):
    table = np.asarray(table, np.float32)
    top = table.astype(BF16)
    rest = (table - top.astype(np.float32)).astype(BF16)
    return top, rest


def halves(value):
    top = value.astype(BF16)
    rest = (value - top.astype(F32)).astype(BF16)
    return top, rest


def mm(left, right):
    return jnp.dot(left, right, preferred_element_type=F32)


def in_hbm(value):
    return pltpu.with_memory_space_constraint(jnp.asarray(value), pltpu.HBM)


def in_vmem(value):
    return pltpu.with_memory_space_constraint(jnp.asarray(value), pltpu.VMEM)


def real_waves(places, period, most, width):
    angles = 2.0 * np.pi * np.outer(places, np.arange(most + 1)) / period
    waves = np.concatenate([np.cos(angles), np.sin(angles[:, 1:])], axis=1)
    return np.pad(waves, ((0, 0), (0, width - waves.shape[1])))


def signed_picks(count, width):
    freqs = np.arange(count) - count // 2
    most = count // 2
    even = np.zeros((count, width))
    odd = np.zeros((count, width))
    for at, freq in enumerate(freqs):
        even[at, abs(freq)] = 1.0
        if freq != 0:
            odd[at, most + abs(freq)] = np.sign(freq)
    return even, odd


def mask_tables(tile_px, freq_y, freq_x):
    win = tile_px + 2 * AMBIT
    mid_x = (GRID_X - 1) / 2 * (win // GRID_X)
    mid_y = (GRID_Y - 1) / 2 * (tile_px // GRID_Y)
    most = freq_x // 2
    cols = real_waves(np.arange(AMBIT), win, most, LANES)
    rows = real_waves(np.arange(tile_px) - mid_y, tile_px, freq_y // 2, ROWS_PAD)
    blocks = win // AMBIT
    angles = 2.0 * np.pi * np.outer(AMBIT * np.arange(blocks) - mid_x, np.arange(most + 1)) / win
    turns = np.zeros((2, blocks, LANES))
    turns[0, :, : most + 1] = np.cos(angles)
    turns[0, :, most + 1 : 2 * most + 1] = np.cos(angles[:, 1:])
    turns[1, :, : most + 1] = -np.sin(angles)
    turns[1, :, most + 1 : 2 * most + 1] = np.sin(angles[:, 1:])
    return cols, turns.astype(np.float32).reshape(2 * blocks, 1, LANES), rows


def swapped(value, used):
    lane = lax.broadcasted_iota(jnp.int32, value.shape, 1)
    most = (used - 1) // 2
    return jnp.where(lane <= most, pltpu.roll(value, LANES - most, 1), pltpu.roll(value, most, 1))


def packed(tall, used):
    rows = tall.shape[0] - 8
    body, line = tall[:rows], jnp.broadcast_to(tall[rows : rows + 1], (8, LANES))
    lane = lax.broadcasted_iota(jnp.int32, (8, LANES), 1)
    row = lax.broadcasted_iota(jnp.int32, (8, LANES), 0)
    spare = LANES - used
    first = jnp.where(lane < used, body[:8], 0.0)
    for at in range(-(-used // spare)):
        moved = pltpu.roll(line, (used - spare * at) % LANES, 1)
        first = jnp.where((row == at) & (lane >= used), moved, first)
    return jnp.concatenate([first, body[8:]], axis=0)


def unpacked(packet, used):
    lane = lax.broadcasted_iota(jnp.int32, packet.shape, 1)
    first = packet[:8]
    lane8 = lane[:8]
    row = lax.broadcasted_iota(jnp.int32, (8, LANES), 0)
    spare = LANES - used
    line = jnp.zeros((8, LANES), F32)
    for at in range(-(-used // spare)):
        moved = pltpu.roll(first, (spare * at - used) % LANES, 1)
        here = (row == at) & (lane8 >= spare * at) & (lane8 < min(spare * at + spare, used))
        line = line + jnp.where(here, moved, 0.0)
    line = jnp.where(row == 0, jnp.sum(line, axis=0, keepdims=True), 0.0)
    return jnp.concatenate([jnp.where(lane < used, packet, 0.0), line], axis=0)


def own_place():
    return lax.axis_index("tile").astype(jnp.int32)


def fetch(pairs, sems):
    copies = [pltpu.make_async_copy(src, dst, sems.at[at]) for at, (src, dst) in enumerate(pairs)]
    for copy in copies:
        copy.start()
    return copies


def spectrum_kernel(
    used, mask_hbm, cols_hbm, turns_hbm, rows_hbm, target_hbm, out_ref, mask, cols, turns, rows, sems, target_sems
):
    tile_px = mask.shape[0]
    width = AMBIT
    count = tile_px // width
    pairs = [(rows_hbm, rows)]
    for at in range(count):
        place = pl.ds(at * width, width)
        pairs.append((mask_hbm.at[0, :, place], mask.at[:, place]))
    pairs[2:2] = [(cols_hbm, cols), (turns_hbm, turns)]
    copies = fetch(pairs, sems)
    table_copies = [copies.pop(2), copies.pop(2)]
    size = target_hbm.shape[0] // PIECES
    goals = fetch(
        [(target_hbm.at[pl.ds(at * size, size)], out_ref.at[at, pl.ds(16, size)]) for at in range(PIECES)],
        target_sems,
    )

    def turned(both, block):
        return turns[block] * both[0] + turns[block + turns.shape[0] // 2] * both[1]

    copies[0].wait()
    terms = []
    for at in range(count):
        copies[1 + at].wait()
        top, rest = halves(mask[:, at * width : (at + 1) * width])
        both = mm(rows[...], top)
        top, rest = halves(both[:ROWS_PAD] + both[ROWS_PAD:] + mm(rows[:ROWS_PAD], rest))
        terms.append(jnp.concatenate([top, rest, top], axis=1))

    for copy in table_copies:
        copy.wait()
    table = jnp.concatenate([cols[:, :LANES], cols[:, :LANES], cols[:, LANES:]], axis=0)
    waves = []
    for some in (terms,):
        wave = mm(jnp.concatenate(some, axis=0), table)
        waves += [wave[at * ROWS_PAD : (at + 1) * ROWS_PAD] for at in range(len(some))]
    waves = [(wave, swapped(wave, used)) for wave in waves]
    own = sum(turned(wave, at + 1) for at, wave in enumerate(waves))
    low, high = turned(waves[0], count + 1), turned(waves[-1], 0)

    own, low, high = [packed(part[:ROWS], used) for part in (own, low, high)]
    groups = own.shape[0] // 8
    low = pltpu.roll(low.reshape(groups, 8, LANES), 4, 1)
    upper = lax.broadcasted_iota(jnp.int32, (8, LANES), 0) < 4
    for at in range(groups):
        mine, other = own[8 * at : 8 * at + 8], low[at]
        out_ref[2 * at, :8] = jnp.where(upper, mine, other)
        out_ref[2 * at + 1, :8] = jnp.where(upper, other, mine)
        out_ref[2 * at, 8:16] = high[8 * at : 8 * at + 8]
        out_ref[2 * at + 1, 8:16] = high[8 * at : 8 * at + 8]
    for copy in goals:
        copy.wait()


def mask_spectrum(mask_tiles, target, cols, turns, rows, freq_x):
    tile_px = mask_tiles.shape[1]
    col_stack = np.concatenate(halves_np(cols), axis=1)
    row_stack = np.concatenate(halves_np(rows.T), axis=0)
    hbm = pl.BlockSpec(memory_space=pltpu.HBM)
    return pl.pallas_call(
        functools.partial(spectrum_kernel, freq_x + 1),
        in_specs=[hbm] * 5,
        out_specs=pl.BlockSpec(memory_space=pltpu.VMEM),
        out_shape=jax.ShapeDtypeStruct((PIECES, 24, LANES), F32),
        scratch_shapes=[
            pltpu.VMEM((tile_px, tile_px), F32),
            pltpu.VMEM(col_stack.shape, BF16),
            pltpu.VMEM(turns.shape, F32),
            pltpu.VMEM(row_stack.shape, BF16),
            pltpu.SemaphoreType.DMA((3 + tile_px // AMBIT,)),
            pltpu.SemaphoreType.DMA((PIECES,)),
        ],
        compiler_params=pltpu.CompilerParams(vmem_limit_bytes=20 * 2**20),
        name="mask_spectrum",
    )(in_hbm(mask_tiles), in_hbm(col_stack), in_hbm(turns), in_hbm(row_stack), in_hbm(target))


def slot_pair(first, second, used):
    spare = LANES - used
    lane = lax.broadcasted_iota(jnp.int32, (8, LANES), 1)
    groups = [part[at : at + 8] for part in (first, second) for at in range(0, part.shape[0], 8)]
    last = groups.pop()
    for at, host in enumerate((1, 2, 3, 5)):
        groups[host] = jnp.where(lane < used, groups[host], pltpu.roll(last, (used - spare * at) % LANES, 1))
    return jnp.concatenate(groups, axis=0)


def slot_half(pair, slot, used):
    spare = LANES - used
    lane = lax.broadcasted_iota(jnp.int32, (8, LANES), 1)
    last = jnp.zeros((8, LANES), F32)
    for at, host in enumerate((1, 2, 3, 5)):
        moved = pltpu.roll(pair[8 * host : 8 * host + 8], (spare * at - used) % LANES, 1)
        last = jnp.where((lane >= spare * at) & (lane < min(spare * at + spare, used)), moved, last)
    return jnp.where(slot == 0, pair[:32], jnp.concatenate([pair[32:], last], axis=0))


def each(count, body, carry):
    if count > PIECES:
        return lax.fori_loop(0, count, body, carry)
    for at in range(count):
        carry = body(jnp.int32(at), carry)
    return carry


def slots_of(owner_ref, tiles):
    owners = [owner_ref[tile] for tile in tiles]

    def count(other, before):
        held = owner_ref[other]
        return tuple(
            seen + ((held == owner) & (other < tile)).astype(jnp.int32)
            for seen, owner, tile in zip(before, owners, tiles)
        )

    ranks = each(owner_ref.shape[0], count, (jnp.int32(0),) * len(tiles))
    return list(zip(owners, ranks))


def tiles_of(owner_ref, owner):
    def find(tile, carry):
        count, first, second = carry
        mine = owner_ref[tile] == owner
        first = jnp.where(mine & (count == 0), tile, first)
        second = jnp.where(mine & (count == 1), tile, second)
        return count + mine.astype(jnp.int32), first, second

    zero = jnp.int32(0)
    return lax.fori_loop(0, owner_ref.shape[0], find, (zero, zero, zero))


def mate_of(me):
    return me + 1 - 2 * lax.rem(me, 2)


def route_kernel(owner_ref, pieces_ref, *rest):
    edges_ref = rest[0] if len(rest) == 3 else None
    out_ref, seen = rest[-2:]
    tiles = owner_ref.shape[0]
    me = own_place()
    base = me // PIECES * PIECES if tiles > PIECES else 0
    row = lax.broadcasted_iota(jnp.int32, (8, LANES), 0)
    mine = row // 4 == lax.rem(me, 2)

    def clear(at, carry):
        seen[at] = 0
        return carry

    each(tiles, clear, 0)

    def send(tile, carry):
        owner = owner_ref[tile]
        slot = seen[owner]
        seen[owner] = slot + 1
        at = tile - base

        def forward():
            high = pieces_ref[jnp.maximum(at - 1, 0), 8:16]
            low = pieces_ref[jnp.minimum(at + 1, PIECES - 1), :8]
            if edges_ref is None:
                edge_high, edge_low = jnp.zeros_like(high), jnp.zeros_like(low)
            else:
                edge_high, edge_low = edges_ref[0, 8:16], edges_ref[1, :8]
            high = jnp.where(at > 0, high, edge_high)
            low = jnp.where(at < PIECES - 1, low, edge_low)
            packet = pieces_ref[at, :8] + high + pltpu.roll(low, 4, 0)
            beside = jnp.where(mine, out_ref[owner, :8], pltpu.roll(packet, 4, 0))
            out_ref[owner, :8] = jnp.where(slot == 0, packet, beside)
            out_ref[owner, pl.ds(pl.multiple_of(8 + 8 * slot, 8), 8)] = pieces_ref[at, 16:]

        if tiles > PIECES:
            pl.when((at >= 0) & (at < PIECES))(forward)
        else:
            forward()
        return carry

    each(tiles, send, 0)


def route(owner_list, pieces, edges):
    smem = pl.BlockSpec(memory_space=pltpu.SMEM)
    vmem = pl.BlockSpec(memory_space=pltpu.VMEM)
    tiles = owner_list.shape[0]
    extra = [] if edges is None else [edges]
    return pl.pallas_call(
        route_kernel,
        in_specs=[smem, vmem] + [vmem] * len(extra),
        out_specs=vmem,
        out_shape=jax.ShapeDtypeStruct((tiles, 24, LANES), F32),
        scratch_shapes=[pltpu.SMEM((tiles,), jnp.int32)],
        compiler_params=pltpu.CompilerParams(vmem_limit_bytes=2**20),
        name="route",
    )(owner_list, in_vmem(pieces), *extra)


def around(tile, tiles):
    return [
        (tile, None),
        (jnp.maximum(tile - 1, 0), tile > 0),
        (jnp.minimum(tile + 1, tiles - 1), tile < tiles - 1),
    ]


def tile_pick_kernel(used, owner_ref, slopes_ref, out_ref):
    tiles = [tile for tile, _ in around(mate_of(own_place()), owner_ref.shape[0])]
    for at, (owner, slot) in enumerate(slots_of(owner_ref, tiles)):
        out_ref[at] = slot_half(slopes_ref[owner], slot, used)


def tile_pick(owner_list, slopes, freq_x):
    smem = pl.BlockSpec(memory_space=pltpu.SMEM)
    vmem = pl.BlockSpec(memory_space=pltpu.VMEM)
    return pl.pallas_call(
        functools.partial(tile_pick_kernel, freq_x + 1),
        in_specs=[smem, vmem],
        out_specs=vmem,
        out_shape=jax.ShapeDtypeStruct((3, 32, LANES), F32),
        compiler_params=pltpu.CompilerParams(vmem_limit_bytes=2**20),
        name="tile_pick",
    )(owner_list, in_vmem(slopes))


def joined(me, mine, other):
    odd = lax.rem(me, 2) == 1
    return jnp.concatenate([jnp.where(odd, other, mine), jnp.where(odd, mine, other)], axis=0)


def update_kernel(
    used, owner_ref, slopes_ref, other_ref, mask_ref, cols, turns, rows, out_hbm, out, held, out_sems
):
    tile_px = out.shape[0]
    block = tile_px // BLOCKS
    me = own_place()
    near = around(me, owner_ref.shape[0])
    packets = []
    for at, (owner, slot) in enumerate(slots_of(owner_ref, [tile for tile, _ in near])):
        packet = unpacked(joined(me, slot_half(slopes_ref[owner], slot, used), other_ref[at]), used)
        there = near[at][1]
        packets.append(packet if there is None else jnp.where(there, packet, 0.0))

    own, last, following = [(packet, swapped(packet, used)) for packet in packets]

    def turned_back(both, block):
        return turns[block] * both[0] - turns[block + turns.shape[0] // 2] * both[1]

    count = tile_px // AMBIT
    waves = [turned_back(own, at + 1) for at in range(count)]
    waves[0] = waves[0] + turned_back(last, count + 1)
    waves[-1] = waves[-1] + turned_back(following, 0)
    blank = jnp.zeros((ROWS_PAD - ROWS, LANES), F32)
    top, rest = halves(jnp.concatenate([part for wave in waves for part in (wave, blank)], axis=0))
    wide = mm(
        jnp.concatenate([top, rest, top], axis=1),
        jnp.concatenate([cols[:LANES], cols[:LANES], cols[LANES:]], axis=0),
    )
    for at in range(count):
        top, rest = halves(wide[at * ROWS_PAD : (at + 1) * ROWS_PAD])
        held[:, at * AMBIT : (at + 1) * AMBIT] = jnp.concatenate([top, rest, top], axis=0)
    sent = []
    for at in range(BLOCKS):
        here = slice(at * block, (at + 1) * block)
        place = pl.ds(at * block, block)
        out[here] = mask_ref[0, here] - STEP_SIZE * mm(rows[here], held[...])
        copy = pltpu.make_async_copy(out.at[place], out_hbm.at[0, place], out_sems.at[at])
        copy.start()
        sent.append(copy)
    for copy in sent:
        copy.wait()


def update_tables(cols, turns, rows):
    top, rest = halves_np(rows)
    return (
        np.concatenate(halves_np(cols.T), axis=0),
        turns,
        np.concatenate([top, top, rest], axis=1),
    )


def mask_update(owner_list, slopes, other, mask_tiles, cols, turns, rows, freq_x):
    tile_px = mask_tiles.shape[1]
    smem = pl.BlockSpec(memory_space=pltpu.SMEM)
    vmem = pl.BlockSpec(memory_space=pltpu.VMEM)
    hbm = pl.BlockSpec(memory_space=pltpu.HBM)
    return pl.pallas_call(
        functools.partial(update_kernel, freq_x + 1),
        in_specs=[smem] + [vmem] * 6,
        out_specs=hbm,
        out_shape=jax.ShapeDtypeStruct(mask_tiles.shape, F32),
        scratch_shapes=[
            pltpu.VMEM((tile_px, tile_px), F32),
            pltpu.VMEM((3 * ROWS_PAD, tile_px), BF16),
            pltpu.SemaphoreType.DMA((BLOCKS,)),
        ],
        compiler_params=pltpu.CompilerParams(vmem_limit_bytes=16 * 2**20),
        name="mask_update",
    )(
        owner_list, in_vmem(slopes), other, in_vmem(mask_tiles),
        in_vmem(cols), in_vmem(turns), in_vmem(rows),
    )


def half_order():
    return np.arange(GRID_Y // 2).reshape(8, -1).T.reshape(-1)


def image_tables(freq_y, freq_x):
    places_v = np.arange(GRID_X) - (GRID_X - 1) / 2
    freqs_b = np.arange(freq_x) - (freq_x - 1) / 2
    beta = 2.0 * np.pi * np.outer(freqs_b, places_v) / GRID_X
    first = (GRID_X - CORE_X) // 2

    def block(lane_of):
        table = np.zeros((2 * LANES, 2 * LANES))
        for place, lane in lane_of:
            table[:freq_x, lane] = np.cos(beta[:, place])
            table[:freq_x, LANES + lane] = np.sin(beta[:, place])
            table[LANES : LANES + freq_x, lane] = -np.sin(beta[:, place])
            table[LANES : LANES + freq_x, LANES + lane] = np.cos(beta[:, place])
        return table

    core = block([(first + lane, lane) for lane in range(CORE_X)])
    last = first + CORE_X
    rim = block(
        [(first - 2, LANES - 2), (first - 1, LANES - 1), (last, 0), (last + 1, 1)]
    )
    places_u = half_order() + 0.5
    freqs_a = np.arange(freq_y) - (freq_y - 1) / 2
    alpha = 2.0 * np.pi * np.outer(places_u, freqs_a) / GRID_Y
    rows = np.concatenate([np.cos(alpha), np.sin(alpha)], axis=0)
    return core, rim, rows


def rim_tables(rim, kern_count):
    seats = [(LANES - 2 + at) % LANES for at in range(4)]
    top, rest = halves_np(rim)
    rim_in = np.zeros((4 * LANES, LANES), BF16)
    for seat in seats:
        for quarter, source in enumerate((seat, LANES + seat)):
            place = (seat + quarter * QUARTER) % LANES
            rim_in[: 2 * LANES, place] = top[:, source]
            rim_in[2 * LANES :, place] = top[:, source]
            rim_in[: 2 * LANES, (place + 2 * QUARTER) % LANES] = rest[:, source]
    seats = seats + [LANES + seat for seat in seats]
    top, rest = halves_np(rim.T[seats])
    blank = np.zeros((LANES - 8, 2 * LANES), BF16)
    rim_out = np.concatenate([top, top, blank[8:], rest, blank], axis=0)
    width = -(-kern_count * RIM_WIDTH // LANES) * LANES
    scatter = np.zeros((4 * LANES, width))
    for kern in range(kern_count):
        for at in range(8):
            lane = (4 * kern - 2 + at % 4) % LANES + at // 4 * LANES
            scatter[lane, kern * RIM_WIDTH + at] = 1.0
            scatter[2 * LANES + lane, kern * RIM_WIDTH + 8 + at] = 1.0
    return rim_in, rim_out, scatter.astype(BF16)


def pick_tables(freq_y, freq_x):
    col_even, col_odd = signed_picks(freq_x, LANES)
    row_even, row_odd = signed_picks(freq_y, ROWS_PAD)
    lanes = np.zeros((LANES, 2 * LANES))
    lanes[:, :freq_x] = col_even.T
    lanes[:, LANES : LANES + freq_x] = col_odd.T
    rows = np.block([[row_even, -row_odd], [-row_odd, -row_even]])
    return lanes, rows


def imaging_kernel(places, used, extra, *refs):
    owner_ref, weight_ref, pieces_ref, kern_ref, table_ref = refs[:5]
    later_hbm, refs = refs[5 : 5 + extra], refs[5 + extra :]
    slopes_ref, error_ref, later_ref, refs = refs[0], refs[1], refs[2 : 2 + extra], refs[2 + extra :]
    spec, field, rim_field, rim_lanes, rim_slope, scale_ref, ready, goal_ref, sems = refs
    kern_count, freq_y, freq_x = kern_ref.shape[2:]
    later = fetch(list(zip(later_hbm, later_ref)), sems)
    chunk = max(size for size in range(1, CHUNK + 1) if kern_count % size == 0)
    count, first, second = tiles_of(owner_ref, own_place())
    slots = (first, second)
    split = freq_y // 2
    firsts = [slot // PIECES * PIECES for slot in slots]

    def table(name):
        start, height, width = places[name]
        return table_ref[start : start + height, :width]

    upper = lax.broadcasted_iota(jnp.int32, (8, LANES), 0) < 4
    blank = jnp.zeros((ROWS_PAD - ROWS, LANES), F32)
    targets, packets = [], []
    for slot in range(MOST):
        target = jnp.concatenate(
            [pieces_ref[firsts[slot] + at, 8 + 8 * slot : 16 + 8 * slot] for at in range(PIECES)], axis=0
        )
        targets.append(jnp.where(slot < count, target, 0.0))
        pieces = []
        for at in range(0, PIECES, 2):
            even, odd = pieces_ref[firsts[slot] + at, :8], pieces_ref[firsts[slot] + at + 1, :8]
            if slot == 0:
                pieces.append(jnp.where(upper, even, odd))
            else:
                pieces.append(pltpu.roll(jnp.where(upper, odd, even), 4, 0))
        packet = jnp.concatenate(pieces, axis=0)
        packets += [jnp.where(slot < count, unpacked(packet, used), 0.0), blank]

    top, rest = halves(jnp.concatenate(packets, axis=0))
    both = mm(
        jnp.concatenate([top, rest], axis=1), jnp.concatenate([table("lanes"), table("lanes")], axis=0)
    )
    tall = [
        jnp.concatenate([both[at : at + ROWS_PAD, :LANES], both[at : at + ROWS_PAD, LANES:]], axis=0)
        for at in range(0, MOST * ROWS_PAD, ROWS_PAD)
    ]
    top, rest = halves(jnp.concatenate(tall, axis=1))
    both = mm(table("picks"), top) + mm(table("picks"), rest)
    for slot in range(MOST):
        spec[slot] = both[:, slot * LANES : (slot + 1) * LANES]

    target = jnp.concatenate(targets, axis=1)
    one = target.astype(BF16)
    target = target - one.astype(F32)
    two = target.astype(BF16)
    three = (target - two.astype(F32)).astype(BF16)
    both = mm(table("turn"), one) + mm(table("turn"), two) + mm(table("turn"), three)
    for slot in range(MOST):
        goal_ref[slot] = both[:, slot * LANES : (slot + 1) * LANES]

    half = GRID_Y // 2
    lane = lax.broadcasted_iota(jnp.int32, (freq_y, LANES), 1)
    live_lane = lane < freq_x

    def kern_at(k):
        def one(part):
            raw = kern_ref[0, part, k]
            wide = jnp.concatenate([raw, jnp.zeros((freq_y, LANES - freq_x), F32)], axis=1)
            return wide
        return one(0), one(1)

    def side_by_side(pieces):
        return pieces[0] if len(pieces) == 1 else jnp.concatenate(pieces, axis=1)

    def apart(wide):
        size = 2 * LANES
        return [wide[:, at : at + size] for at in range(0, wide.shape[1], size)]

    def to_image(stacks):
        pieces = []
        for stack in stacks:
            top, rest = halves(stack)
            pieces.append(jnp.concatenate([top, rest, top], axis=0))
        return apart(mm(table("rows"), side_by_side(pieces)))

    def from_image(stacks):
        pieces = [jnp.concatenate(halves(stack), axis=0) for stack in stacks]
        both = mm(table("rows_t"), side_by_side(pieces))
        return apart(both[:freq_y] + both[freq_y:])

    def thrice(top, rest, name):
        both = table(name)
        height = both.shape[0] // 2
        return mm(
            jnp.concatenate([top, rest, top], axis=1),
            jnp.concatenate([both[:height], both[:height], both[height:]], axis=0),
        )

    def waves(stack):
        even_re, even_im = stack[:half, :LANES], stack[:half, LANES:]
        odd_re, odd_im = stack[half:, :LANES], stack[half:, LANES:]
        return even_re - odd_im, even_im + odd_re, even_re + odd_im, even_im - odd_re

    def unwaves(plus_re, plus_im, minus_re, minus_im):
        above = jnp.concatenate([plus_re + minus_re, plus_im + minus_im], axis=1)
        below = jnp.concatenate([plus_im - minus_im, minus_re - plus_re], axis=1)
        return jnp.concatenate([above, below], axis=0)


    def forward_chunk(start, new):
        tops, rests = [], []
        for step in range(chunk):
            kern_re, kern_im = kern_at(start + step)
            for slot in range(MOST):
                spec_re, spec_im = spec[slot, :freq_y], spec[slot, freq_y:]
                wave = jnp.concatenate(
                    [kern_re * spec_re - kern_im * spec_im, kern_re * spec_im + kern_im * spec_re], axis=1
                )
                top, rest = halves(wave)
                tops.append(top)
                rests.append(rest)
        top, rest = jnp.concatenate(tops, axis=0), jnp.concatenate(rests, axis=0)
        cols = thrice(top, rest, "core")
        edges = mm(jnp.concatenate([top, rest], axis=1), table("rim"))
        places = [(step, slot) for step in range(chunk) for slot in range(MOST)]
        images = to_image([cols[at * freq_y : (at + 1) * freq_y] for at in range(len(places))])
        for at, (step, slot) in enumerate(places):
            k = start + step
            weight = weight_ref[k]
            new[2] = jnp.where(group_of == k, weight, new[2])
            edge = edges[at * freq_y : (at + 1) * freq_y]
            column, place = divmod(k, QUARTER // 4)
            here = slice(column * LANES, (column + 1) * LANES)
            if place == 0:
                rim_lanes[slot, :, here] = edge
            else:
                rim_lanes[slot, :, here] += pltpu.roll(edge, 4 * place, 1)
            parts = waves(images[at])
            for part in range(4):
                field[slot, k, part] = parts[part]
            plus, minus = new[slot]
            plus = plus + weight * (parts[0] * parts[0] + parts[1] * parts[1])
            minus = minus + weight * (parts[2] * parts[2] + parts[3] * parts[3])
            new[slot] = (plus, minus)

    blank = jnp.zeros((half, LANES), F32)
    group_of = lax.rem(lax.broadcasted_iota(jnp.int32, (8, LANES), 1) + 2, LANES) // 4
    sums = [(blank, blank), (blank, blank), jnp.zeros((8, LANES), F32)]
    for start in range(0, kern_count, chunk):
        forward_chunk(start, sums)
    lane_weight = sums.pop()

    norm = 1.0 / (64.0 * GRID_Y * GRID_X)
    square = norm * norm
    lane_half = lax.broadcasted_iota(jnp.int32, (half, LANES), 1)
    near = (lane_half < 2) | (lane_half >= LANES - 2)
    row_8 = lax.broadcasted_iota(jnp.int32, (8, LANES), 0)

    def rows_beside(value, other):
        first, last = value[:8], value[half - 8 :]
        later = jnp.where(row_8 == 7, last, pltpu.roll(first, 7, 0))
        sooner = jnp.where(row_8 == 0, other[:8], pltpu.roll(last, 1, 0))
        return jnp.concatenate([value[8:], later], axis=0) + jnp.concatenate([sooner, value[:-8]], axis=0)

    at_first, at_last = lane_half == 0, lane_half == LANES - 1

    def spread_out(value, rows, left, right):
        return value + DIFFUSE_RATE * (rows + left + right - 4.0 * value)

    def sides(value):
        return pltpu.roll(value, 1, 1), pltpu.roll(value, LANES - 1, 1)

    def beside(core, rim):
        return jnp.where(at_first, rim[0], core[0]), jnp.where(at_last, rim[1], core[1])

    def blur(core, rim):
        core_sides = [sides(value) for value in core]
        rim_sides = [sides(value) for value in rim]
        rim_one = [
            spread_out(rim[at], rows_beside(rim[at], rim[1 - at]), *beside(rim_sides[at], core_sides[at]))
            for at in range(2)
        ]
        core_one = [
            spread_out(core[at], rows_beside(core[at], core[1 - at]), *beside(core_sides[at], rim_sides[at]))
            for at in range(2)
        ]
        return [
            spread_out(
                core_one[at],
                rows_beside(core_one[at], core_one[1 - at]),
                *beside(sides(core_one[at]), sides(rim_one[at])),
            )
            for at in range(2)
        ]

    def blur_back(core):
        core_sides = [sides(value) for value in core]
        none = jnp.zeros((half, LANES), F32)
        rim_one = [DIFFUSE_RATE * sum(beside((none, none), core_sides[at])) for at in range(2)]
        core_one = [
            spread_out(core[at], rows_beside(core[at], core[1 - at]), *beside(core_sides[at], (none, none)))
            for at in range(2)
        ]
        core_sides = [sides(value) for value in core_one]
        rim_sides = [sides(value) for value in rim_one]
        rim_two = [
            spread_out(rim_one[at], rows_beside(rim_one[at], rim_one[1 - at]), *beside(rim_sides[at], core_sides[at]))
            for at in range(2)
        ]
        core_two = [
            spread_out(core_one[at], rows_beside(core_one[at], core_one[1 - at]), *beside(core_sides[at], rim_sides[at]))
            for at in range(2)
        ]
        return core_two, rim_two

    def fold(value):
        def back(amount):
            return pltpu.roll(value, LANES - amount, 1)
        value = value + back(48)
        value = value + back(24)
        value = value + back(12)
        return value + back(4) + back(8)

    def unfold(value):
        value = jnp.where(near, value, 0.0)
        value = value + pltpu.roll(value, 4, 1) + pltpu.roll(value, 8, 1)
        value = value + pltpu.roll(value, 12, 1)
        value = value + pltpu.roll(value, 24, 1)
        return value + pltpu.roll(value, 48, 1)

    def rim_columns(slot):
        quarter = lax.rem(lane + 2, LANES) // QUARTER
        real = imag = jnp.zeros((freq_y, LANES), F32)
        for column in range(rim_lanes.shape[2] // LANES):
            both = rim_lanes[slot, :, column * LANES : (column + 1) * LANES]
            both = both + pltpu.roll(both, 2 * QUARTER, 1)
            for_real = both if column == 0 else pltpu.roll(both, column * QUARTER, 1)
            for_imag = both if column == 1 else pltpu.roll(both, (column - 1) * QUARTER % LANES, 1)
            real = jnp.where(quarter == column, for_real, real)
            imag = jnp.where(quarter == column, for_imag, imag)
        return jnp.concatenate([real, imag], axis=1)

    error = jnp.float32(0.0)
    rim_halves = []
    for slot in range(2):
        live = (slot < count).astype(F32)
        rim_parts = waves(to_image([rim_columns(slot)])[0])
        for part in range(4):
            rim_field[slot, part] = rim_parts[part]
        weights = jnp.concatenate([lane_weight] * (half // 8), axis=0)
        rim_plus = weights * (rim_parts[0] * rim_parts[0] + rim_parts[1] * rim_parts[1])
        rim_minus = weights * (rim_parts[2] * rim_parts[2] + rim_parts[3] * rim_parts[3])
        core = [part * square for part in sums[slot]]
        rim = [jnp.where(near, fold(part), 0.0) * square for part in (rim_plus, rim_minus)]
        core = blur(core, rim)

        def slope_of(value, goal):
            resist = 1.0 / (1.0 + jnp.exp(-RESIST_SLOPE * (value - RESIST_LEVEL)))
            misfit = resist - goal
            return (2.0 * RESIST_SLOPE) * misfit * resist * (1.0 - resist), jnp.sum(misfit * misfit)

        slope_plus, err_plus = slope_of(core[0], goal_ref[slot, :half])
        slope_minus, err_minus = slope_of(core[1], goal_ref[slot, half:])
        error = error + live * (err_plus + err_minus)
        core, rim = blur_back([slope_plus, slope_minus])
        factor = 2.0 * square
        for at in range(2):
            scale_ref[slot, at] = core[at] * factor
        rim_f_plus = unfold(rim[0] * factor) * weights
        rim_f_minus = unfold(rim[1] * factor) * weights
        edge = from_image(
            [
                unwaves(
                    rim_f_plus * rim_field[slot, 0],
                    rim_f_plus * rim_field[slot, 1],
                    rim_f_minus * rim_field[slot, 2],
                    rim_f_minus * rim_field[slot, 3],
                )
            ]
        )[0]
        rim_halves.append(jnp.concatenate(halves(edge), axis=1))
    rim_stack = jnp.concatenate(rim_halves, axis=0)
    for part in range(0, rim_slope.shape[2], 2 * LANES):
        moved = mm(rim_stack, table(f"scatter{part}"))
        for slot in range(MOST):
            rim_slope[slot, :, part : part + moved.shape[1]] = moved[slot * freq_y : (slot + 1) * freq_y]
    error_ref[0] = error * (1.0 / (GRID_Y * CORE_X))


    def backward_chunk(start, sums):
        images, edges = [], []
        for step in range(chunk):
            k = start + step
            weight = weight_ref[k]
            for slot in range(MOST):
                plus = scale_ref[slot, 0] * weight
                minus = scale_ref[slot, 1] * weight
                images.append(
                    unwaves(
                        plus * field[slot, k, 0],
                        plus * field[slot, k, 1],
                        minus * field[slot, k, 2],
                        minus * field[slot, k, 3],
                    )
                )
                column = k // RIM_KERNS * LANES
                edge = rim_slope[slot, :, column : column + LANES]
                if k % RIM_KERNS != 0:
                    edge = pltpu.roll(edge, LANES - k % RIM_KERNS * RIM_WIDTH, 1)
                edge = edge.astype(BF16)
                edges.append(jnp.concatenate([edge, edge], axis=1))
        pairs = [halves(cols) for cols in from_image(images)]
        top, rest = [jnp.concatenate(part, axis=0) for part in zip(*pairs)]
        waves_all = thrice(top, rest, "core_t") + mm(jnp.concatenate(edges, axis=0), table("rim_t"))
        for step in range(chunk):
            kern_re, kern_im = kern_at(start + step)
            for slot in range(MOST):
                at = (MOST * step + slot) * freq_y
                wave_re, wave_im = waves_all[at : at + freq_y, :LANES], waves_all[at : at + freq_y, LANES:]
                sums[slot][0] += wave_re * kern_re + wave_im * kern_im
                sums[slot][1] += wave_im * kern_re - wave_re * kern_im

    slopes = [[jnp.zeros((freq_y, LANES), F32)] * 2 for _ in range(MOST)]
    for start in range(0, kern_count, chunk):
        backward_chunk(start, slopes)

    tall = jnp.concatenate([jnp.concatenate(slopes[slot], axis=0) for slot in range(MOST)], axis=1)
    both = mm(table("picks_t"), jnp.concatenate(halves(tall), axis=0))
    wide = [
        jnp.concatenate([both[:ROWS_PAD, at : at + LANES], both[ROWS_PAD:, at : at + LANES]], axis=1)
        for at in range(0, MOST * LANES, LANES)
    ]
    top, rest = halves(jnp.concatenate(wide, axis=0))
    both = mm(
        jnp.concatenate([top, rest], axis=1), jnp.concatenate([table("lanes_t"), table("lanes_t")], axis=0)
    )
    packets = [packed(both[at : at + ROWS], used) for at in range(0, MOST * ROWS_PAD, ROWS_PAD)]
    for at in range(2):
        here = slice(at * split, (at + 1) * split)
        ready[at] = slot_pair(packets[0][here], packets[1][here], used)

    def give(pair_at, carry):
        slopes_ref[2 * pair_at] = ready[0]
        slopes_ref[2 * pair_at + 1] = ready[1]
        return carry

    lax.fori_loop(0, slopes_ref.shape[0] // 2, give, 0)
    for copy in later:
        copy.wait()


def imaging_table(kern_count, freq_y, freq_x):
    core, rim, rows = image_tables(freq_y, freq_x)
    lanes, picks = pick_tables(freq_y, freq_x)

    def tall(table):
        return np.concatenate(halves_np(table), axis=0)

    def three(table):
        top, rest = halves_np(table)
        return np.concatenate([top, top, rest], axis=1)

    def square_up(table):
        top, rest = halves_np(table)
        return np.block([[top, top], [rest, np.zeros_like(rest)]])

    rim_in, rim_out, scatter = rim_tables(rim, kern_count)
    tables = {
        "core": tall(core),
        "core_t": tall(core.T),
        "rim": rim_in,
        "rim_t": rim_out,
        "rows": three(rows),
        "rows_t": square_up(rows.T),
        "lanes": lanes.astype(BF16),
        "lanes_t": lanes.T.astype(BF16),
        "picks": picks.astype(BF16),
        "picks_t": np.concatenate([picks.T, picks.T], axis=1).astype(BF16),
        "turn": np.eye(GRID_Y)[
            np.concatenate([GRID_Y // 2 + half_order(), GRID_Y // 2 - 1 - half_order()])
        ].astype(BF16),
    }
    for part in range(0, scatter.shape[1], 2 * LANES):
        tables[f"scatter{part}"] = scatter[:, part : part + 2 * LANES]
    places, stacked, start = {}, [], 0
    for name, piece in tables.items():
        height, width = piece.shape
        places[name] = (start, height, width)
        stacked.append(np.pad(piece, ((0, 0), (0, 2 * LANES - width))))
        start += height
    return places, np.concatenate(stacked, axis=0)


def owner_imaging(owner_list, kern_weight, pieces, kernels, places, table, later):
    kern_count, freq_y, freq_x = kernels.shape[2:]
    tiles, split = owner_list.shape[0], freq_y // 2
    half = GRID_Y // 2
    smem = pl.BlockSpec(memory_space=pltpu.SMEM)
    vmem = pl.BlockSpec(memory_space=pltpu.VMEM)
    hbm = pl.BlockSpec(memory_space=pltpu.HBM)
    return pl.pallas_call(
        functools.partial(imaging_kernel, places, freq_x + 1, len(later)),
        in_specs=[smem, smem, vmem, vmem, vmem] + [hbm] * len(later),
        out_specs=(vmem, smem) + (vmem,) * len(later),
        out_shape=(
            jax.ShapeDtypeStruct((tiles, 2 * split - 8, LANES), F32),
            jax.ShapeDtypeStruct((1,), F32),
        )
        + tuple(jax.ShapeDtypeStruct(part.shape, part.dtype) for part in later),
        scratch_shapes=[
            pltpu.VMEM((MOST, 2 * freq_y, LANES), F32),
            pltpu.VMEM((MOST, kern_count, 4, half, LANES), F32),
            pltpu.VMEM((MOST, 4, half, LANES), F32),
            pltpu.VMEM((MOST, freq_y, -(-kern_count * 4 // QUARTER) * LANES), F32),
            pltpu.VMEM((MOST, freq_y, -(-kern_count * RIM_WIDTH // LANES) * LANES), F32),
            pltpu.VMEM((MOST, 2, half, LANES), F32),
            pltpu.VMEM((2, 2 * split - 8, LANES), F32),
            pltpu.VMEM((MOST, 2 * half, LANES), F32),
            pltpu.SemaphoreType.DMA((len(later),)),
        ],
        compiler_params=pltpu.CompilerParams(vmem_limit_bytes=20 * 2**20),
        name="owner_imaging",
    )(
        owner_list, kern_weight, in_vmem(pieces), in_vmem(kernels),
        in_vmem(table), *[in_hbm(part) for part in later],
    )


def on_device(mask_tiles, target_grid, kernels, kern_weight, owner_list):
    tile_px = mask_tiles.shape[1]
    freq_y, freq_x = kernels.shape[3:]
    count = lax.axis_size("tile")
    cols, turns, rows = mask_tables(tile_px, freq_y, freq_x)
    owner_list = owner_list.reshape(-1)
    mates = [(i, i + 1 - 2 * (i % 2)) for i in range(count)]

    pieces = mask_spectrum(mask_tiles, target_grid.reshape(GRID_Y, CORE_X), cols, turns, rows, freq_x)
    places, table = imaging_table(kernels.shape[2], freq_y, freq_x)
    pieces, table = lax.optimization_barrier((pieces, jnp.asarray(table)))
    if count == PIECES:
        pieces, edges = lax.all_to_all(pieces, "tile", 0, 0, tiled=True), None
    else:
        groups = [list(range(at, at + PIECES)) for at in range(0, count, PIECES)]
        pieces = lax.all_to_all(pieces, "tile", 0, 0, axis_index_groups=groups, tiled=True)
        later = [(i, i + PIECES) for i in range(count - PIECES)]
        sooner = [(i + PIECES, i) for i in range(count - PIECES)]
        edges = jnp.stack(
            [lax.ppermute(pieces[PIECES - 1], "tile", later), lax.ppermute(pieces[0], "tile", sooner)]
        )
    pieces = lax.all_to_all(route(owner_list, pieces, edges), "tile", 0, 0, tiled=True)
    slopes, owner_error, *held = owner_imaging(
        owner_list, kern_weight, pieces, kernels, places, table,
        (mask_tiles,) + update_tables(cols, turns, rows),
    )
    slopes = lax.all_to_all(slopes, "tile", 0, 0, tiled=True)
    other = lax.ppermute(tile_pick(owner_list, slopes, freq_x), "tile", mates)
    current = mask_update(owner_list, slopes, other, *held, freq_x)
    return (current, owner_error)


def solution(mesh):
    placed = (
        P(("stripe", "tile"), None, None),
        P(("stripe", "tile"), None),
        P("tile", None, None, None, None),
        P(),
        P("stripe", None),
    )
    return jax.shard_map(
        on_device,
        mesh=mesh,
        in_specs=placed,
        out_specs=(P(("stripe", "tile"), None, None), P(("stripe", "tile"))),
        check_vma=False,
    )
```

```python
import functools

import jax
import jax.numpy as jnp
import numpy as np
from jax import lax
from jax.experimental import pallas as pl
from jax.experimental.pallas import tpu as pltpu
from jax.sharding import PartitionSpec as P

AMBIT = 256
GRID_X = 192
GRID_Y = 128
CORE_X = 128
RESIST_SLOPE = 3.0
RESIST_LEVEL = 1.2
DIFFUSE_RATE = 0.2
STEP_SIZE = 1.0

LANES = 128
MOST = 2
BLOCKS = 4
PIECES = 16
CHUNK = 6
QUARTER = 32
RIM_WIDTH = 16
RIM_KERNS = LANES // RIM_WIDTH
ROWS = 72
ROWS_PAD = 80
F32 = jnp.float32
BF16 = jnp.bfloat16


def halves_np(table):
    table = np.asarray(table, np.float32)
    top = table.astype(BF16)
    rest = (table - top.astype(np.float32)).astype(BF16)
    return top, rest


def halves(value):
    top = value.astype(BF16)
    rest = (value - top.astype(F32)).astype(BF16)
    return top, rest


def mm(left, right):
    return jnp.dot(left, right, preferred_element_type=F32)


def in_hbm(value):
    return pltpu.with_memory_space_constraint(jnp.asarray(value), pltpu.HBM)


def in_vmem(value):
    return pltpu.with_memory_space_constraint(jnp.asarray(value), pltpu.VMEM)


def real_waves(places, period, most, width):
    angles = 2.0 * np.pi * np.outer(places, np.arange(most + 1)) / period
    waves = np.concatenate([np.cos(angles), np.sin(angles[:, 1:])], axis=1)
    return np.pad(waves, ((0, 0), (0, width - waves.shape[1])))


def signed_picks(count, width):
    freqs = np.arange(count) - count // 2
    most = count // 2
    even = np.zeros((count, width))
    odd = np.zeros((count, width))
    for at, freq in enumerate(freqs):
        even[at, abs(freq)] = 1.0
        if freq != 0:
            odd[at, most + abs(freq)] = np.sign(freq)
    return even, odd


def mask_tables(tile_px, freq_y, freq_x):
    win = tile_px + 2 * AMBIT
    mid_x = (GRID_X - 1) / 2 * (win // GRID_X)
    mid_y = (GRID_Y - 1) / 2 * (tile_px // GRID_Y)
    most = freq_x // 2
    cols = real_waves(np.arange(AMBIT), win, most, LANES)
    rows = real_waves(np.arange(tile_px) - mid_y, tile_px, freq_y // 2, ROWS_PAD)
    blocks = win // AMBIT
    angles = 2.0 * np.pi * np.outer(AMBIT * np.arange(blocks) - mid_x, np.arange(most + 1)) / win
    turns = np.zeros((2, blocks, LANES))
    turns[0, :, : most + 1] = np.cos(angles)
    turns[0, :, most + 1 : 2 * most + 1] = np.cos(angles[:, 1:])
    turns[1, :, : most + 1] = -np.sin(angles)
    turns[1, :, most + 1 : 2 * most + 1] = np.sin(angles[:, 1:])
    return cols, turns.astype(np.float32).reshape(2 * blocks, 1, LANES), rows


def swapped(value, used):
    lane = lax.broadcasted_iota(jnp.int32, value.shape, 1)
    most = (used - 1) // 2
    return jnp.where(lane <= most, pltpu.roll(value, LANES - most, 1), pltpu.roll(value, most, 1))


def packed(tall, used):
    rows = tall.shape[0] - 8
    body, line = tall[:rows], jnp.broadcast_to(tall[rows : rows + 1], (8, LANES))
    lane = lax.broadcasted_iota(jnp.int32, (8, LANES), 1)
    row = lax.broadcasted_iota(jnp.int32, (8, LANES), 0)
    spare = LANES - used
    first = jnp.where(lane < used, body[:8], 0.0)
    for at in range(-(-used // spare)):
        moved = pltpu.roll(line, (used - spare * at) % LANES, 1)
        first = jnp.where((row == at) & (lane >= used), moved, first)
    return jnp.concatenate([first, body[8:]], axis=0)


def unpacked(packet, used):
    lane = lax.broadcasted_iota(jnp.int32, packet.shape, 1)
    first = packet[:8]
    lane8 = lane[:8]
    row = lax.broadcasted_iota(jnp.int32, (8, LANES), 0)
    spare = LANES - used
    line = jnp.zeros((8, LANES), F32)
    for at in range(-(-used // spare)):
        moved = pltpu.roll(first, (spare * at - used) % LANES, 1)
        here = (row == at) & (lane8 >= spare * at) & (lane8 < min(spare * at + spare, used))
        line = line + jnp.where(here, moved, 0.0)
    line = jnp.where(row == 0, jnp.sum(line, axis=0, keepdims=True), 0.0)
    return jnp.concatenate([jnp.where(lane < used, packet, 0.0), line], axis=0)


def own_place():
    return lax.axis_index("tile").astype(jnp.int32)


def fetch(pairs, sems):
    copies = [pltpu.make_async_copy(src, dst, sems.at[at]) for at, (src, dst) in enumerate(pairs)]
    for copy in copies:
        copy.start()
    return copies


def spectrum_kernel(
    used, mask_hbm, cols_hbm, turns_hbm, rows_hbm, target_hbm, out_ref, mask, cols, turns, rows, sems, target_sems
):
    tile_px = mask.shape[0]
    width = AMBIT
    count = tile_px // width
    pairs = [(rows_hbm, rows)]
    for at in range(count):
        place = pl.ds(at * width, width)
        pairs.append((mask_hbm.at[0, :, place], mask.at[:, place]))
    pairs[2:2] = [(cols_hbm, cols), (turns_hbm, turns)]
    copies = fetch(pairs, sems)
    table_copies = [copies.pop(2), copies.pop(2)]
    size = target_hbm.shape[0] // PIECES
    goals = fetch(
        [(target_hbm.at[pl.ds(at * size, size)], out_ref.at[at, pl.ds(16, size)]) for at in range(PIECES)],
        target_sems,
    )

    def turned(both, block):
        return turns[block] * both[0] + turns[block + turns.shape[0] // 2] * both[1]

    copies[0].wait()
    terms = []
    for at in range(count):
        copies[1 + at].wait()
        top, rest = halves(mask[:, at * width : (at + 1) * width])
        both = mm(rows[...], top)
        top, rest = halves(both[:ROWS_PAD] + both[ROWS_PAD:] + mm(rows[:ROWS_PAD], rest))
        terms.append(jnp.concatenate([top, rest, top], axis=1))

    for copy in table_copies:
        copy.wait()
    table = jnp.concatenate([cols[:, :LANES], cols[:, :LANES], cols[:, LANES:]], axis=0)
    waves = []
    for some in (terms,):
        wave = mm(jnp.concatenate(some, axis=0), table)
        waves += [wave[at * ROWS_PAD : (at + 1) * ROWS_PAD] for at in range(len(some))]
    waves = [(wave, swapped(wave, used)) for wave in waves]
    own = sum(turned(wave, at + 1) for at, wave in enumerate(waves))
    low, high = turned(waves[0], count + 1), turned(waves[-1], 0)

    own, low, high = [packed(part[:ROWS], used) for part in (own, low, high)]
    groups = own.shape[0] // 8
    low = pltpu.roll(low.reshape(groups, 8, LANES), 4, 1)
    upper = lax.broadcasted_iota(jnp.int32, (8, LANES), 0) < 4
    for at in range(groups):
        mine, other = own[8 * at : 8 * at + 8], low[at]
        out_ref[2 * at, :8] = jnp.where(upper, mine, other)
        out_ref[2 * at + 1, :8] = jnp.where(upper, other, mine)
        out_ref[2 * at, 8:16] = high[8 * at : 8 * at + 8]
        out_ref[2 * at + 1, 8:16] = high[8 * at : 8 * at + 8]
    for copy in goals:
        copy.wait()


def mask_spectrum(mask_tiles, target, cols, turns, rows, freq_x):
    tile_px = mask_tiles.shape[1]
    col_stack = np.concatenate(halves_np(cols), axis=1)
    row_stack = np.concatenate(halves_np(rows.T), axis=0)
    hbm = pl.BlockSpec(memory_space=pltpu.HBM)
    return pl.pallas_call(
        functools.partial(spectrum_kernel, freq_x + 1),
        in_specs=[hbm] * 5,
        out_specs=pl.BlockSpec(memory_space=pltpu.VMEM),
        out_shape=jax.ShapeDtypeStruct((PIECES, 24, LANES), F32),
        scratch_shapes=[
            pltpu.VMEM((tile_px, tile_px), F32),
            pltpu.VMEM(col_stack.shape, BF16),
            pltpu.VMEM(turns.shape, F32),
            pltpu.VMEM(row_stack.shape, BF16),
            pltpu.SemaphoreType.DMA((3 + tile_px // AMBIT,)),
            pltpu.SemaphoreType.DMA((PIECES,)),
        ],
        compiler_params=pltpu.CompilerParams(vmem_limit_bytes=20 * 2**20),
        name="mask_spectrum",
    )(in_hbm(mask_tiles), in_hbm(col_stack), in_hbm(turns), in_hbm(row_stack), in_hbm(target))


def slot_pair(first, second, used):
    spare = LANES - used
    lane = lax.broadcasted_iota(jnp.int32, (8, LANES), 1)
    groups = [part[at : at + 8] for part in (first, second) for at in range(0, part.shape[0], 8)]
    last = groups.pop()
    for at, host in enumerate((1, 2, 3, 5)):
        groups[host] = jnp.where(lane < used, groups[host], pltpu.roll(last, (used - spare * at) % LANES, 1))
    return jnp.concatenate(groups, axis=0)


def slot_half(pair, slot, used):
    spare = LANES - used
    lane = lax.broadcasted_iota(jnp.int32, (8, LANES), 1)
    last = jnp.zeros((8, LANES), F32)
    for at, host in enumerate((1, 2, 3, 5)):
        moved = pltpu.roll(pair[8 * host : 8 * host + 8], (spare * at - used) % LANES, 1)
        last = jnp.where((lane >= spare * at) & (lane < min(spare * at + spare, used)), moved, last)
    return jnp.where(slot == 0, pair[:32], jnp.concatenate([pair[32:], last], axis=0))


def slots_of(owner_ref, tiles):
    owners = owner_ref[...].astype(F32)
    lane = lax.broadcasted_iota(jnp.int32, owners.shape, 1)
    found = []
    for tile in tiles:
        owner = jnp.sum(jnp.where(lane == tile, owners, 0.0), axis=1, keepdims=True)
        before = jnp.where((owners == owner) & (lane < tile), 1.0, 0.0)
        found.append((jnp.sum(owner).astype(jnp.int32), jnp.sum(before).astype(jnp.int32)))
    return found


def tiles_of(owner_ref, owner):
    owners = owner_ref[...].astype(F32)
    lane = lax.broadcasted_iota(jnp.int32, owners.shape, 1).astype(F32)
    mine = owners == owner.astype(F32)
    tiles = owners.shape[1]
    count = jnp.sum(jnp.where(mine, 1.0, 0.0))
    if tiles == PIECES:
        return count, jnp.int32(0), jnp.int32(0)
    first = jnp.min(jnp.where(mine, lane, tiles - 1.0)).astype(jnp.int32)
    last = jnp.max(jnp.where(mine, lane, 0.0)).astype(jnp.int32)
    return count, first, last


def mate_of(me):
    return me + 1 - 2 * lax.rem(me, 2)


def route_kernel(owner_ref, pieces_ref, *rest):
    edges_ref = rest[0] if len(rest) == 3 else None
    out_ref, seen = rest[-2:]
    tiles = owner_ref.shape[1]
    me = own_place()
    base = me // PIECES * PIECES if tiles > PIECES else 0
    row = lax.broadcasted_iota(jnp.int32, (8, LANES), 0)
    mine = row // 4 == lax.rem(me, 2)

    def send(tile, owner, slot):
        at = tile - base
        high = pieces_ref[jnp.maximum(at - 1, 0), 8:16]
        low = pieces_ref[jnp.minimum(at + 1, PIECES - 1), :8]
        if edges_ref is None:
            edge_high, edge_low = jnp.zeros_like(high), jnp.zeros_like(low)
        else:
            edge_high, edge_low = edges_ref[0, 8:16], edges_ref[1, :8]
        high = jnp.where(at > 0, high, edge_high)
        low = jnp.where(at < PIECES - 1, low, edge_low)
        packet = pieces_ref[at, :8] + high + pltpu.roll(low, 4, 0)
        beside = jnp.where(mine, out_ref[owner, :8], pltpu.roll(packet, 4, 0))
        out_ref[owner, :8] = jnp.where(slot == 0, packet, beside)
        out_ref[owner, pl.ds(pl.multiple_of(8 + 8 * slot, 8), 8)] = pieces_ref[at, 16:]

    if tiles == PIECES:
        for tile, (owner, slot) in enumerate(slots_of(owner_ref, list(range(tiles)))):
            send(jnp.int32(tile), owner, slot)
        return

    def clear(at, carry):
        seen[at] = 0
        return carry

    def count(tile, carry):
        owner = owner_ref[0, tile]
        slot = seen[owner]
        seen[owner] = slot + 1
        pl.when((tile >= base) & (tile < base + PIECES))(lambda: send(tile, owner, slot))
        return carry

    lax.fori_loop(0, tiles, clear, 0)
    lax.fori_loop(0, tiles, count, 0)


def route(owner_list, pieces, edges):
    smem = pl.BlockSpec(memory_space=pltpu.SMEM)
    vmem = pl.BlockSpec(memory_space=pltpu.VMEM)
    tiles = owner_list.shape[0]
    extra = [] if edges is None else [edges]
    return pl.pallas_call(
        route_kernel,
        in_specs=[vmem if tiles == PIECES else smem, vmem] + [vmem] * len(extra),
        out_specs=vmem,
        out_shape=jax.ShapeDtypeStruct((tiles, 24, LANES), F32),
        scratch_shapes=[pltpu.SMEM((tiles,), jnp.int32)],
        compiler_params=pltpu.CompilerParams(vmem_limit_bytes=2**20),
        name="route",
    )(owner_list.reshape(1, -1), in_vmem(pieces), *extra)


def around(tile, tiles):
    return [
        (tile, None),
        (jnp.maximum(tile - 1, 0), tile > 0),
        (jnp.minimum(tile + 1, tiles - 1), tile < tiles - 1),
    ]


def tile_pick_kernel(used, owner_ref, slopes_ref, out_ref):
    tiles = [tile for tile, _ in around(mate_of(own_place()), owner_ref.shape[1])]
    for at, (owner, slot) in enumerate(slots_of(owner_ref, tiles)):
        out_ref[at] = slot_half(slopes_ref[owner], slot, used)


def tile_pick(owner_list, slopes, freq_x):
    smem = pl.BlockSpec(memory_space=pltpu.SMEM)
    vmem = pl.BlockSpec(memory_space=pltpu.VMEM)
    return pl.pallas_call(
        functools.partial(tile_pick_kernel, freq_x + 1),
        in_specs=[vmem, vmem],
        out_specs=vmem,
        out_shape=jax.ShapeDtypeStruct((3, 32, LANES), F32),
        compiler_params=pltpu.CompilerParams(vmem_limit_bytes=2**20),
        name="tile_pick",
    )(owner_list.reshape(1, -1), in_vmem(slopes))


def joined(me, mine, other):
    odd = lax.rem(me, 2) == 1
    return jnp.concatenate([jnp.where(odd, other, mine), jnp.where(odd, mine, other)], axis=0)


def update_kernel(
    used, owner_ref, slopes_ref, other_ref, mask_ref, cols, turns, rows, out_hbm, out, held, out_sems
):
    tile_px = out.shape[0]
    block = tile_px // BLOCKS
    me = own_place()
    near = around(me, owner_ref.shape[1])
    packets = []
    for at, (owner, slot) in enumerate(slots_of(owner_ref, [tile for tile, _ in near])):
        packet = unpacked(joined(me, slot_half(slopes_ref[owner], slot, used), other_ref[at]), used)
        there = near[at][1]
        packets.append(packet if there is None else jnp.where(there, packet, 0.0))

    own, last, following = [(packet, swapped(packet, used)) for packet in packets]

    def turned_back(both, block):
        return turns[block] * both[0] - turns[block + turns.shape[0] // 2] * both[1]

    count = tile_px // AMBIT
    waves = [turned_back(own, at + 1) for at in range(count)]
    waves[0] = waves[0] + turned_back(last, count + 1)
    waves[-1] = waves[-1] + turned_back(following, 0)
    blank = jnp.zeros((ROWS_PAD - ROWS, LANES), F32)
    top, rest = halves(jnp.concatenate([part for wave in waves for part in (wave, blank)], axis=0))
    wide = mm(
        jnp.concatenate([top, rest, top], axis=1),
        jnp.concatenate([cols[:LANES], cols[:LANES], cols[LANES:]], axis=0),
    )
    for at in range(count):
        top, rest = halves(wide[at * ROWS_PAD : (at + 1) * ROWS_PAD])
        held[:, at * AMBIT : (at + 1) * AMBIT] = jnp.concatenate([top, rest, top], axis=0)
    sent = []
    for at in range(BLOCKS):
        here = slice(at * block, (at + 1) * block)
        place = pl.ds(at * block, block)
        out[here] = mask_ref[0, here] - STEP_SIZE * mm(rows[here], held[...])
        copy = pltpu.make_async_copy(out.at[place], out_hbm.at[0, place], out_sems.at[at])
        copy.start()
        sent.append(copy)
    for copy in sent:
        copy.wait()


def update_tables(cols, turns, rows):
    top, rest = halves_np(rows)
    return (
        np.concatenate(halves_np(cols.T), axis=0),
        turns,
        np.concatenate([top, top, rest], axis=1),
    )


def mask_update(owner_list, slopes, other, mask_tiles, cols, turns, rows, freq_x):
    tile_px = mask_tiles.shape[1]
    smem = pl.BlockSpec(memory_space=pltpu.SMEM)
    vmem = pl.BlockSpec(memory_space=pltpu.VMEM)
    hbm = pl.BlockSpec(memory_space=pltpu.HBM)
    return pl.pallas_call(
        functools.partial(update_kernel, freq_x + 1),
        in_specs=[vmem] * 7,
        out_specs=hbm,
        out_shape=jax.ShapeDtypeStruct(mask_tiles.shape, F32),
        scratch_shapes=[
            pltpu.VMEM((tile_px, tile_px), F32),
            pltpu.VMEM((3 * ROWS_PAD, tile_px), BF16),
            pltpu.SemaphoreType.DMA((BLOCKS,)),
        ],
        compiler_params=pltpu.CompilerParams(vmem_limit_bytes=16 * 2**20),
        name="mask_update",
    )(
        owner_list.reshape(1, -1), in_vmem(slopes), other, in_vmem(mask_tiles),
        in_vmem(cols), in_vmem(turns), in_vmem(rows),
    )


def half_order():
    return np.arange(GRID_Y // 2).reshape(8, -1).T.reshape(-1)


def image_tables(freq_y, freq_x):
    places_v = np.arange(GRID_X) - (GRID_X - 1) / 2
    freqs_b = np.arange(freq_x) - (freq_x - 1) / 2
    beta = 2.0 * np.pi * np.outer(freqs_b, places_v) / GRID_X
    first = (GRID_X - CORE_X) // 2

    def block(lane_of):
        table = np.zeros((2 * LANES, 2 * LANES))
        for place, lane in lane_of:
            table[:freq_x, lane] = np.cos(beta[:, place])
            table[:freq_x, LANES + lane] = np.sin(beta[:, place])
            table[LANES : LANES + freq_x, lane] = -np.sin(beta[:, place])
            table[LANES : LANES + freq_x, LANES + lane] = np.cos(beta[:, place])
        return table

    core = block([(first + lane, lane) for lane in range(CORE_X)])
    last = first + CORE_X
    rim = block(
        [(first - 2, LANES - 2), (first - 1, LANES - 1), (last, 0), (last + 1, 1)]
    )
    places_u = half_order() + 0.5
    freqs_a = np.arange(freq_y) - (freq_y - 1) / 2
    alpha = 2.0 * np.pi * np.outer(places_u, freqs_a) / GRID_Y
    rows = np.concatenate([np.cos(alpha), np.sin(alpha)], axis=0)
    return core, rim, rows


def rim_tables(rim, kern_count):
    seats = [(LANES - 2 + at) % LANES for at in range(4)]
    top, rest = halves_np(rim)
    rim_in = np.zeros((4 * LANES, LANES), BF16)
    for seat in seats:
        for quarter, source in enumerate((seat, LANES + seat)):
            place = (seat + quarter * QUARTER) % LANES
            rim_in[: 2 * LANES, place] = top[:, source]
            rim_in[2 * LANES :, place] = top[:, source]
            rim_in[: 2 * LANES, (place + 2 * QUARTER) % LANES] = rest[:, source]
    seats = seats + [LANES + seat for seat in seats]
    top, rest = halves_np(rim.T[seats])
    blank = np.zeros((LANES - 8, 2 * LANES), BF16)
    rim_out = np.concatenate([top, top, blank[8:], rest, blank], axis=0)
    width = -(-kern_count * RIM_WIDTH // LANES) * LANES
    scatter = np.zeros((4 * LANES, width))
    for kern in range(kern_count):
        for at in range(8):
            lane = (4 * kern - 2 + at % 4) % LANES + at // 4 * LANES
            scatter[lane, kern * RIM_WIDTH + at] = 1.0
            scatter[2 * LANES + lane, kern * RIM_WIDTH + 8 + at] = 1.0
    return rim_in, rim_out, scatter.astype(BF16)


def pick_tables(freq_y, freq_x):
    col_even, col_odd = signed_picks(freq_x, LANES)
    row_even, row_odd = signed_picks(freq_y, ROWS_PAD)
    lanes = np.zeros((LANES, 2 * LANES))
    lanes[:, :freq_x] = col_even.T
    lanes[:, LANES : LANES + freq_x] = col_odd.T
    rows = np.block([[row_even, -row_odd], [-row_odd, -row_even]])
    return lanes, rows


def imaging_kernel(places, used, extra, *refs):
    owner_ref, weight_ref, pieces_ref, kern_ref, table_ref = refs[:5]
    later_hbm, refs = refs[5 : 5 + extra], refs[5 + extra :]
    slopes_ref, error_ref, later_ref, refs = refs[0], refs[1], refs[2 : 2 + extra], refs[2 + extra :]
    spec, field, rim_field, rim_lanes, rim_slope, scale_ref, ready, goal_ref, sems = refs
    kern_count, freq_y, freq_x = kern_ref.shape[2:]
    later = fetch(list(zip(later_hbm, later_ref)), sems)
    chunk = max(size for size in range(1, CHUNK + 1) if kern_count % size == 0)
    count, first, second = tiles_of(owner_ref, own_place())
    slots = (first, second)
    split = freq_y // 2
    firsts = [slot // PIECES * PIECES for slot in slots]

    def table(name):
        start, height, width = places[name]
        return table_ref[start : start + height, :width]

    upper = lax.broadcasted_iota(jnp.int32, (8, LANES), 0) < 4
    blank = jnp.zeros((ROWS_PAD - ROWS, LANES), F32)
    targets, packets = [], []
    for slot in range(MOST):
        target = jnp.concatenate(
            [pieces_ref[firsts[slot] + at, 8 + 8 * slot : 16 + 8 * slot] for at in range(PIECES)], axis=0
        )
        targets.append(jnp.where(count > slot, target, 0.0))
        pieces = []
        for at in range(0, PIECES, 2):
            even, odd = pieces_ref[firsts[slot] + at, :8], pieces_ref[firsts[slot] + at + 1, :8]
            if slot == 0:
                pieces.append(jnp.where(upper, even, odd))
            else:
                pieces.append(pltpu.roll(jnp.where(upper, odd, even), 4, 0))
        packet = jnp.concatenate(pieces, axis=0)
        packets += [jnp.where(count > slot, unpacked(packet, used), 0.0), blank]

    top, rest = halves(jnp.concatenate(packets, axis=0))
    both = mm(
        jnp.concatenate([top, rest], axis=1), jnp.concatenate([table("lanes"), table("lanes")], axis=0)
    )
    tall = [
        jnp.concatenate([both[at : at + ROWS_PAD, :LANES], both[at : at + ROWS_PAD, LANES:]], axis=0)
        for at in range(0, MOST * ROWS_PAD, ROWS_PAD)
    ]
    top, rest = halves(jnp.concatenate(tall, axis=1))
    both = mm(table("picks"), top) + mm(table("picks"), rest)
    for slot in range(MOST):
        spec[slot] = both[:, slot * LANES : (slot + 1) * LANES]

    target = jnp.concatenate(targets, axis=1)
    one = target.astype(BF16)
    target = target - one.astype(F32)
    two = target.astype(BF16)
    three = (target - two.astype(F32)).astype(BF16)
    both = mm(table("turn"), one) + mm(table("turn"), two) + mm(table("turn"), three)
    for slot in range(MOST):
        goal_ref[slot] = both[:, slot * LANES : (slot + 1) * LANES]

    half = GRID_Y // 2
    lane = lax.broadcasted_iota(jnp.int32, (freq_y, LANES), 1)
    live_lane = lane < freq_x

    def kern_at(k):
        def one(part):
            raw = kern_ref[0, part, k]
            wide = jnp.concatenate([raw, jnp.zeros((freq_y, LANES - freq_x), F32)], axis=1)
            return wide
        return one(0), one(1)

    def side_by_side(pieces):
        return pieces[0] if len(pieces) == 1 else jnp.concatenate(pieces, axis=1)

    def apart(wide):
        size = 2 * LANES
        return [wide[:, at : at + size] for at in range(0, wide.shape[1], size)]

    def to_image(stacks):
        pieces = []
        for stack in stacks:
            top, rest = halves(stack)
            pieces.append(jnp.concatenate([top, rest, top], axis=0))
        return apart(mm(table("rows"), side_by_side(pieces)))

    def from_image(stacks):
        pieces = [jnp.concatenate(halves(stack), axis=0) for stack in stacks]
        both = mm(table("rows_t"), side_by_side(pieces))
        return apart(both[:freq_y] + both[freq_y:])

    def thrice(top, rest, name):
        both = table(name)
        height = both.shape[0] // 2
        return mm(
            jnp.concatenate([top, rest, top], axis=1),
            jnp.concatenate([both[:height], both[:height], both[height:]], axis=0),
        )

    def waves(stack):
        even_re, even_im = stack[:half, :LANES], stack[:half, LANES:]
        odd_re, odd_im = stack[half:, :LANES], stack[half:, LANES:]
        return even_re - odd_im, even_im + odd_re, even_re + odd_im, even_im - odd_re

    def unwaves(plus_re, plus_im, minus_re, minus_im):
        above = jnp.concatenate([plus_re + minus_re, plus_im + minus_im], axis=1)
        below = jnp.concatenate([plus_im - minus_im, minus_re - plus_re], axis=1)
        return jnp.concatenate([above, below], axis=0)


    def forward_chunk(start, new):
        tops, rests = [], []
        for step in range(chunk):
            kern_re, kern_im = kern_at(start + step)
            for slot in range(MOST):
                spec_re, spec_im = spec[slot, :freq_y], spec[slot, freq_y:]
                wave = jnp.concatenate(
                    [kern_re * spec_re - kern_im * spec_im, kern_re * spec_im + kern_im * spec_re], axis=1
                )
                top, rest = halves(wave)
                tops.append(top)
                rests.append(rest)
        top, rest = jnp.concatenate(tops, axis=0), jnp.concatenate(rests, axis=0)
        cols = thrice(top, rest, "core")
        edges = mm(jnp.concatenate([top, rest], axis=1), table("rim"))
        places = [(step, slot) for step in range(chunk) for slot in range(MOST)]
        images = to_image([cols[at * freq_y : (at + 1) * freq_y] for at in range(len(places))])
        for at, (step, slot) in enumerate(places):
            k = start + step
            weight = weight_ref[:, k : k + 1]
            new[2] = jnp.where(group_of == k, jnp.broadcast_to(weight, (8, LANES)), new[2])
            edge = edges[at * freq_y : (at + 1) * freq_y]
            column, place = divmod(k, QUARTER // 4)
            here = slice(column * LANES, (column + 1) * LANES)
            if place == 0:
                rim_lanes[slot, :, here] = edge
            else:
                rim_lanes[slot, :, here] += pltpu.roll(edge, 4 * place, 1)
            parts = waves(images[at])
            for part in range(4):
                field[slot, k, part] = parts[part]
            plus, minus = new[slot]
            plus = plus + weight * (parts[0] * parts[0] + parts[1] * parts[1])
            minus = minus + weight * (parts[2] * parts[2] + parts[3] * parts[3])
            new[slot] = (plus, minus)

    blank = jnp.zeros((half, LANES), F32)
    group_of = lax.rem(lax.broadcasted_iota(jnp.int32, (8, LANES), 1) + 2, LANES) // 4
    sums = [(blank, blank), (blank, blank), jnp.zeros((8, LANES), F32)]
    for start in range(0, kern_count, chunk):
        forward_chunk(start, sums)
    lane_weight = sums.pop()

    norm = 1.0 / (64.0 * GRID_Y * GRID_X)
    square = norm * norm
    lane_half = lax.broadcasted_iota(jnp.int32, (half, LANES), 1)
    near = (lane_half < 2) | (lane_half >= LANES - 2)
    row_8 = lax.broadcasted_iota(jnp.int32, (8, LANES), 0)

    def rows_beside(value, other):
        first, last = value[:8], value[half - 8 :]
        later = jnp.where(row_8 == 7, last, pltpu.roll(first, 7, 0))
        sooner = jnp.where(row_8 == 0, other[:8], pltpu.roll(last, 1, 0))
        return jnp.concatenate([value[8:], later], axis=0) + jnp.concatenate([sooner, value[:-8]], axis=0)

    at_first, at_last = lane_half == 0, lane_half == LANES - 1

    def spread_out(value, rows, left, right):
        return value + DIFFUSE_RATE * (rows + left + right - 4.0 * value)

    def sides(value):
        return pltpu.roll(value, 1, 1), pltpu.roll(value, LANES - 1, 1)

    def beside(core, rim):
        return jnp.where(at_first, rim[0], core[0]), jnp.where(at_last, rim[1], core[1])

    def blur(core, rim):
        core_sides = [sides(value) for value in core]
        rim_sides = [sides(value) for value in rim]
        rim_one = [
            spread_out(rim[at], rows_beside(rim[at], rim[1 - at]), *beside(rim_sides[at], core_sides[at]))
            for at in range(2)
        ]
        core_one = [
            spread_out(core[at], rows_beside(core[at], core[1 - at]), *beside(core_sides[at], rim_sides[at]))
            for at in range(2)
        ]
        return [
            spread_out(
                core_one[at],
                rows_beside(core_one[at], core_one[1 - at]),
                *beside(sides(core_one[at]), sides(rim_one[at])),
            )
            for at in range(2)
        ]

    def blur_back(core):
        core_sides = [sides(value) for value in core]
        none = jnp.zeros((half, LANES), F32)
        rim_one = [DIFFUSE_RATE * sum(beside((none, none), core_sides[at])) for at in range(2)]
        core_one = [
            spread_out(core[at], rows_beside(core[at], core[1 - at]), *beside(core_sides[at], (none, none)))
            for at in range(2)
        ]
        core_sides = [sides(value) for value in core_one]
        rim_sides = [sides(value) for value in rim_one]
        rim_two = [
            spread_out(rim_one[at], rows_beside(rim_one[at], rim_one[1 - at]), *beside(rim_sides[at], core_sides[at]))
            for at in range(2)
        ]
        core_two = [
            spread_out(core_one[at], rows_beside(core_one[at], core_one[1 - at]), *beside(core_sides[at], rim_sides[at]))
            for at in range(2)
        ]
        return core_two, rim_two

    def fold(value):
        def back(amount):
            return pltpu.roll(value, LANES - amount, 1)
        value = value + back(48)
        value = value + back(24)
        value = value + back(12)
        return value + back(4) + back(8)

    def unfold(value):
        value = jnp.where(near, value, 0.0)
        value = value + pltpu.roll(value, 4, 1) + pltpu.roll(value, 8, 1)
        value = value + pltpu.roll(value, 12, 1)
        value = value + pltpu.roll(value, 24, 1)
        return value + pltpu.roll(value, 48, 1)

    def rim_columns(slot):
        quarter = lax.rem(lane + 2, LANES) // QUARTER
        real = imag = jnp.zeros((freq_y, LANES), F32)
        for column in range(rim_lanes.shape[2] // LANES):
            both = rim_lanes[slot, :, column * LANES : (column + 1) * LANES]
            both = both + pltpu.roll(both, 2 * QUARTER, 1)
            for_real = both if column == 0 else pltpu.roll(both, column * QUARTER, 1)
            for_imag = both if column == 1 else pltpu.roll(both, (column - 1) * QUARTER % LANES, 1)
            real = jnp.where(quarter == column, for_real, real)
            imag = jnp.where(quarter == column, for_imag, imag)
        return jnp.concatenate([real, imag], axis=1)

    error = jnp.float32(0.0)
    rim_halves = []
    for slot in range(2):
        live = (count > slot).astype(F32)
        rim_parts = waves(to_image([rim_columns(slot)])[0])
        for part in range(4):
            rim_field[slot, part] = rim_parts[part]
        weights = jnp.concatenate([lane_weight] * (half // 8), axis=0)
        rim_plus = weights * (rim_parts[0] * rim_parts[0] + rim_parts[1] * rim_parts[1])
        rim_minus = weights * (rim_parts[2] * rim_parts[2] + rim_parts[3] * rim_parts[3])
        core = [part * square for part in sums[slot]]
        rim = [jnp.where(near, fold(part), 0.0) * square for part in (rim_plus, rim_minus)]
        core = blur(core, rim)

        def slope_of(value, goal):
            resist = 1.0 / (1.0 + jnp.exp(-RESIST_SLOPE * (value - RESIST_LEVEL)))
            misfit = resist - goal
            return (2.0 * RESIST_SLOPE) * misfit * resist * (1.0 - resist), jnp.sum(misfit * misfit)

        slope_plus, err_plus = slope_of(core[0], goal_ref[slot, :half])
        slope_minus, err_minus = slope_of(core[1], goal_ref[slot, half:])
        error = error + live * (err_plus + err_minus)
        core, rim = blur_back([slope_plus, slope_minus])
        factor = 2.0 * square
        for at in range(2):
            scale_ref[slot, at] = core[at] * factor
        rim_f_plus = unfold(rim[0] * factor) * weights
        rim_f_minus = unfold(rim[1] * factor) * weights
        edge = from_image(
            [
                unwaves(
                    rim_f_plus * rim_field[slot, 0],
                    rim_f_plus * rim_field[slot, 1],
                    rim_f_minus * rim_field[slot, 2],
                    rim_f_minus * rim_field[slot, 3],
                )
            ]
        )[0]
        rim_halves.append(jnp.concatenate(halves(edge), axis=1))
    rim_stack = jnp.concatenate(rim_halves, axis=0)
    for part in range(0, rim_slope.shape[2], 2 * LANES):
        moved = mm(rim_stack, table(f"scatter{part}"))
        for slot in range(MOST):
            rim_slope[slot, :, part : part + moved.shape[1]] = moved[slot * freq_y : (slot + 1) * freq_y]
    error_ref[0] = error * (1.0 / (GRID_Y * CORE_X))


    def backward_chunk(start, sums):
        images, edges = [], []
        for step in range(chunk):
            k = start + step
            weight = weight_ref[:, k : k + 1]
            for slot in range(MOST):
                plus = scale_ref[slot, 0] * weight
                minus = scale_ref[slot, 1] * weight
                images.append(
                    unwaves(
                        plus * field[slot, k, 0],
                        plus * field[slot, k, 1],
                        minus * field[slot, k, 2],
                        minus * field[slot, k, 3],
                    )
                )
                column = k // RIM_KERNS * LANES
                edge = rim_slope[slot, :, column : column + LANES]
                if k % RIM_KERNS != 0:
                    edge = pltpu.roll(edge, LANES - k % RIM_KERNS * RIM_WIDTH, 1)
                edge = edge.astype(BF16)
                edges.append(jnp.concatenate([edge, edge], axis=1))
        pairs = [halves(cols) for cols in from_image(images)]
        top, rest = [jnp.concatenate(part, axis=0) for part in zip(*pairs)]
        waves_all = thrice(top, rest, "core_t") + mm(jnp.concatenate(edges, axis=0), table("rim_t"))
        for step in range(chunk):
            kern_re, kern_im = kern_at(start + step)
            for slot in range(MOST):
                at = (MOST * step + slot) * freq_y
                wave_re, wave_im = waves_all[at : at + freq_y, :LANES], waves_all[at : at + freq_y, LANES:]
                sums[slot][0] += wave_re * kern_re + wave_im * kern_im
                sums[slot][1] += wave_im * kern_re - wave_re * kern_im

    slopes = [[jnp.zeros((freq_y, LANES), F32)] * 2 for _ in range(MOST)]
    for start in range(0, kern_count, chunk):
        backward_chunk(start, slopes)

    tall = jnp.concatenate([jnp.concatenate(slopes[slot], axis=0) for slot in range(MOST)], axis=1)
    both = mm(table("picks_t"), jnp.concatenate(halves(tall), axis=0))
    wide = [
        jnp.concatenate([both[:ROWS_PAD, at : at + LANES], both[ROWS_PAD:, at : at + LANES]], axis=1)
        for at in range(0, MOST * LANES, LANES)
    ]
    top, rest = halves(jnp.concatenate(wide, axis=0))
    both = mm(
        jnp.concatenate([top, rest], axis=1), jnp.concatenate([table("lanes_t"), table("lanes_t")], axis=0)
    )
    packets = [packed(both[at : at + ROWS], used) for at in range(0, MOST * ROWS_PAD, ROWS_PAD)]
    for at in range(2):
        here = slice(at * split, (at + 1) * split)
        ready[at] = slot_pair(packets[0][here], packets[1][here], used)

    def give(pair_at, carry):
        slopes_ref[2 * pair_at] = ready[0]
        slopes_ref[2 * pair_at + 1] = ready[1]
        return carry

    lax.fori_loop(0, slopes_ref.shape[0] // 2, give, 0)
    for copy in later:
        copy.wait()


def imaging_table(kern_count, freq_y, freq_x):
    core, rim, rows = image_tables(freq_y, freq_x)
    lanes, picks = pick_tables(freq_y, freq_x)

    def tall(table):
        return np.concatenate(halves_np(table), axis=0)

    def three(table):
        top, rest = halves_np(table)
        return np.concatenate([top, top, rest], axis=1)

    def square_up(table):
        top, rest = halves_np(table)
        return np.block([[top, top], [rest, np.zeros_like(rest)]])

    rim_in, rim_out, scatter = rim_tables(rim, kern_count)
    tables = {
        "core": tall(core),
        "core_t": tall(core.T),
        "rim": rim_in,
        "rim_t": rim_out,
        "rows": three(rows),
        "rows_t": square_up(rows.T),
        "lanes": lanes.astype(BF16),
        "lanes_t": lanes.T.astype(BF16),
        "picks": picks.astype(BF16),
        "picks_t": np.concatenate([picks.T, picks.T], axis=1).astype(BF16),
        "turn": np.eye(GRID_Y)[
            np.concatenate([GRID_Y // 2 + half_order(), GRID_Y // 2 - 1 - half_order()])
        ].astype(BF16),
    }
    for part in range(0, scatter.shape[1], 2 * LANES):
        tables[f"scatter{part}"] = scatter[:, part : part + 2 * LANES]
    places, stacked, start = {}, [], 0
    for name, piece in tables.items():
        height, width = piece.shape
        places[name] = (start, height, width)
        stacked.append(np.pad(piece, ((0, 0), (0, 2 * LANES - width))))
        start += height
    return places, np.concatenate(stacked, axis=0)


def owner_imaging(owner_list, kern_weight, pieces, kernels, places, table, later):
    kern_count, freq_y, freq_x = kernels.shape[2:]
    tiles, split = owner_list.shape[0], freq_y // 2
    half = GRID_Y // 2
    smem = pl.BlockSpec(memory_space=pltpu.SMEM)
    vmem = pl.BlockSpec(memory_space=pltpu.VMEM)
    hbm = pl.BlockSpec(memory_space=pltpu.HBM)
    return pl.pallas_call(
        functools.partial(imaging_kernel, places, freq_x + 1, len(later)),
        in_specs=[vmem] * 5 + [hbm] * len(later),
        out_specs=(vmem, smem) + (vmem,) * len(later),
        out_shape=(
            jax.ShapeDtypeStruct((tiles, 2 * split - 8, LANES), F32),
            jax.ShapeDtypeStruct((1,), F32),
        )
        + tuple(jax.ShapeDtypeStruct(part.shape, part.dtype) for part in later),
        scratch_shapes=[
            pltpu.VMEM((MOST, 2 * freq_y, LANES), F32),
            pltpu.VMEM((MOST, kern_count, 4, half, LANES), F32),
            pltpu.VMEM((MOST, 4, half, LANES), F32),
            pltpu.VMEM((MOST, freq_y, -(-kern_count * 4 // QUARTER) * LANES), F32),
            pltpu.VMEM((MOST, freq_y, -(-kern_count * RIM_WIDTH // LANES) * LANES), F32),
            pltpu.VMEM((MOST, 2, half, LANES), F32),
            pltpu.VMEM((2, 2 * split - 8, LANES), F32),
            pltpu.VMEM((MOST, 2 * half, LANES), F32),
            pltpu.SemaphoreType.DMA((len(later),)),
        ],
        compiler_params=pltpu.CompilerParams(vmem_limit_bytes=20 * 2**20),
        name="owner_imaging",
    )(
        owner_list.reshape(1, -1), kern_weight.reshape(1, -1), in_vmem(pieces), in_vmem(kernels),
        in_vmem(table), *[in_hbm(part) for part in later],
    )


def on_device(mask_tiles, target_grid, kernels, kern_weight, owner_list):
    tile_px = mask_tiles.shape[1]
    freq_y, freq_x = kernels.shape[3:]
    count = lax.axis_size("tile")
    cols, turns, rows = mask_tables(tile_px, freq_y, freq_x)
    owner_list = owner_list.reshape(-1)
    mates = [(i, i + 1 - 2 * (i % 2)) for i in range(count)]

    pieces = mask_spectrum(mask_tiles, target_grid.reshape(GRID_Y, CORE_X), cols, turns, rows, freq_x)
    places, table = imaging_table(kernels.shape[2], freq_y, freq_x)
    pieces, table = lax.optimization_barrier((pieces, jnp.asarray(table)))
    if count == PIECES:
        pieces, edges = lax.all_to_all(pieces, "tile", 0, 0, tiled=True), None
    else:
        groups = [list(range(at, at + PIECES)) for at in range(0, count, PIECES)]
        pieces = lax.all_to_all(pieces, "tile", 0, 0, axis_index_groups=groups, tiled=True)
        later = [(i, i + PIECES) for i in range(count - PIECES)]
        sooner = [(i + PIECES, i) for i in range(count - PIECES)]
        edges = jnp.stack(
            [lax.ppermute(pieces[PIECES - 1], "tile", later), lax.ppermute(pieces[0], "tile", sooner)]
        )
    pieces = lax.all_to_all(route(owner_list, pieces, edges), "tile", 0, 0, tiled=True)
    slopes, owner_error, *held = owner_imaging(
        owner_list, kern_weight, pieces, kernels, places, table,
        (mask_tiles,) + update_tables(cols, turns, rows),
    )
    slopes = lax.all_to_all(slopes, "tile", 0, 0, tiled=True)
    other = lax.ppermute(tile_pick(owner_list, slopes, freq_x), "tile", mates)
    current = mask_update(owner_list, slopes, other, *held, freq_x)
    return (current, owner_error)


def solution(mesh):
    placed = (
        P(("stripe", "tile"), None, None),
        P(("stripe", "tile"), None),
        P("tile", None, None, None, None),
        P(),
        P("stripe", None),
    )
    return jax.shard_map(
        on_device,
        mesh=mesh,
        in_specs=placed,
        out_specs=(P(("stripe", "tile"), None, None), P(("stripe", "tile"))),
        check_vma=False,
    )
```

```python
import functools

import jax
import jax.numpy as jnp
import numpy as np
from jax import lax
from jax.experimental import pallas as pl
from jax.experimental.pallas import tpu as pltpu
from jax.sharding import PartitionSpec as P

AMBIT = 256
GRID_X = 192
GRID_Y = 128
CORE_X = 128
RESIST_SLOPE = 3.0
RESIST_LEVEL = 1.2
DIFFUSE_RATE = 0.2
STEP_SIZE = 1.0

LANES = 128
MOST = 2
BLOCKS = 4
PIECES = 16
CHUNK = 6
QUARTER = 32
RIM_WIDTH = 16
RIM_KERNS = LANES // RIM_WIDTH
ROWS = 72
ROWS_PAD = 80
F32 = jnp.float32
BF16 = jnp.bfloat16


def halves_np(table):
    table = np.asarray(table, np.float32)
    top = table.astype(BF16)
    rest = (table - top.astype(np.float32)).astype(BF16)
    return top, rest


def halves(value):
    top = value.astype(BF16)
    rest = (value - top.astype(F32)).astype(BF16)
    return top, rest


def mm(left, right):
    return jnp.dot(left, right, preferred_element_type=F32)


def in_hbm(value):
    return pltpu.with_memory_space_constraint(jnp.asarray(value), pltpu.HBM)


def in_vmem(value):
    return pltpu.with_memory_space_constraint(jnp.asarray(value), pltpu.VMEM)


def real_waves(places, period, most, width):
    angles = 2.0 * np.pi * np.outer(places, np.arange(most + 1)) / period
    waves = np.concatenate([np.cos(angles), np.sin(angles[:, 1:])], axis=1)
    return np.pad(waves, ((0, 0), (0, width - waves.shape[1])))


def signed_picks(count, width):
    freqs = np.arange(count) - count // 2
    most = count // 2
    even = np.zeros((count, width))
    odd = np.zeros((count, width))
    for at, freq in enumerate(freqs):
        even[at, abs(freq)] = 1.0
        if freq != 0:
            odd[at, most + abs(freq)] = np.sign(freq)
    return even, odd


def mask_tables(tile_px, freq_y, freq_x):
    win = tile_px + 2 * AMBIT
    mid_x = (GRID_X - 1) / 2 * (win // GRID_X)
    mid_y = (GRID_Y - 1) / 2 * (tile_px // GRID_Y)
    most = freq_x // 2
    cols = real_waves(np.arange(AMBIT), win, most, LANES)
    rows = real_waves(np.arange(tile_px) - mid_y, tile_px, freq_y // 2, ROWS_PAD)
    blocks = win // AMBIT
    angles = 2.0 * np.pi * np.outer(AMBIT * np.arange(blocks) - mid_x, np.arange(most + 1)) / win
    turns = np.zeros((2, blocks, LANES))
    turns[0, :, : most + 1] = np.cos(angles)
    turns[0, :, most + 1 : 2 * most + 1] = np.cos(angles[:, 1:])
    turns[1, :, : most + 1] = -np.sin(angles)
    turns[1, :, most + 1 : 2 * most + 1] = np.sin(angles[:, 1:])
    return cols, turns.astype(np.float32).reshape(2 * blocks, 1, LANES), rows


def swapped(value, used):
    lane = lax.broadcasted_iota(jnp.int32, value.shape, 1)
    most = (used - 1) // 2
    return jnp.where(lane <= most, pltpu.roll(value, LANES - most, 1), pltpu.roll(value, most, 1))


def packed(tall, used):
    rows = tall.shape[0] - 8
    body, line = tall[:rows], jnp.broadcast_to(tall[rows : rows + 1], (8, LANES))
    lane = lax.broadcasted_iota(jnp.int32, (8, LANES), 1)
    row = lax.broadcasted_iota(jnp.int32, (8, LANES), 0)
    spare = LANES - used
    first = jnp.where(lane < used, body[:8], 0.0)
    for at in range(-(-used // spare)):
        moved = pltpu.roll(line, (used - spare * at) % LANES, 1)
        first = jnp.where((row == at) & (lane >= used), moved, first)
    return jnp.concatenate([first, body[8:]], axis=0)


def unpacked(packet, used):
    lane = lax.broadcasted_iota(jnp.int32, packet.shape, 1)
    first = packet[:8]
    lane8 = lane[:8]
    row = lax.broadcasted_iota(jnp.int32, (8, LANES), 0)
    spare = LANES - used
    line = jnp.zeros((8, LANES), F32)
    for at in range(-(-used // spare)):
        moved = pltpu.roll(first, (spare * at - used) % LANES, 1)
        here = (row == at) & (lane8 >= spare * at) & (lane8 < min(spare * at + spare, used))
        line = line + jnp.where(here, moved, 0.0)
    line = jnp.where(row == 0, jnp.sum(line, axis=0, keepdims=True), 0.0)
    return jnp.concatenate([jnp.where(lane < used, packet, 0.0), line], axis=0)


def own_place():
    return lax.axis_index("tile").astype(jnp.int32)


def fetch(pairs, sems):
    copies = [pltpu.make_async_copy(src, dst, sems.at[at]) for at, (src, dst) in enumerate(pairs)]
    for copy in copies:
        copy.start()
    return copies


def spectrum_kernel(
    used, mask_hbm, cols_hbm, turns_hbm, rows_hbm, target_hbm, out_ref, mask, cols, turns, rows, sems, target_sems
):
    tile_px = mask.shape[0]
    width = AMBIT
    count = tile_px // width
    pairs = [(rows_hbm, rows)]
    for at in range(count):
        place = pl.ds(at * width, width)
        pairs.append((mask_hbm.at[0, :, place], mask.at[:, place]))
    pairs[2:2] = [(cols_hbm, cols), (turns_hbm, turns)]
    copies = fetch(pairs, sems)
    table_copies = [copies.pop(2), copies.pop(2)]
    size = target_hbm.shape[0] // PIECES
    goals = fetch(
        [(target_hbm.at[pl.ds(at * size, size)], out_ref.at[at, pl.ds(16, size)]) for at in range(PIECES)],
        target_sems,
    )

    def turned(both, block):
        return turns[block] * both[0] + turns[block + turns.shape[0] // 2] * both[1]

    copies[0].wait()
    terms = []
    for at in range(count):
        copies[1 + at].wait()
        top, rest = halves(mask[:, at * width : (at + 1) * width])
        both = mm(rows[...], top)
        top, rest = halves(both[:ROWS_PAD] + both[ROWS_PAD:] + mm(rows[:ROWS_PAD], rest))
        terms.append(jnp.concatenate([top, rest, top], axis=1))

    for copy in table_copies:
        copy.wait()
    table = jnp.concatenate([cols[:, :LANES], cols[:, :LANES], cols[:, LANES:]], axis=0)
    waves = []
    for some in (terms,):
        wave = mm(jnp.concatenate(some, axis=0), table)
        waves += [wave[at * ROWS_PAD : (at + 1) * ROWS_PAD] for at in range(len(some))]
    waves = [(wave, swapped(wave, used)) for wave in waves]
    own = sum(turned(wave, at + 1) for at, wave in enumerate(waves))
    low, high = turned(waves[0], count + 1), turned(waves[-1], 0)

    own, low, high = [packed(part[:ROWS], used) for part in (own, low, high)]
    groups = own.shape[0] // 8
    low = pltpu.roll(low.reshape(groups, 8, LANES), 4, 1)
    upper = lax.broadcasted_iota(jnp.int32, (8, LANES), 0) < 4
    for at in range(groups):
        mine, other = own[8 * at : 8 * at + 8], low[at]
        out_ref[2 * at, :8] = jnp.where(upper, mine, other)
        out_ref[2 * at + 1, :8] = jnp.where(upper, other, mine)
        out_ref[2 * at, 8:16] = high[8 * at : 8 * at + 8]
        out_ref[2 * at + 1, 8:16] = high[8 * at : 8 * at + 8]
    for copy in goals:
        copy.wait()


def mask_spectrum(mask_tiles, target, cols, turns, rows, freq_x):
    tile_px = mask_tiles.shape[1]
    col_stack = np.concatenate(halves_np(cols), axis=1)
    row_stack = np.concatenate(halves_np(rows.T), axis=0)
    hbm = pl.BlockSpec(memory_space=pltpu.HBM)
    return pl.pallas_call(
        functools.partial(spectrum_kernel, freq_x + 1),
        in_specs=[hbm] * 5,
        out_specs=pl.BlockSpec(memory_space=pltpu.VMEM),
        out_shape=jax.ShapeDtypeStruct((PIECES, 24, LANES), F32),
        scratch_shapes=[
            pltpu.VMEM((tile_px, tile_px), F32),
            pltpu.VMEM(col_stack.shape, BF16),
            pltpu.VMEM(turns.shape, F32),
            pltpu.VMEM(row_stack.shape, BF16),
            pltpu.SemaphoreType.DMA((3 + tile_px // AMBIT,)),
            pltpu.SemaphoreType.DMA((PIECES,)),
        ],
        compiler_params=pltpu.CompilerParams(vmem_limit_bytes=20 * 2**20),
        name="mask_spectrum",
    )(in_hbm(mask_tiles), in_hbm(col_stack), in_hbm(turns), in_hbm(row_stack), in_hbm(target))


def slot_pair(first, second, used):
    spare = LANES - used
    lane = lax.broadcasted_iota(jnp.int32, (8, LANES), 1)
    groups = [part[at : at + 8] for part in (first, second) for at in range(0, part.shape[0], 8)]
    last = groups.pop()
    for at, host in enumerate((1, 2, 3, 5)):
        groups[host] = jnp.where(lane < used, groups[host], pltpu.roll(last, (used - spare * at) % LANES, 1))
    return jnp.concatenate(groups, axis=0)


def slot_half(pair, slot, used):
    spare = LANES - used
    lane = lax.broadcasted_iota(jnp.int32, (8, LANES), 1)
    last = jnp.zeros((8, LANES), F32)
    for at, host in enumerate((1, 2, 3, 5)):
        moved = pltpu.roll(pair[8 * host : 8 * host + 8], (spare * at - used) % LANES, 1)
        last = jnp.where((lane >= spare * at) & (lane < min(spare * at + spare, used)), moved, last)
    return jnp.where(slot == 0, pair[:32], jnp.concatenate([pair[32:], last], axis=0))


def slots_of(owner_ref, tiles):
    owners = owner_ref[...].astype(F32)
    lane = lax.broadcasted_iota(jnp.int32, owners.shape, 1)
    found = []
    for tile in tiles:
        owner = jnp.sum(jnp.where(lane == tile, owners, 0.0), axis=1, keepdims=True)
        before = jnp.where((owners == owner) & (lane < tile), 1.0, 0.0)
        found.append((jnp.sum(owner).astype(jnp.int32), jnp.sum(before).astype(jnp.int32)))
    return found


def tiles_of(owner_ref, owner):
    owners = owner_ref[...].astype(F32)
    lane = lax.broadcasted_iota(jnp.int32, owners.shape, 1).astype(F32)
    mine = owners == owner.astype(F32)
    tiles = owners.shape[1]
    count = jnp.sum(jnp.where(mine, 1.0, 0.0))
    if tiles == PIECES:
        return count, jnp.int32(0), jnp.int32(0)
    first = jnp.min(jnp.where(mine, lane, tiles - 1.0)).astype(jnp.int32)
    last = jnp.max(jnp.where(mine, lane, 0.0)).astype(jnp.int32)
    return count, first, last


def mate_of(me):
    return me + 1 - 2 * lax.rem(me, 2)


def route_kernel(owner_ref, pieces_ref, *rest):
    edges_ref = rest[0] if len(rest) == 3 else None
    out_ref, seen = rest[-2:]
    tiles = owner_ref.shape[1]
    me = own_place()
    base = me // PIECES * PIECES if tiles > PIECES else 0
    row = lax.broadcasted_iota(jnp.int32, (8, LANES), 0)
    mine = row // 4 == lax.rem(me, 2)

    def send(tile, owner, slot):
        at = tile - base
        high = pieces_ref[jnp.maximum(at - 1, 0), 8:16]
        low = pieces_ref[jnp.minimum(at + 1, PIECES - 1), :8]
        if edges_ref is None:
            edge_high, edge_low = jnp.zeros_like(high), jnp.zeros_like(low)
        else:
            edge_high, edge_low = edges_ref[0, 8:16], edges_ref[1, :8]
        high = jnp.where(at > 0, high, edge_high)
        low = jnp.where(at < PIECES - 1, low, edge_low)
        packet = pieces_ref[at, :8] + high + pltpu.roll(low, 4, 0)
        beside = jnp.where(mine, out_ref[owner, :8], pltpu.roll(packet, 4, 0))
        out_ref[owner, :8] = jnp.where(slot == 0, packet, beside)
        out_ref[owner, pl.ds(pl.multiple_of(8 + 8 * slot, 8), 8)] = pieces_ref[at, 16:]

    if tiles == PIECES:
        for tile, (owner, slot) in enumerate(slots_of(owner_ref, list(range(tiles)))):
            send(jnp.int32(tile), owner, slot)
        return

    def clear(at, carry):
        seen[at] = 0
        return carry

    def count(tile, carry):
        owner = owner_ref[0, tile]
        slot = seen[owner]
        seen[owner] = slot + 1
        pl.when((tile >= base) & (tile < base + PIECES))(lambda: send(tile, owner, slot))
        return carry

    lax.fori_loop(0, tiles, clear, 0)
    lax.fori_loop(0, tiles, count, 0)


def route(owner_list, pieces, edges):
    smem = pl.BlockSpec(memory_space=pltpu.SMEM)
    vmem = pl.BlockSpec(memory_space=pltpu.VMEM)
    tiles = owner_list.shape[0]
    extra = [] if edges is None else [edges]
    return pl.pallas_call(
        route_kernel,
        in_specs=[vmem if tiles == PIECES else smem, vmem] + [vmem] * len(extra),
        out_specs=vmem,
        out_shape=jax.ShapeDtypeStruct((tiles, 24, LANES), F32),
        scratch_shapes=[pltpu.SMEM((tiles,), jnp.int32)],
        compiler_params=pltpu.CompilerParams(vmem_limit_bytes=2**20),
        name="route",
    )(owner_list.reshape(1, -1), in_vmem(pieces), *extra)


def around(tile, tiles):
    return [
        (tile, None),
        (jnp.maximum(tile - 1, 0), tile > 0),
        (jnp.minimum(tile + 1, tiles - 1), tile < tiles - 1),
    ]


def tile_pick_kernel(used, owner_ref, slopes_ref, out_ref):
    tiles = [tile for tile, _ in around(mate_of(own_place()), owner_ref.shape[1])]
    for at, (owner, slot) in enumerate(slots_of(owner_ref, tiles)):
        out_ref[at] = slot_half(slopes_ref[owner], slot, used)


def tile_pick(owner_list, slopes, freq_x):
    smem = pl.BlockSpec(memory_space=pltpu.SMEM)
    vmem = pl.BlockSpec(memory_space=pltpu.VMEM)
    return pl.pallas_call(
        functools.partial(tile_pick_kernel, freq_x + 1),
        in_specs=[vmem, vmem],
        out_specs=vmem,
        out_shape=jax.ShapeDtypeStruct((3, 32, LANES), F32),
        compiler_params=pltpu.CompilerParams(vmem_limit_bytes=2**20),
        name="tile_pick",
    )(owner_list.reshape(1, -1), in_vmem(slopes))


def joined(me, mine, other):
    odd = lax.rem(me, 2) == 1
    return jnp.concatenate([jnp.where(odd, other, mine), jnp.where(odd, mine, other)], axis=0)


def update_kernel(
    used, owner_ref, slopes_ref, other_ref, mask_ref, cols, turns, rows, out_hbm, out, held, out_sems
):
    tile_px = out.shape[0]
    block = tile_px // BLOCKS
    me = own_place()
    near = around(me, owner_ref.shape[1])
    packets = []
    for at, (owner, slot) in enumerate(slots_of(owner_ref, [tile for tile, _ in near])):
        packet = unpacked(joined(me, slot_half(slopes_ref[owner], slot, used), other_ref[at]), used)
        there = near[at][1]
        packets.append(packet if there is None else jnp.where(there, packet, 0.0))

    own, last, following = [(packet, swapped(packet, used)) for packet in packets]

    def turned_back(both, block):
        return turns[block] * both[0] - turns[block + turns.shape[0] // 2] * both[1]

    count = tile_px // AMBIT
    waves = [turned_back(own, at + 1) for at in range(count)]
    waves[0] = waves[0] + turned_back(last, count + 1)
    waves[-1] = waves[-1] + turned_back(following, 0)
    blank = jnp.zeros((ROWS_PAD - ROWS, LANES), F32)
    top, rest = halves(jnp.concatenate([part for wave in waves for part in (wave, blank)], axis=0))
    wide = mm(
        jnp.concatenate([top, rest, top], axis=1),
        jnp.concatenate([cols[:LANES], cols[:LANES], cols[LANES:]], axis=0),
    )
    for at in range(count):
        top, rest = halves(wide[at * ROWS_PAD : (at + 1) * ROWS_PAD])
        held[:, at * AMBIT : (at + 1) * AMBIT] = jnp.concatenate([top, rest, top], axis=0)
    sent = []
    for at in range(BLOCKS):
        here = slice(at * block, (at + 1) * block)
        place = pl.ds(at * block, block)
        out[here] = mask_ref[0, here] - STEP_SIZE * mm(rows[here], held[...])
        copy = pltpu.make_async_copy(out.at[place], out_hbm.at[0, place], out_sems.at[at])
        copy.start()
        sent.append(copy)
    for copy in sent:
        copy.wait()


def update_tables(cols, turns, rows):
    top, rest = halves_np(rows)
    return (
        np.concatenate(halves_np(cols.T), axis=0),
        turns,
        np.concatenate([top, top, rest], axis=1),
    )


def mask_update(owner_list, slopes, other, mask_tiles, cols, turns, rows, freq_x):
    tile_px = mask_tiles.shape[1]
    smem = pl.BlockSpec(memory_space=pltpu.SMEM)
    vmem = pl.BlockSpec(memory_space=pltpu.VMEM)
    hbm = pl.BlockSpec(memory_space=pltpu.HBM)
    return pl.pallas_call(
        functools.partial(update_kernel, freq_x + 1),
        in_specs=[vmem] * 7,
        out_specs=hbm,
        out_shape=jax.ShapeDtypeStruct(mask_tiles.shape, F32),
        scratch_shapes=[
            pltpu.VMEM((tile_px, tile_px), F32),
            pltpu.VMEM((3 * ROWS_PAD, tile_px), BF16),
            pltpu.SemaphoreType.DMA((BLOCKS,)),
        ],
        compiler_params=pltpu.CompilerParams(vmem_limit_bytes=16 * 2**20),
        name="mask_update",
    )(
        owner_list.reshape(1, -1), in_vmem(slopes), other, in_vmem(mask_tiles),
        in_vmem(cols), in_vmem(turns), in_vmem(rows),
    )


def half_order():
    return np.arange(GRID_Y // 2).reshape(8, -1).T.reshape(-1)


def image_tables(freq_y, freq_x):
    places_v = np.arange(GRID_X) - (GRID_X - 1) / 2
    freqs_b = np.arange(freq_x) - (freq_x - 1) / 2
    beta = 2.0 * np.pi * np.outer(freqs_b, places_v) / GRID_X
    first = (GRID_X - CORE_X) // 2

    def block(lane_of):
        table = np.zeros((2 * LANES, 2 * LANES))
        for place, lane in lane_of:
            table[:freq_x, lane] = np.cos(beta[:, place])
            table[:freq_x, LANES + lane] = np.sin(beta[:, place])
            table[LANES : LANES + freq_x, lane] = -np.sin(beta[:, place])
            table[LANES : LANES + freq_x, LANES + lane] = np.cos(beta[:, place])
        return table

    core = block([(first + lane, lane) for lane in range(CORE_X)])
    last = first + CORE_X
    rim = block(
        [(first - 2, LANES - 2), (first - 1, LANES - 1), (last, 0), (last + 1, 1)]
    )
    places_u = half_order() + 0.5
    freqs_a = np.arange(freq_y) - (freq_y - 1) / 2
    alpha = 2.0 * np.pi * np.outer(places_u, freqs_a) / GRID_Y
    rows = np.concatenate([np.cos(alpha), np.sin(alpha)], axis=0)
    return core, rim, rows


def rim_tables(rim, kern_count):
    seats = [(LANES - 2 + at) % LANES for at in range(4)]
    top, rest = halves_np(rim)
    rim_in = np.zeros((4 * LANES, LANES), BF16)
    for seat in seats:
        for quarter, source in enumerate((seat, LANES + seat)):
            place = (seat + quarter * QUARTER) % LANES
            rim_in[: 2 * LANES, place] = top[:, source]
            rim_in[2 * LANES :, place] = top[:, source]
            rim_in[: 2 * LANES, (place + 2 * QUARTER) % LANES] = rest[:, source]
    seats = seats + [LANES + seat for seat in seats]
    top, rest = halves_np(rim.T[seats])
    blank = np.zeros((LANES - 8, 2 * LANES), BF16)
    rim_out = np.concatenate([top, top, blank[8:], rest, blank], axis=0)
    width = -(-kern_count * RIM_WIDTH // LANES) * LANES
    scatter = np.zeros((4 * LANES, width))
    for kern in range(kern_count):
        for at in range(8):
            lane = (4 * kern - 2 + at % 4) % LANES + at // 4 * LANES
            scatter[lane, kern * RIM_WIDTH + at] = 1.0
            scatter[2 * LANES + lane, kern * RIM_WIDTH + 8 + at] = 1.0
    return rim_in, rim_out, scatter.astype(BF16)


def pick_tables(freq_y, freq_x):
    col_even, col_odd = signed_picks(freq_x, LANES)
    row_even, row_odd = signed_picks(freq_y, ROWS_PAD)
    lanes = np.zeros((LANES, 2 * LANES))
    lanes[:, :freq_x] = col_even.T
    lanes[:, LANES : LANES + freq_x] = col_odd.T
    rows = np.block([[row_even, -row_odd], [-row_odd, -row_even]])
    return lanes, rows


def imaging_kernel(places, used, extra, *refs):
    owner_ref, weight_ref, pieces_ref, kern_ref, table_ref = refs[:5]
    later_hbm, refs = refs[5 : 5 + extra], refs[5 + extra :]
    slopes_ref, error_ref, later_ref, refs = refs[0], refs[1], refs[2 : 2 + extra], refs[2 + extra :]
    spec, field, rim_field, rim_slope, scale_ref, ready, goal_ref, sems = refs
    kern_count, freq_y, freq_x = kern_ref.shape[2:]
    later = fetch(list(zip(later_hbm, later_ref)), sems)
    chunk = max(size for size in range(1, CHUNK + 1) if kern_count % size == 0)
    count, first, second = tiles_of(owner_ref, own_place())
    slots = (first, second)
    split = freq_y // 2
    firsts = [slot // PIECES * PIECES for slot in slots]

    def table(name):
        start, height, width = places[name]
        return table_ref[start : start + height, :width]

    upper = lax.broadcasted_iota(jnp.int32, (8, LANES), 0) < 4
    blank = jnp.zeros((ROWS_PAD - ROWS, LANES), F32)
    targets, packets = [], []
    for slot in range(MOST):
        target = jnp.concatenate(
            [pieces_ref[firsts[slot] + at, 8 + 8 * slot : 16 + 8 * slot] for at in range(PIECES)], axis=0
        )
        targets.append(jnp.where(count > slot, target, 0.0))
        pieces = []
        for at in range(0, PIECES, 2):
            even, odd = pieces_ref[firsts[slot] + at, :8], pieces_ref[firsts[slot] + at + 1, :8]
            if slot == 0:
                pieces.append(jnp.where(upper, even, odd))
            else:
                pieces.append(pltpu.roll(jnp.where(upper, odd, even), 4, 0))
        packet = jnp.concatenate(pieces, axis=0)
        packets += [jnp.where(count > slot, unpacked(packet, used), 0.0), blank]

    top, rest = halves(jnp.concatenate(packets, axis=0))
    both = mm(
        jnp.concatenate([top, rest], axis=1), jnp.concatenate([table("lanes"), table("lanes")], axis=0)
    )
    tall = [
        jnp.concatenate([both[at : at + ROWS_PAD, :LANES], both[at : at + ROWS_PAD, LANES:]], axis=0)
        for at in range(0, MOST * ROWS_PAD, ROWS_PAD)
    ]
    top, rest = halves(jnp.concatenate(tall, axis=1))
    both = mm(table("picks"), top) + mm(table("picks"), rest)
    for slot in range(MOST):
        spec[slot] = both[:, slot * LANES : (slot + 1) * LANES]

    target = jnp.concatenate(targets, axis=1)
    one = target.astype(BF16)
    target = target - one.astype(F32)
    two = target.astype(BF16)
    three = (target - two.astype(F32)).astype(BF16)
    both = mm(table("turn"), one) + mm(table("turn"), two) + mm(table("turn"), three)
    for slot in range(MOST):
        goal_ref[slot] = both[:, slot * LANES : (slot + 1) * LANES]

    half = GRID_Y // 2
    lane = lax.broadcasted_iota(jnp.int32, (freq_y, LANES), 1)
    live_lane = lane < freq_x

    def kern_at(k):
        def one(part):
            raw = kern_ref[0, part, k]
            wide = jnp.concatenate([raw, jnp.zeros((freq_y, LANES - freq_x), F32)], axis=1)
            return wide
        return one(0), one(1)

    def side_by_side(pieces):
        return pieces[0] if len(pieces) == 1 else jnp.concatenate(pieces, axis=1)

    def apart(wide):
        size = 2 * LANES
        return [wide[:, at : at + size] for at in range(0, wide.shape[1], size)]

    def to_image(stacks):
        pieces = []
        for stack in stacks:
            top, rest = halves(stack)
            pieces.append(jnp.concatenate([top, rest, top], axis=0))
        return apart(mm(table("rows"), side_by_side(pieces)))

    def from_image(stacks):
        pieces = [jnp.concatenate(halves(stack), axis=0) for stack in stacks]
        both = mm(table("rows_t"), side_by_side(pieces))
        return apart(both[:freq_y] + both[freq_y:])

    def thrice(top, rest, name):
        both = table(name)
        height = both.shape[0] // 2
        return mm(
            jnp.concatenate([top, rest, top], axis=1),
            jnp.concatenate([both[:height], both[:height], both[height:]], axis=0),
        )

    def waves(stack):
        even_re, even_im = stack[:half, :LANES], stack[:half, LANES:]
        odd_re, odd_im = stack[half:, :LANES], stack[half:, LANES:]
        return even_re - odd_im, even_im + odd_re, even_re + odd_im, even_im - odd_re

    def unwaves(plus_re, plus_im, minus_re, minus_im):
        above = jnp.concatenate([plus_re + minus_re, plus_im + minus_im], axis=1)
        below = jnp.concatenate([plus_im - minus_im, minus_re - plus_re], axis=1)
        return jnp.concatenate([above, below], axis=0)


    rim_sums = [[] for _ in range(MOST)]

    def forward_chunk(start, new):
        tops, rests = [], []
        for step in range(chunk):
            kern_re, kern_im = kern_at(start + step)
            for slot in range(MOST):
                spec_re, spec_im = spec[slot, :freq_y], spec[slot, freq_y:]
                wave = jnp.concatenate(
                    [kern_re * spec_re - kern_im * spec_im, kern_re * spec_im + kern_im * spec_re], axis=1
                )
                top, rest = halves(wave)
                tops.append(top)
                rests.append(rest)
        top, rest = jnp.concatenate(tops, axis=0), jnp.concatenate(rests, axis=0)
        cols = thrice(top, rest, "core")
        edges = mm(jnp.concatenate([top, rest], axis=1), table("rim"))
        places = [(step, slot) for step in range(chunk) for slot in range(MOST)]
        images = to_image([cols[at * freq_y : (at + 1) * freq_y] for at in range(len(places))])
        for at, (step, slot) in enumerate(places):
            k = start + step
            weight = weight_ref[:, k : k + 1]
            new[2] = jnp.where(group_of == k, jnp.broadcast_to(weight, (8, LANES)), new[2])
            edge = edges[at * freq_y : (at + 1) * freq_y]
            column, place = divmod(k, QUARTER // 4)
            if place == 0:
                rim_sums[slot].append(edge)
            else:
                rim_sums[slot][column] = rim_sums[slot][column] + pltpu.roll(edge, 4 * place, 1)
            parts = waves(images[at])
            for part in range(4):
                field[slot, k, part] = parts[part]
            plus, minus = new[slot]
            plus = plus + weight * (parts[0] * parts[0] + parts[1] * parts[1])
            minus = minus + weight * (parts[2] * parts[2] + parts[3] * parts[3])
            new[slot] = (plus, minus)

    blank = jnp.zeros((half, LANES), F32)
    group_of = lax.rem(lax.broadcasted_iota(jnp.int32, (8, LANES), 1) + 2, LANES) // 4
    sums = [(blank, blank), (blank, blank), jnp.zeros((8, LANES), F32)]
    for start in range(0, kern_count, chunk):
        forward_chunk(start, sums)
    lane_weight = sums.pop()

    norm = 1.0 / (64.0 * GRID_Y * GRID_X)
    square = norm * norm
    lane_half = lax.broadcasted_iota(jnp.int32, (half, LANES), 1)
    near = (lane_half < 2) | (lane_half >= LANES - 2)
    row_8 = lax.broadcasted_iota(jnp.int32, (8, LANES), 0)

    def rows_beside(value, other):
        first, last = value[:8], value[half - 8 :]
        later = jnp.where(row_8 == 7, last, pltpu.roll(first, 7, 0))
        sooner = jnp.where(row_8 == 0, other[:8], pltpu.roll(last, 1, 0))
        return jnp.concatenate([value[8:], later], axis=0) + jnp.concatenate([sooner, value[:-8]], axis=0)

    at_first, at_last = lane_half == 0, lane_half == LANES - 1

    def spread_out(value, rows, left, right):
        return value + DIFFUSE_RATE * (rows + left + right - 4.0 * value)

    def sides(value):
        return pltpu.roll(value, 1, 1), pltpu.roll(value, LANES - 1, 1)

    def beside(core, rim):
        return jnp.where(at_first, rim[0], core[0]), jnp.where(at_last, rim[1], core[1])

    def blur(core, rim):
        core_sides = [sides(value) for value in core]
        rim_sides = [sides(value) for value in rim]
        rim_one = [
            spread_out(rim[at], rows_beside(rim[at], rim[1 - at]), *beside(rim_sides[at], core_sides[at]))
            for at in range(2)
        ]
        core_one = [
            spread_out(core[at], rows_beside(core[at], core[1 - at]), *beside(core_sides[at], rim_sides[at]))
            for at in range(2)
        ]
        return [
            spread_out(
                core_one[at],
                rows_beside(core_one[at], core_one[1 - at]),
                *beside(sides(core_one[at]), sides(rim_one[at])),
            )
            for at in range(2)
        ]

    def blur_back(core):
        core_sides = [sides(value) for value in core]
        none = jnp.zeros((half, LANES), F32)
        rim_one = [DIFFUSE_RATE * sum(beside((none, none), core_sides[at])) for at in range(2)]
        core_one = [
            spread_out(core[at], rows_beside(core[at], core[1 - at]), *beside(core_sides[at], (none, none)))
            for at in range(2)
        ]
        core_sides = [sides(value) for value in core_one]
        rim_sides = [sides(value) for value in rim_one]
        rim_two = [
            spread_out(rim_one[at], rows_beside(rim_one[at], rim_one[1 - at]), *beside(rim_sides[at], core_sides[at]))
            for at in range(2)
        ]
        core_two = [
            spread_out(core_one[at], rows_beside(core_one[at], core_one[1 - at]), *beside(core_sides[at], rim_sides[at]))
            for at in range(2)
        ]
        return core_two, rim_two

    def fold(value):
        def back(amount):
            return pltpu.roll(value, LANES - amount, 1)
        value = value + back(48)
        value = value + back(24)
        value = value + back(12)
        return value + back(4) + back(8)

    def unfold(value):
        value = jnp.where(near, value, 0.0)
        value = value + pltpu.roll(value, 4, 1) + pltpu.roll(value, 8, 1)
        value = value + pltpu.roll(value, 12, 1)
        value = value + pltpu.roll(value, 24, 1)
        return value + pltpu.roll(value, 48, 1)

    def rim_columns(slot):
        quarter = lax.rem(lane + 2, LANES) // QUARTER
        real = imag = jnp.zeros((freq_y, LANES), F32)
        for column, both in enumerate(rim_sums[slot]):
            both = both + pltpu.roll(both, 2 * QUARTER, 1)
            for_real = both if column == 0 else pltpu.roll(both, column * QUARTER, 1)
            for_imag = both if column == 1 else pltpu.roll(both, (column - 1) * QUARTER % LANES, 1)
            real = jnp.where(quarter == column, for_real, real)
            imag = jnp.where(quarter == column, for_imag, imag)
        return jnp.concatenate([real, imag], axis=1)

    error = jnp.float32(0.0)
    rim_halves = []
    for slot in range(2):
        live = (count > slot).astype(F32)
        rim_parts = waves(to_image([rim_columns(slot)])[0])
        for part in range(4):
            rim_field[slot, part] = rim_parts[part]
        weights = jnp.concatenate([lane_weight] * (half // 8), axis=0)
        rim_plus = weights * (rim_parts[0] * rim_parts[0] + rim_parts[1] * rim_parts[1])
        rim_minus = weights * (rim_parts[2] * rim_parts[2] + rim_parts[3] * rim_parts[3])
        core = [part * square for part in sums[slot]]
        rim = [jnp.where(near, fold(part), 0.0) * square for part in (rim_plus, rim_minus)]
        core = blur(core, rim)

        def slope_of(value, goal):
            resist = 1.0 / (1.0 + jnp.exp(-RESIST_SLOPE * (value - RESIST_LEVEL)))
            misfit = resist - goal
            return (2.0 * RESIST_SLOPE) * misfit * resist * (1.0 - resist), jnp.sum(misfit * misfit)

        slope_plus, err_plus = slope_of(core[0], goal_ref[slot, :half])
        slope_minus, err_minus = slope_of(core[1], goal_ref[slot, half:])
        error = error + live * (err_plus + err_minus)
        core, rim = blur_back([slope_plus, slope_minus])
        factor = 2.0 * square
        for at in range(2):
            scale_ref[slot, at] = core[at] * factor
        rim_f_plus = unfold(rim[0] * factor) * weights
        rim_f_minus = unfold(rim[1] * factor) * weights
        edge = from_image(
            [
                unwaves(
                    rim_f_plus * rim_field[slot, 0],
                    rim_f_plus * rim_field[slot, 1],
                    rim_f_minus * rim_field[slot, 2],
                    rim_f_minus * rim_field[slot, 3],
                )
            ]
        )[0]
        rim_halves.append(jnp.concatenate(halves(edge), axis=1))
    rim_stack = jnp.concatenate(rim_halves, axis=0)
    for part in range(0, rim_slope.shape[2], 2 * LANES):
        moved = mm(rim_stack, table(f"scatter{part}"))
        for slot in range(MOST):
            rim_slope[slot, :, part : part + moved.shape[1]] = moved[slot * freq_y : (slot + 1) * freq_y]
    error_ref[0] = error * (1.0 / (GRID_Y * CORE_X))


    def backward_chunk(start, sums):
        images, edges = [], []
        for step in range(chunk):
            k = start + step
            weight = weight_ref[:, k : k + 1]
            for slot in range(MOST):
                plus = scale_ref[slot, 0] * weight
                minus = scale_ref[slot, 1] * weight
                images.append(
                    unwaves(
                        plus * field[slot, k, 0],
                        plus * field[slot, k, 1],
                        minus * field[slot, k, 2],
                        minus * field[slot, k, 3],
                    )
                )
                column = k // RIM_KERNS * LANES
                edge = rim_slope[slot, :, column : column + LANES]
                if k % RIM_KERNS != 0:
                    edge = pltpu.roll(edge, LANES - k % RIM_KERNS * RIM_WIDTH, 1)
                edge = edge.astype(BF16)
                edges.append(jnp.concatenate([edge, edge], axis=1))
        pairs = [halves(cols) for cols in from_image(images)]
        top, rest = [jnp.concatenate(part, axis=0) for part in zip(*pairs)]
        waves_all = thrice(top, rest, "core_t") + mm(jnp.concatenate(edges, axis=0), table("rim_t"))
        for step in range(chunk):
            kern_re, kern_im = kern_at(start + step)
            for slot in range(MOST):
                at = (MOST * step + slot) * freq_y
                wave_re, wave_im = waves_all[at : at + freq_y, :LANES], waves_all[at : at + freq_y, LANES:]
                sums[slot][0] += wave_re * kern_re + wave_im * kern_im
                sums[slot][1] += wave_im * kern_re - wave_re * kern_im

    slopes = [[jnp.zeros((freq_y, LANES), F32)] * 2 for _ in range(MOST)]
    for start in range(0, kern_count, chunk):
        backward_chunk(start, slopes)

    tall = jnp.concatenate([jnp.concatenate(slopes[slot], axis=0) for slot in range(MOST)], axis=1)
    both = mm(table("picks_t"), jnp.concatenate(halves(tall), axis=0))
    wide = [
        jnp.concatenate([both[:ROWS_PAD, at : at + LANES], both[ROWS_PAD:, at : at + LANES]], axis=1)
        for at in range(0, MOST * LANES, LANES)
    ]
    top, rest = halves(jnp.concatenate(wide, axis=0))
    both = mm(
        jnp.concatenate([top, rest], axis=1), jnp.concatenate([table("lanes_t"), table("lanes_t")], axis=0)
    )
    packets = [packed(both[at : at + ROWS], used) for at in range(0, MOST * ROWS_PAD, ROWS_PAD)]
    for at in range(2):
        here = slice(at * split, (at + 1) * split)
        ready[at] = slot_pair(packets[0][here], packets[1][here], used)

    def give(pair_at, carry):
        slopes_ref[2 * pair_at] = ready[0]
        slopes_ref[2 * pair_at + 1] = ready[1]
        return carry

    lax.fori_loop(0, slopes_ref.shape[0] // 2, give, 0)
    for copy in later:
        copy.wait()


def imaging_table(kern_count, freq_y, freq_x):
    core, rim, rows = image_tables(freq_y, freq_x)
    lanes, picks = pick_tables(freq_y, freq_x)

    def tall(table):
        return np.concatenate(halves_np(table), axis=0)

    def three(table):
        top, rest = halves_np(table)
        return np.concatenate([top, top, rest], axis=1)

    def square_up(table):
        top, rest = halves_np(table)
        return np.block([[top, top], [rest, np.zeros_like(rest)]])

    rim_in, rim_out, scatter = rim_tables(rim, kern_count)
    tables = {
        "core": tall(core),
        "core_t": tall(core.T),
        "rim": rim_in,
        "rim_t": rim_out,
        "rows": three(rows),
        "rows_t": square_up(rows.T),
        "lanes": lanes.astype(BF16),
        "lanes_t": lanes.T.astype(BF16),
        "picks": picks.astype(BF16),
        "picks_t": np.concatenate([picks.T, picks.T], axis=1).astype(BF16),
        "turn": np.eye(GRID_Y)[
            np.concatenate([GRID_Y // 2 + half_order(), GRID_Y // 2 - 1 - half_order()])
        ].astype(BF16),
    }
    for part in range(0, scatter.shape[1], 2 * LANES):
        tables[f"scatter{part}"] = scatter[:, part : part + 2 * LANES]
    places, stacked, start = {}, [], 0
    for name, piece in tables.items():
        height, width = piece.shape
        places[name] = (start, height, width)
        stacked.append(np.pad(piece, ((0, 0), (0, 2 * LANES - width))))
        start += height
    return places, np.concatenate(stacked, axis=0)


def owner_imaging(owner_list, kern_weight, pieces, kernels, places, table, later):
    kern_count, freq_y, freq_x = kernels.shape[2:]
    tiles, split = owner_list.shape[0], freq_y // 2
    half = GRID_Y // 2
    smem = pl.BlockSpec(memory_space=pltpu.SMEM)
    vmem = pl.BlockSpec(memory_space=pltpu.VMEM)
    hbm = pl.BlockSpec(memory_space=pltpu.HBM)
    return pl.pallas_call(
        functools.partial(imaging_kernel, places, freq_x + 1, len(later)),
        in_specs=[vmem] * 5 + [hbm] * len(later),
        out_specs=(vmem, smem) + (vmem,) * len(later),
        out_shape=(
            jax.ShapeDtypeStruct((tiles, 2 * split - 8, LANES), F32),
            jax.ShapeDtypeStruct((1,), F32),
        )
        + tuple(jax.ShapeDtypeStruct(part.shape, part.dtype) for part in later),
        scratch_shapes=[
            pltpu.VMEM((MOST, 2 * freq_y, LANES), F32),
            pltpu.VMEM((MOST, kern_count, 4, half, LANES), F32),
            pltpu.VMEM((MOST, 4, half, LANES), F32),
            pltpu.VMEM((MOST, freq_y, -(-kern_count * RIM_WIDTH // LANES) * LANES), F32),
            pltpu.VMEM((MOST, 2, half, LANES), F32),
            pltpu.VMEM((2, 2 * split - 8, LANES), F32),
            pltpu.VMEM((MOST, 2 * half, LANES), F32),
            pltpu.SemaphoreType.DMA((len(later),)),
        ],
        compiler_params=pltpu.CompilerParams(vmem_limit_bytes=20 * 2**20),
        name="owner_imaging",
    )(
        owner_list.reshape(1, -1), kern_weight.reshape(1, -1), in_vmem(pieces), in_vmem(kernels),
        in_vmem(table), *[in_hbm(part) for part in later],
    )


def on_device(mask_tiles, target_grid, kernels, kern_weight, owner_list):
    tile_px = mask_tiles.shape[1]
    freq_y, freq_x = kernels.shape[3:]
    count = lax.axis_size("tile")
    cols, turns, rows = mask_tables(tile_px, freq_y, freq_x)
    owner_list = owner_list.reshape(-1)
    mates = [(i, i + 1 - 2 * (i % 2)) for i in range(count)]

    pieces = mask_spectrum(mask_tiles, target_grid.reshape(GRID_Y, CORE_X), cols, turns, rows, freq_x)
    places, table = imaging_table(kernels.shape[2], freq_y, freq_x)
    pieces, table = lax.optimization_barrier((pieces, jnp.asarray(table)))
    if count == PIECES:
        pieces, edges = lax.all_to_all(pieces, "tile", 0, 0, tiled=True), None
    else:
        groups = [list(range(at, at + PIECES)) for at in range(0, count, PIECES)]
        pieces = lax.all_to_all(pieces, "tile", 0, 0, axis_index_groups=groups, tiled=True)
        later = [(i, i + PIECES) for i in range(count - PIECES)]
        sooner = [(i + PIECES, i) for i in range(count - PIECES)]
        edges = jnp.stack(
            [lax.ppermute(pieces[PIECES - 1], "tile", later), lax.ppermute(pieces[0], "tile", sooner)]
        )
    pieces = lax.all_to_all(route(owner_list, pieces, edges), "tile", 0, 0, tiled=True)
    slopes, owner_error, *held = owner_imaging(
        owner_list, kern_weight, pieces, kernels, places, table,
        (mask_tiles,) + update_tables(cols, turns, rows),
    )
    slopes = lax.all_to_all(slopes, "tile", 0, 0, tiled=True)
    other = lax.ppermute(tile_pick(owner_list, slopes, freq_x), "tile", mates)
    current = mask_update(owner_list, slopes, other, *held, freq_x)
    return (current, owner_error)


def solution(mesh):
    placed = (
        P(("stripe", "tile"), None, None),
        P(("stripe", "tile"), None),
        P("tile", None, None, None, None),
        P(),
        P("stripe", None),
    )
    return jax.shard_map(
        on_device,
        mesh=mesh,
        in_specs=placed,
        out_specs=(P(("stripe", "tile"), None, None), P(("stripe", "tile"))),
        check_vma=False,
    )
```

```python
import functools

import jax
import jax.numpy as jnp
import numpy as np
from jax import lax
from jax.experimental import pallas as pl
from jax.experimental.pallas import tpu as pltpu
from jax.sharding import PartitionSpec as P

AMBIT = 256
GRID_X = 192
GRID_Y = 128
CORE_X = 128
RESIST_SLOPE = 3.0
RESIST_LEVEL = 1.2
DIFFUSE_RATE = 0.2
STEP_SIZE = 1.0

LANES = 128
MOST = 2
BLOCKS = 8
PIECES = 16
CHUNK = 6
QUARTER = 32
RIM_WIDTH = 16
RIM_KERNS = LANES // RIM_WIDTH
ROWS = 72
ROWS_PAD = 80
F32 = jnp.float32
BF16 = jnp.bfloat16


def halves_np(table):
    table = np.asarray(table, np.float32)
    top = table.astype(BF16)
    rest = (table - top.astype(np.float32)).astype(BF16)
    return top, rest


def halves(value):
    top = value.astype(BF16)
    rest = (value - top.astype(F32)).astype(BF16)
    return top, rest


def mm(left, right):
    return jnp.dot(left, right, preferred_element_type=F32)


def in_hbm(value):
    return pltpu.with_memory_space_constraint(jnp.asarray(value), pltpu.HBM)


def in_vmem(value):
    return pltpu.with_memory_space_constraint(jnp.asarray(value), pltpu.VMEM)


def real_waves(places, period, most, width):
    angles = 2.0 * np.pi * np.outer(places, np.arange(most + 1)) / period
    waves = np.concatenate([np.cos(angles), np.sin(angles[:, 1:])], axis=1)
    return np.pad(waves, ((0, 0), (0, width - waves.shape[1])))


def signed_picks(count, width):
    freqs = np.arange(count) - count // 2
    most = count // 2
    even = np.zeros((count, width))
    odd = np.zeros((count, width))
    for at, freq in enumerate(freqs):
        even[at, abs(freq)] = 1.0
        if freq != 0:
            odd[at, most + abs(freq)] = np.sign(freq)
    return even, odd


def mask_tables(tile_px, freq_y, freq_x):
    win = tile_px + 2 * AMBIT
    mid_x = (GRID_X - 1) / 2 * (win // GRID_X)
    mid_y = (GRID_Y - 1) / 2 * (tile_px // GRID_Y)
    most = freq_x // 2
    cols = real_waves(np.arange(AMBIT), win, most, LANES)
    rows = real_waves(np.arange(tile_px) - mid_y, tile_px, freq_y // 2, ROWS_PAD)
    blocks = win // AMBIT
    angles = 2.0 * np.pi * np.outer(AMBIT * np.arange(blocks) - mid_x, np.arange(most + 1)) / win
    turns = np.zeros((2, blocks, LANES))
    turns[0, :, : most + 1] = np.cos(angles)
    turns[0, :, most + 1 : 2 * most + 1] = np.cos(angles[:, 1:])
    turns[1, :, : most + 1] = -np.sin(angles)
    turns[1, :, most + 1 : 2 * most + 1] = np.sin(angles[:, 1:])
    return cols, turns.astype(np.float32).reshape(2 * blocks, 1, LANES), rows


def swapped(value, used):
    lane = lax.broadcasted_iota(jnp.int32, value.shape, 1)
    most = (used - 1) // 2
    return jnp.where(lane <= most, pltpu.roll(value, LANES - most, 1), pltpu.roll(value, most, 1))


def packed(tall, used):
    rows = tall.shape[0] - 8
    body, line = tall[:rows], jnp.broadcast_to(tall[rows : rows + 1], (8, LANES))
    lane = lax.broadcasted_iota(jnp.int32, (8, LANES), 1)
    row = lax.broadcasted_iota(jnp.int32, (8, LANES), 0)
    spare = LANES - used
    first = jnp.where(lane < used, body[:8], 0.0)
    for at in range(-(-used // spare)):
        moved = pltpu.roll(line, (used - spare * at) % LANES, 1)
        first = jnp.where((row == at) & (lane >= used), moved, first)
    return jnp.concatenate([first, body[8:]], axis=0)


def unpacked(packet, used):
    lane = lax.broadcasted_iota(jnp.int32, packet.shape, 1)
    first = packet[:8]
    lane8 = lane[:8]
    row = lax.broadcasted_iota(jnp.int32, (8, LANES), 0)
    spare = LANES - used
    line = jnp.zeros((8, LANES), F32)
    for at in range(-(-used // spare)):
        moved = pltpu.roll(first, (spare * at - used) % LANES, 1)
        here = (row == at) & (lane8 >= spare * at) & (lane8 < min(spare * at + spare, used))
        line = line + jnp.where(here, moved, 0.0)
    line = jnp.where(row == 0, jnp.sum(line, axis=0, keepdims=True), 0.0)
    return jnp.concatenate([jnp.where(lane < used, packet, 0.0), line], axis=0)


def own_place():
    return lax.axis_index("tile").astype(jnp.int32)


def fetch(pairs, sems):
    copies = [pltpu.make_async_copy(src, dst, sems.at[at]) for at, (src, dst) in enumerate(pairs)]
    for copy in copies:
        copy.start()
    return copies


def spectrum_kernel(
    used, mask_hbm, cols_hbm, turns_hbm, rows_hbm, target_hbm, out_ref, mask, cols, turns, rows, sems, target_sems
):
    tile_px = mask.shape[0]
    width = AMBIT
    count = tile_px // width
    pairs = [(rows_hbm, rows)]
    for at in range(count):
        place = pl.ds(at * width, width)
        pairs.append((mask_hbm.at[0, :, place], mask.at[:, place]))
    pairs[2:2] = [(cols_hbm, cols), (turns_hbm, turns)]
    copies = fetch(pairs, sems)
    table_copies = [copies.pop(2), copies.pop(2)]
    size = target_hbm.shape[0] // PIECES
    goals = fetch(
        [(target_hbm.at[pl.ds(at * size, size)], out_ref.at[at, pl.ds(16, size)]) for at in range(PIECES)],
        target_sems,
    )

    def turned(both, block):
        return turns[block] * both[0] + turns[block + turns.shape[0] // 2] * both[1]

    copies[0].wait()
    terms = []
    for at in range(count):
        copies[1 + at].wait()
        top, rest = halves(mask[:, at * width : (at + 1) * width])
        both = mm(rows[...], top)
        top, rest = halves(both[:ROWS_PAD] + both[ROWS_PAD:] + mm(rows[:ROWS_PAD], rest))
        terms.append(jnp.concatenate([top, rest, top], axis=1))

    for copy in table_copies:
        copy.wait()
    table = jnp.concatenate([cols[:, :LANES], cols[:, :LANES], cols[:, LANES:]], axis=0)
    waves = []
    for some in (terms,):
        wave = mm(jnp.concatenate(some, axis=0), table)
        waves += [wave[at * ROWS_PAD : (at + 1) * ROWS_PAD] for at in range(len(some))]
    waves = [(wave, swapped(wave, used)) for wave in waves]
    own = sum(turned(wave, at + 1) for at, wave in enumerate(waves))
    low, high = turned(waves[0], count + 1), turned(waves[-1], 0)

    own, low, high = [packed(part[:ROWS], used) for part in (own, low, high)]
    groups = own.shape[0] // 8
    low = pltpu.roll(low.reshape(groups, 8, LANES), 4, 1)
    upper = lax.broadcasted_iota(jnp.int32, (8, LANES), 0) < 4
    for at in range(groups):
        mine, other = own[8 * at : 8 * at + 8], low[at]
        out_ref[2 * at, :8] = jnp.where(upper, mine, other)
        out_ref[2 * at + 1, :8] = jnp.where(upper, other, mine)
        out_ref[2 * at, 8:16] = high[8 * at : 8 * at + 8]
        out_ref[2 * at + 1, 8:16] = high[8 * at : 8 * at + 8]
    for copy in goals:
        copy.wait()


def mask_spectrum(mask_tiles, target, cols, turns, rows, freq_x):
    tile_px = mask_tiles.shape[1]
    col_stack = np.concatenate(halves_np(cols), axis=1)
    row_stack = np.concatenate(halves_np(rows.T), axis=0)
    hbm = pl.BlockSpec(memory_space=pltpu.HBM)
    return pl.pallas_call(
        functools.partial(spectrum_kernel, freq_x + 1),
        in_specs=[hbm] * 5,
        out_specs=pl.BlockSpec(memory_space=pltpu.VMEM),
        out_shape=jax.ShapeDtypeStruct((PIECES, 24, LANES), F32),
        scratch_shapes=[
            pltpu.VMEM((tile_px, tile_px), F32),
            pltpu.VMEM(col_stack.shape, BF16),
            pltpu.VMEM(turns.shape, F32),
            pltpu.VMEM(row_stack.shape, BF16),
            pltpu.SemaphoreType.DMA((3 + tile_px // AMBIT,)),
            pltpu.SemaphoreType.DMA((PIECES,)),
        ],
        compiler_params=pltpu.CompilerParams(vmem_limit_bytes=20 * 2**20),
        name="mask_spectrum",
    )(in_hbm(mask_tiles), in_hbm(col_stack), in_hbm(turns), in_hbm(row_stack), in_hbm(target))


def slot_pair(first, second, used):
    spare = LANES - used
    lane = lax.broadcasted_iota(jnp.int32, (8, LANES), 1)
    groups = [part[at : at + 8] for part in (first, second) for at in range(0, part.shape[0], 8)]
    last = groups.pop()
    for at, host in enumerate((1, 2, 3, 5)):
        groups[host] = jnp.where(lane < used, groups[host], pltpu.roll(last, (used - spare * at) % LANES, 1))
    return jnp.concatenate(groups, axis=0)


def slot_half(pair, slot, used):
    spare = LANES - used
    lane = lax.broadcasted_iota(jnp.int32, (8, LANES), 1)
    last = jnp.zeros((8, LANES), F32)
    for at, host in enumerate((1, 2, 3, 5)):
        moved = pltpu.roll(pair[8 * host : 8 * host + 8], (spare * at - used) % LANES, 1)
        last = jnp.where((lane >= spare * at) & (lane < min(spare * at + spare, used)), moved, last)
    return jnp.where(slot == 0, pair[:32], jnp.concatenate([pair[32:], last], axis=0))


def slots_of(owner_ref, tiles):
    owners = owner_ref[...].astype(F32)
    lane = lax.broadcasted_iota(jnp.int32, owners.shape, 1)
    found = []
    for tile in tiles:
        owner = jnp.sum(jnp.where(lane == tile, owners, 0.0), axis=1, keepdims=True)
        before = jnp.where((owners == owner) & (lane < tile), 1.0, 0.0)
        found.append((jnp.sum(owner).astype(jnp.int32), jnp.sum(before).astype(jnp.int32)))
    return found


def tiles_of(owner_ref, owner):
    owners = owner_ref[...].astype(F32)
    lane = lax.broadcasted_iota(jnp.int32, owners.shape, 1).astype(F32)
    mine = owners == owner.astype(F32)
    tiles = owners.shape[1]
    count = jnp.sum(jnp.where(mine, 1.0, 0.0))
    if tiles == PIECES:
        return count, jnp.int32(0), jnp.int32(0)
    first = jnp.min(jnp.where(mine, lane, tiles - 1.0)).astype(jnp.int32)
    last = jnp.max(jnp.where(mine, lane, 0.0)).astype(jnp.int32)
    return count, first, last


def mate_of(me):
    return me + 1 - 2 * lax.rem(me, 2)


def route_kernel(owner_ref, pieces_ref, *rest):
    edges_ref = rest[0] if len(rest) == 3 else None
    out_ref, seen = rest[-2:]
    tiles = owner_ref.shape[1]
    me = own_place()
    base = me // PIECES * PIECES if tiles > PIECES else 0
    row = lax.broadcasted_iota(jnp.int32, (8, LANES), 0)
    mine = row // 4 == lax.rem(me, 2)

    def send(tile, owner, slot):
        at = tile - base
        high = pieces_ref[jnp.maximum(at - 1, 0), 8:16]
        low = pieces_ref[jnp.minimum(at + 1, PIECES - 1), :8]
        if edges_ref is None:
            edge_high, edge_low = jnp.zeros_like(high), jnp.zeros_like(low)
        else:
            edge_high, edge_low = edges_ref[0, 8:16], edges_ref[1, :8]
        high = jnp.where(at > 0, high, edge_high)
        low = jnp.where(at < PIECES - 1, low, edge_low)
        packet = pieces_ref[at, :8] + high + pltpu.roll(low, 4, 0)
        beside = jnp.where(mine, out_ref[owner, :8], pltpu.roll(packet, 4, 0))
        out_ref[owner, :8] = jnp.where(slot == 0, packet, beside)
        out_ref[owner, pl.ds(pl.multiple_of(8 + 8 * slot, 8), 8)] = pieces_ref[at, 16:]

    if tiles == PIECES:
        for tile, (owner, slot) in enumerate(slots_of(owner_ref, list(range(tiles)))):
            send(jnp.int32(tile), owner, slot)
        return

    def clear(at, carry):
        seen[at] = 0
        return carry

    def count(tile, carry):
        owner = owner_ref[0, tile]
        slot = seen[owner]
        seen[owner] = slot + 1
        pl.when((tile >= base) & (tile < base + PIECES))(lambda: send(tile, owner, slot))
        return carry

    lax.fori_loop(0, tiles, clear, 0)
    lax.fori_loop(0, tiles, count, 0)


def route(owner_list, pieces, edges):
    smem = pl.BlockSpec(memory_space=pltpu.SMEM)
    vmem = pl.BlockSpec(memory_space=pltpu.VMEM)
    tiles = owner_list.shape[0]
    extra = [] if edges is None else [edges]
    return pl.pallas_call(
        route_kernel,
        in_specs=[vmem if tiles == PIECES else smem, vmem] + [vmem] * len(extra),
        out_specs=vmem,
        out_shape=jax.ShapeDtypeStruct((tiles, 24, LANES), F32),
        scratch_shapes=[pltpu.SMEM((tiles,), jnp.int32)],
        compiler_params=pltpu.CompilerParams(vmem_limit_bytes=2**20),
        name="route",
    )(owner_list.reshape(1, -1), in_vmem(pieces), *extra)


def around(tile, tiles):
    return [
        (tile, None),
        (jnp.maximum(tile - 1, 0), tile > 0),
        (jnp.minimum(tile + 1, tiles - 1), tile < tiles - 1),
    ]


def tile_pick_kernel(used, owner_ref, slopes_ref, out_ref):
    tiles = [tile for tile, _ in around(mate_of(own_place()), owner_ref.shape[1])]
    for at, (owner, slot) in enumerate(slots_of(owner_ref, tiles)):
        out_ref[at] = slot_half(slopes_ref[owner], slot, used)


def tile_pick(owner_list, slopes, freq_x):
    smem = pl.BlockSpec(memory_space=pltpu.SMEM)
    vmem = pl.BlockSpec(memory_space=pltpu.VMEM)
    return pl.pallas_call(
        functools.partial(tile_pick_kernel, freq_x + 1),
        in_specs=[vmem, vmem],
        out_specs=vmem,
        out_shape=jax.ShapeDtypeStruct((3, 32, LANES), F32),
        compiler_params=pltpu.CompilerParams(vmem_limit_bytes=2**20),
        name="tile_pick",
    )(owner_list.reshape(1, -1), in_vmem(slopes))


def joined(me, mine, other):
    odd = lax.rem(me, 2) == 1
    return jnp.concatenate([jnp.where(odd, other, mine), jnp.where(odd, mine, other)], axis=0)


def update_kernel(
    used, owner_ref, slopes_ref, other_ref, mask_ref, cols, turns, rows, out_hbm, out, held, out_sems
):
    tile_px = out.shape[0]
    block = tile_px // BLOCKS
    me = own_place()
    near = around(me, owner_ref.shape[1])
    packets = []
    for at, (owner, slot) in enumerate(slots_of(owner_ref, [tile for tile, _ in near])):
        packet = unpacked(joined(me, slot_half(slopes_ref[owner], slot, used), other_ref[at]), used)
        there = near[at][1]
        packets.append(packet if there is None else jnp.where(there, packet, 0.0))

    own, last, following = [(packet, swapped(packet, used)) for packet in packets]

    def turned_back(both, block):
        return turns[block] * both[0] - turns[block + turns.shape[0] // 2] * both[1]

    count = tile_px // AMBIT
    waves = [turned_back(own, at + 1) for at in range(count)]
    waves[0] = waves[0] + turned_back(last, count + 1)
    waves[-1] = waves[-1] + turned_back(following, 0)
    blank = jnp.zeros((ROWS_PAD - ROWS, LANES), F32)
    top, rest = halves(jnp.concatenate([part for wave in waves for part in (wave, blank)], axis=0))
    wide = mm(
        jnp.concatenate([top, rest, top], axis=1),
        jnp.concatenate([cols[:LANES], cols[:LANES], cols[LANES:]], axis=0),
    )
    for at in range(count):
        top, rest = halves(wide[at * ROWS_PAD : (at + 1) * ROWS_PAD])
        held[:, at * AMBIT : (at + 1) * AMBIT] = jnp.concatenate([top, rest, top], axis=0)
    sent = []
    for at in range(BLOCKS):
        here = slice(at * block, (at + 1) * block)
        place = pl.ds(at * block, block)
        out[here] = mask_ref[0, here] - STEP_SIZE * mm(rows[here], held[...])
        copy = pltpu.make_async_copy(out.at[place], out_hbm.at[0, place], out_sems.at[at])
        copy.start()
        sent.append(copy)
    for copy in sent:
        copy.wait()


def update_tables(cols, turns, rows):
    top, rest = halves_np(rows)
    return (
        np.concatenate(halves_np(cols.T), axis=0),
        turns,
        np.concatenate([top, top, rest], axis=1),
    )


def mask_update(owner_list, slopes, other, mask_tiles, cols, turns, rows, freq_x):
    tile_px = mask_tiles.shape[1]
    smem = pl.BlockSpec(memory_space=pltpu.SMEM)
    vmem = pl.BlockSpec(memory_space=pltpu.VMEM)
    hbm = pl.BlockSpec(memory_space=pltpu.HBM)
    return pl.pallas_call(
        functools.partial(update_kernel, freq_x + 1),
        in_specs=[vmem] * 7,
        out_specs=hbm,
        out_shape=jax.ShapeDtypeStruct(mask_tiles.shape, F32),
        scratch_shapes=[
            pltpu.VMEM((tile_px, tile_px), F32),
            pltpu.VMEM((3 * ROWS_PAD, tile_px), BF16),
            pltpu.SemaphoreType.DMA((BLOCKS,)),
        ],
        compiler_params=pltpu.CompilerParams(vmem_limit_bytes=16 * 2**20),
        name="mask_update",
    )(
        owner_list.reshape(1, -1), in_vmem(slopes), other, in_vmem(mask_tiles),
        in_vmem(cols), in_vmem(turns), in_vmem(rows),
    )


def half_order():
    return np.arange(GRID_Y // 2).reshape(8, -1).T.reshape(-1)


def image_tables(freq_y, freq_x):
    places_v = np.arange(GRID_X) - (GRID_X - 1) / 2
    freqs_b = np.arange(freq_x) - (freq_x - 1) / 2
    beta = 2.0 * np.pi * np.outer(freqs_b, places_v) / GRID_X
    first = (GRID_X - CORE_X) // 2

    def block(lane_of):
        table = np.zeros((2 * LANES, 2 * LANES))
        for place, lane in lane_of:
            table[:freq_x, lane] = np.cos(beta[:, place])
            table[:freq_x, LANES + lane] = np.sin(beta[:, place])
            table[LANES : LANES + freq_x, lane] = -np.sin(beta[:, place])
            table[LANES : LANES + freq_x, LANES + lane] = np.cos(beta[:, place])
        return table

    core = block([(first + lane, lane) for lane in range(CORE_X)])
    last = first + CORE_X
    rim = block(
        [(first - 2, LANES - 2), (first - 1, LANES - 1), (last, 0), (last + 1, 1)]
    )
    places_u = half_order() + 0.5
    freqs_a = np.arange(freq_y) - (freq_y - 1) / 2
    alpha = 2.0 * np.pi * np.outer(places_u, freqs_a) / GRID_Y
    rows = np.concatenate([np.cos(alpha), np.sin(alpha)], axis=0)
    return core, rim, rows


def rim_tables(rim, kern_count):
    seats = [(LANES - 2 + at) % LANES for at in range(4)]
    top, rest = halves_np(rim)
    rim_in = np.zeros((4 * LANES, LANES), BF16)
    for seat in seats:
        for quarter, source in enumerate((seat, LANES + seat)):
            place = (seat + quarter * QUARTER) % LANES
            rim_in[: 2 * LANES, place] = top[:, source]
            rim_in[2 * LANES :, place] = top[:, source]
            rim_in[: 2 * LANES, (place + 2 * QUARTER) % LANES] = rest[:, source]
    seats = seats + [LANES + seat for seat in seats]
    top, rest = halves_np(rim.T[seats])
    blank = np.zeros((LANES - 8, 2 * LANES), BF16)
    rim_out = np.concatenate([top, top, blank[8:], rest, blank], axis=0)
    width = -(-kern_count * RIM_WIDTH // LANES) * LANES
    scatter = np.zeros((4 * LANES, width))
    for kern in range(kern_count):
        for at in range(8):
            lane = (4 * kern - 2 + at % 4) % LANES + at // 4 * LANES
            scatter[lane, kern * RIM_WIDTH + at] = 1.0
            scatter[2 * LANES + lane, kern * RIM_WIDTH + 8 + at] = 1.0
    return rim_in, rim_out, scatter.astype(BF16)


def pick_tables(freq_y, freq_x):
    col_even, col_odd = signed_picks(freq_x, LANES)
    row_even, row_odd = signed_picks(freq_y, ROWS_PAD)
    lanes = np.zeros((LANES, 2 * LANES))
    lanes[:, :freq_x] = col_even.T
    lanes[:, LANES : LANES + freq_x] = col_odd.T
    rows = np.block([[row_even, -row_odd], [-row_odd, -row_even]])
    return lanes, rows


def imaging_kernel(places, used, extra, *refs):
    owner_ref, weight_ref, pieces_ref, kern_ref, table_ref = refs[:5]
    later_hbm, refs = refs[5 : 5 + extra], refs[5 + extra :]
    slopes_ref, error_ref, later_ref, refs = refs[0], refs[1], refs[2 : 2 + extra], refs[2 + extra :]
    spec, field, rim_field, rim_lanes, rim_slope, scale_ref, ready, goal_ref, sems = refs
    kern_count, freq_y, freq_x = kern_ref.shape[2:]
    later = fetch(list(zip(later_hbm, later_ref)), sems)
    chunk = max(size for size in range(1, CHUNK + 1) if kern_count % size == 0)
    count, first, second = tiles_of(owner_ref, own_place())
    slots = (first, second)
    split = freq_y // 2
    firsts = [slot // PIECES * PIECES for slot in slots]

    def table(name):
        start, height, width = places[name]
        return table_ref[start : start + height, :width]

    upper = lax.broadcasted_iota(jnp.int32, (8, LANES), 0) < 4
    blank = jnp.zeros((ROWS_PAD - ROWS, LANES), F32)
    targets, packets = [], []
    for slot in range(MOST):
        target = jnp.concatenate(
            [pieces_ref[firsts[slot] + at, 8 + 8 * slot : 16 + 8 * slot] for at in range(PIECES)], axis=0
        )
        targets.append(jnp.where(count > slot, target, 0.0))
        pieces = []
        for at in range(0, PIECES, 2):
            even, odd = pieces_ref[firsts[slot] + at, :8], pieces_ref[firsts[slot] + at + 1, :8]
            if slot == 0:
                pieces.append(jnp.where(upper, even, odd))
            else:
                pieces.append(pltpu.roll(jnp.where(upper, odd, even), 4, 0))
        packet = jnp.concatenate(pieces, axis=0)
        packets += [jnp.where(count > slot, unpacked(packet, used), 0.0), blank]

    top, rest = halves(jnp.concatenate(packets, axis=0))
    both = mm(
        jnp.concatenate([top, rest], axis=1), jnp.concatenate([table("lanes"), table("lanes")], axis=0)
    )
    tall = [
        jnp.concatenate([both[at : at + ROWS_PAD, :LANES], both[at : at + ROWS_PAD, LANES:]], axis=0)
        for at in range(0, MOST * ROWS_PAD, ROWS_PAD)
    ]
    top, rest = halves(jnp.concatenate(tall, axis=1))
    both = mm(table("picks"), top) + mm(table("picks"), rest)
    for slot in range(MOST):
        spec[slot] = both[:, slot * LANES : (slot + 1) * LANES]

    target = jnp.concatenate(targets, axis=1)
    one = target.astype(BF16)
    target = target - one.astype(F32)
    two = target.astype(BF16)
    three = (target - two.astype(F32)).astype(BF16)
    both = mm(table("turn"), one) + mm(table("turn"), two) + mm(table("turn"), three)
    for slot in range(MOST):
        goal_ref[slot] = both[:, slot * LANES : (slot + 1) * LANES]

    half = GRID_Y // 2
    lane = lax.broadcasted_iota(jnp.int32, (freq_y, LANES), 1)
    live_lane = lane < freq_x

    def kern_at(k):
        def one(part):
            raw = kern_ref[0, part, k]
            wide = jnp.concatenate([raw, jnp.zeros((freq_y, LANES - freq_x), F32)], axis=1)
            return wide
        return one(0), one(1)

    def side_by_side(pieces):
        return pieces[0] if len(pieces) == 1 else jnp.concatenate(pieces, axis=1)

    def apart(wide):
        size = 2 * LANES
        return [wide[:, at : at + size] for at in range(0, wide.shape[1], size)]

    def to_image(stacks):
        pieces = []
        for stack in stacks:
            top, rest = halves(stack)
            pieces.append(jnp.concatenate([top, rest, top], axis=0))
        return apart(mm(table("rows"), side_by_side(pieces)))

    def from_image(stacks):
        pieces = [jnp.concatenate(halves(stack), axis=0) for stack in stacks]
        both = mm(table("rows_t"), side_by_side(pieces))
        return apart(both[:freq_y] + both[freq_y:])

    def thrice(top, rest, name):
        both = table(name)
        height = both.shape[0] // 2
        return mm(
            jnp.concatenate([top, rest, top], axis=1),
            jnp.concatenate([both[:height], both[:height], both[height:]], axis=0),
        )

    def waves(stack):
        even_re, even_im = stack[:half, :LANES], stack[:half, LANES:]
        odd_re, odd_im = stack[half:, :LANES], stack[half:, LANES:]
        return even_re - odd_im, even_im + odd_re, even_re + odd_im, even_im - odd_re

    def unwaves(plus_re, plus_im, minus_re, minus_im):
        above = jnp.concatenate([plus_re + minus_re, plus_im + minus_im], axis=1)
        below = jnp.concatenate([plus_im - minus_im, minus_re - plus_re], axis=1)
        return jnp.concatenate([above, below], axis=0)


    def forward_chunk(start, new):
        tops, rests = [], []
        for step in range(chunk):
            kern_re, kern_im = kern_at(start + step)
            for slot in range(MOST):
                spec_re, spec_im = spec[slot, :freq_y], spec[slot, freq_y:]
                wave = jnp.concatenate(
                    [kern_re * spec_re - kern_im * spec_im, kern_re * spec_im + kern_im * spec_re], axis=1
                )
                top, rest = halves(wave)
                tops.append(top)
                rests.append(rest)
        top, rest = jnp.concatenate(tops, axis=0), jnp.concatenate(rests, axis=0)
        cols = thrice(top, rest, "core")
        edges = mm(jnp.concatenate([top, rest], axis=1), table("rim"))
        places = [(step, slot) for step in range(chunk) for slot in range(MOST)]
        images = to_image([cols[at * freq_y : (at + 1) * freq_y] for at in range(len(places))])
        for at, (step, slot) in enumerate(places):
            k = start + step
            weight = weight_ref[:, k : k + 1]
            new[2] = jnp.where(group_of == k, jnp.broadcast_to(weight, (8, LANES)), new[2])
            edge = edges[at * freq_y : (at + 1) * freq_y]
            column, place = divmod(k, QUARTER // 4)
            here = slice(column * LANES, (column + 1) * LANES)
            if place == 0:
                rim_lanes[slot, :, here] = edge
            else:
                rim_lanes[slot, :, here] += pltpu.roll(edge, 4 * place, 1)
            parts = waves(images[at])
            for part in range(4):
                field[slot, k, part] = parts[part]
            plus, minus = new[slot]
            plus = plus + weight * (parts[0] * parts[0] + parts[1] * parts[1])
            minus = minus + weight * (parts[2] * parts[2] + parts[3] * parts[3])
            new[slot] = (plus, minus)

    blank = jnp.zeros((half, LANES), F32)
    group_of = lax.rem(lax.broadcasted_iota(jnp.int32, (8, LANES), 1) + 2, LANES) // 4
    sums = [(blank, blank), (blank, blank), jnp.zeros((8, LANES), F32)]
    for start in range(0, kern_count, chunk):
        forward_chunk(start, sums)
    lane_weight = sums.pop()

    norm = 1.0 / (64.0 * GRID_Y * GRID_X)
    square = norm * norm
    lane_half = lax.broadcasted_iota(jnp.int32, (half, LANES), 1)
    near = (lane_half < 2) | (lane_half >= LANES - 2)
    row_8 = lax.broadcasted_iota(jnp.int32, (8, LANES), 0)

    def rows_beside(value, other):
        first, last = value[:8], value[half - 8 :]
        later = jnp.where(row_8 == 7, last, pltpu.roll(first, 7, 0))
        sooner = jnp.where(row_8 == 0, other[:8], pltpu.roll(last, 1, 0))
        return jnp.concatenate([value[8:], later], axis=0) + jnp.concatenate([sooner, value[:-8]], axis=0)

    at_first, at_last = lane_half == 0, lane_half == LANES - 1

    def spread_out(value, rows, left, right):
        return value + DIFFUSE_RATE * (rows + left + right - 4.0 * value)

    def sides(value):
        return pltpu.roll(value, 1, 1), pltpu.roll(value, LANES - 1, 1)

    def beside(core, rim):
        return jnp.where(at_first, rim[0], core[0]), jnp.where(at_last, rim[1], core[1])

    def blur(core, rim):
        core_sides = [sides(value) for value in core]
        rim_sides = [sides(value) for value in rim]
        rim_one = [
            spread_out(rim[at], rows_beside(rim[at], rim[1 - at]), *beside(rim_sides[at], core_sides[at]))
            for at in range(2)
        ]
        core_one = [
            spread_out(core[at], rows_beside(core[at], core[1 - at]), *beside(core_sides[at], rim_sides[at]))
            for at in range(2)
        ]
        return [
            spread_out(
                core_one[at],
                rows_beside(core_one[at], core_one[1 - at]),
                *beside(sides(core_one[at]), sides(rim_one[at])),
            )
            for at in range(2)
        ]

    def blur_back(core):
        core_sides = [sides(value) for value in core]
        none = jnp.zeros((half, LANES), F32)
        rim_one = [DIFFUSE_RATE * sum(beside((none, none), core_sides[at])) for at in range(2)]
        core_one = [
            spread_out(core[at], rows_beside(core[at], core[1 - at]), *beside(core_sides[at], (none, none)))
            for at in range(2)
        ]
        core_sides = [sides(value) for value in core_one]
        rim_sides = [sides(value) for value in rim_one]
        rim_two = [
            spread_out(rim_one[at], rows_beside(rim_one[at], rim_one[1 - at]), *beside(rim_sides[at], core_sides[at]))
            for at in range(2)
        ]
        core_two = [
            spread_out(core_one[at], rows_beside(core_one[at], core_one[1 - at]), *beside(core_sides[at], rim_sides[at]))
            for at in range(2)
        ]
        return core_two, rim_two

    def fold(value):
        def back(amount):
            return pltpu.roll(value, LANES - amount, 1)
        value = value + back(48)
        value = value + back(24)
        value = value + back(12)
        return value + back(4) + back(8)

    def unfold(value):
        value = jnp.where(near, value, 0.0)
        value = value + pltpu.roll(value, 4, 1) + pltpu.roll(value, 8, 1)
        value = value + pltpu.roll(value, 12, 1)
        value = value + pltpu.roll(value, 24, 1)
        return value + pltpu.roll(value, 48, 1)

    def rim_columns(slot):
        quarter = lax.rem(lane + 2, LANES) // QUARTER
        real = imag = jnp.zeros((freq_y, LANES), F32)
        for column in range(rim_lanes.shape[2] // LANES):
            both = rim_lanes[slot, :, column * LANES : (column + 1) * LANES]
            both = both + pltpu.roll(both, 2 * QUARTER, 1)
            for_real = both if column == 0 else pltpu.roll(both, column * QUARTER, 1)
            for_imag = both if column == 1 else pltpu.roll(both, (column - 1) * QUARTER % LANES, 1)
            real = jnp.where(quarter == column, for_real, real)
            imag = jnp.where(quarter == column, for_imag, imag)
        return jnp.concatenate([real, imag], axis=1)

    error = jnp.float32(0.0)
    rim_halves = []
    for slot in range(2):
        live = (count > slot).astype(F32)
        rim_parts = waves(to_image([rim_columns(slot)])[0])
        for part in range(4):
            rim_field[slot, part] = rim_parts[part]
        weights = jnp.concatenate([lane_weight] * (half // 8), axis=0)
        rim_plus = weights * (rim_parts[0] * rim_parts[0] + rim_parts[1] * rim_parts[1])
        rim_minus = weights * (rim_parts[2] * rim_parts[2] + rim_parts[3] * rim_parts[3])
        core = [part * square for part in sums[slot]]
        rim = [jnp.where(near, fold(part), 0.0) * square for part in (rim_plus, rim_minus)]
        core = blur(core, rim)

        def slope_of(value, goal):
            resist = 1.0 / (1.0 + jnp.exp(-RESIST_SLOPE * (value - RESIST_LEVEL)))
            misfit = resist - goal
            return (2.0 * RESIST_SLOPE) * misfit * resist * (1.0 - resist), jnp.sum(misfit * misfit)

        slope_plus, err_plus = slope_of(core[0], goal_ref[slot, :half])
        slope_minus, err_minus = slope_of(core[1], goal_ref[slot, half:])
        error = error + live * (err_plus + err_minus)
        core, rim = blur_back([slope_plus, slope_minus])
        factor = 2.0 * square
        for at in range(2):
            scale_ref[slot, at] = core[at] * factor
        rim_f_plus = unfold(rim[0] * factor) * weights
        rim_f_minus = unfold(rim[1] * factor) * weights
        edge = from_image(
            [
                unwaves(
                    rim_f_plus * rim_field[slot, 0],
                    rim_f_plus * rim_field[slot, 1],
                    rim_f_minus * rim_field[slot, 2],
                    rim_f_minus * rim_field[slot, 3],
                )
            ]
        )[0]
        rim_halves.append(jnp.concatenate(halves(edge), axis=1))
    rim_stack = jnp.concatenate(rim_halves, axis=0)
    for part in range(0, rim_slope.shape[2], 2 * LANES):
        moved = mm(rim_stack, table(f"scatter{part}"))
        for slot in range(MOST):
            rim_slope[slot, :, part : part + moved.shape[1]] = moved[slot * freq_y : (slot + 1) * freq_y]
    error_ref[0] = error * (1.0 / (GRID_Y * CORE_X))


    def backward_chunk(start, sums):
        images, edges = [], []
        for step in range(chunk):
            k = start + step
            weight = weight_ref[:, k : k + 1]
            for slot in range(MOST):
                plus = scale_ref[slot, 0] * weight
                minus = scale_ref[slot, 1] * weight
                images.append(
                    unwaves(
                        plus * field[slot, k, 0],
                        plus * field[slot, k, 1],
                        minus * field[slot, k, 2],
                        minus * field[slot, k, 3],
                    )
                )
                column = k // RIM_KERNS * LANES
                edge = rim_slope[slot, :, column : column + LANES]
                if k % RIM_KERNS != 0:
                    edge = pltpu.roll(edge, LANES - k % RIM_KERNS * RIM_WIDTH, 1)
                edge = edge.astype(BF16)
                edges.append(jnp.concatenate([edge, edge], axis=1))
        pairs = [halves(cols) for cols in from_image(images)]
        top, rest = [jnp.concatenate(part, axis=0) for part in zip(*pairs)]
        waves_all = thrice(top, rest, "core_t") + mm(jnp.concatenate(edges, axis=0), table("rim_t"))
        for step in range(chunk):
            kern_re, kern_im = kern_at(start + step)
            for slot in range(MOST):
                at = (MOST * step + slot) * freq_y
                wave_re, wave_im = waves_all[at : at + freq_y, :LANES], waves_all[at : at + freq_y, LANES:]
                sums[slot][0] += wave_re * kern_re + wave_im * kern_im
                sums[slot][1] += wave_im * kern_re - wave_re * kern_im

    slopes = [[jnp.zeros((freq_y, LANES), F32)] * 2 for _ in range(MOST)]
    for start in range(0, kern_count, chunk):
        backward_chunk(start, slopes)

    tall = jnp.concatenate([jnp.concatenate(slopes[slot], axis=0) for slot in range(MOST)], axis=1)
    both = mm(table("picks_t"), jnp.concatenate(halves(tall), axis=0))
    wide = [
        jnp.concatenate([both[:ROWS_PAD, at : at + LANES], both[ROWS_PAD:, at : at + LANES]], axis=1)
        for at in range(0, MOST * LANES, LANES)
    ]
    top, rest = halves(jnp.concatenate(wide, axis=0))
    both = mm(
        jnp.concatenate([top, rest], axis=1), jnp.concatenate([table("lanes_t"), table("lanes_t")], axis=0)
    )
    packets = [packed(both[at : at + ROWS], used) for at in range(0, MOST * ROWS_PAD, ROWS_PAD)]
    for at in range(2):
        here = slice(at * split, (at + 1) * split)
        ready[at] = slot_pair(packets[0][here], packets[1][here], used)

    def give(pair_at, carry):
        slopes_ref[2 * pair_at] = ready[0]
        slopes_ref[2 * pair_at + 1] = ready[1]
        return carry

    lax.fori_loop(0, slopes_ref.shape[0] // 2, give, 0)
    for copy in later:
        copy.wait()


def imaging_table(kern_count, freq_y, freq_x):
    core, rim, rows = image_tables(freq_y, freq_x)
    lanes, picks = pick_tables(freq_y, freq_x)

    def tall(table):
        return np.concatenate(halves_np(table), axis=0)

    def three(table):
        top, rest = halves_np(table)
        return np.concatenate([top, top, rest], axis=1)

    def square_up(table):
        top, rest = halves_np(table)
        return np.block([[top, top], [rest, np.zeros_like(rest)]])

    rim_in, rim_out, scatter = rim_tables(rim, kern_count)
    tables = {
        "core": tall(core),
        "core_t": tall(core.T),
        "rim": rim_in,
        "rim_t": rim_out,
        "rows": three(rows),
        "rows_t": square_up(rows.T),
        "lanes": lanes.astype(BF16),
        "lanes_t": lanes.T.astype(BF16),
        "picks": picks.astype(BF16),
        "picks_t": np.concatenate([picks.T, picks.T], axis=1).astype(BF16),
        "turn": np.eye(GRID_Y)[
            np.concatenate([GRID_Y // 2 + half_order(), GRID_Y // 2 - 1 - half_order()])
        ].astype(BF16),
    }
    for part in range(0, scatter.shape[1], 2 * LANES):
        tables[f"scatter{part}"] = scatter[:, part : part + 2 * LANES]
    places, stacked, start = {}, [], 0
    for name, piece in tables.items():
        height, width = piece.shape
        places[name] = (start, height, width)
        stacked.append(np.pad(piece, ((0, 0), (0, 2 * LANES - width))))
        start += height
    return places, np.concatenate(stacked, axis=0)


def owner_imaging(owner_list, kern_weight, pieces, kernels, places, table, later):
    kern_count, freq_y, freq_x = kernels.shape[2:]
    tiles, split = owner_list.shape[0], freq_y // 2
    half = GRID_Y // 2
    smem = pl.BlockSpec(memory_space=pltpu.SMEM)
    vmem = pl.BlockSpec(memory_space=pltpu.VMEM)
    hbm = pl.BlockSpec(memory_space=pltpu.HBM)
    return pl.pallas_call(
        functools.partial(imaging_kernel, places, freq_x + 1, len(later)),
        in_specs=[vmem] * 5 + [hbm] * len(later),
        out_specs=(vmem, smem) + (vmem,) * len(later),
        out_shape=(
            jax.ShapeDtypeStruct((tiles, 2 * split - 8, LANES), F32),
            jax.ShapeDtypeStruct((1,), F32),
        )
        + tuple(jax.ShapeDtypeStruct(part.shape, part.dtype) for part in later),
        scratch_shapes=[
            pltpu.VMEM((MOST, 2 * freq_y, LANES), F32),
            pltpu.VMEM((MOST, kern_count, 4, half, LANES), F32),
            pltpu.VMEM((MOST, 4, half, LANES), F32),
            pltpu.VMEM((MOST, freq_y, -(-kern_count * 4 // QUARTER) * LANES), F32),
            pltpu.VMEM((MOST, freq_y, -(-kern_count * RIM_WIDTH // LANES) * LANES), F32),
            pltpu.VMEM((MOST, 2, half, LANES), F32),
            pltpu.VMEM((2, 2 * split - 8, LANES), F32),
            pltpu.VMEM((MOST, 2 * half, LANES), F32),
            pltpu.SemaphoreType.DMA((len(later),)),
        ],
        compiler_params=pltpu.CompilerParams(vmem_limit_bytes=20 * 2**20),
        name="owner_imaging",
    )(
        owner_list.reshape(1, -1), kern_weight.reshape(1, -1), in_vmem(pieces), in_vmem(kernels),
        in_vmem(table), *[in_hbm(part) for part in later],
    )


def on_device(mask_tiles, target_grid, kernels, kern_weight, owner_list):
    tile_px = mask_tiles.shape[1]
    freq_y, freq_x = kernels.shape[3:]
    count = lax.axis_size("tile")
    cols, turns, rows = mask_tables(tile_px, freq_y, freq_x)
    owner_list = owner_list.reshape(-1)
    mates = [(i, i + 1 - 2 * (i % 2)) for i in range(count)]

    pieces = mask_spectrum(mask_tiles, target_grid.reshape(GRID_Y, CORE_X), cols, turns, rows, freq_x)
    places, table = imaging_table(kernels.shape[2], freq_y, freq_x)
    pieces, table = lax.optimization_barrier((pieces, jnp.asarray(table)))
    if count == PIECES:
        pieces, edges = lax.all_to_all(pieces, "tile", 0, 0, tiled=True), None
    else:
        groups = [list(range(at, at + PIECES)) for at in range(0, count, PIECES)]
        pieces = lax.all_to_all(pieces, "tile", 0, 0, axis_index_groups=groups, tiled=True)
        later = [(i, i + PIECES) for i in range(count - PIECES)]
        sooner = [(i + PIECES, i) for i in range(count - PIECES)]
        edges = jnp.stack(
            [lax.ppermute(pieces[PIECES - 1], "tile", later), lax.ppermute(pieces[0], "tile", sooner)]
        )
    pieces = lax.all_to_all(route(owner_list, pieces, edges), "tile", 0, 0, tiled=True)
    slopes, owner_error, *held = owner_imaging(
        owner_list, kern_weight, pieces, kernels, places, table,
        (mask_tiles,) + update_tables(cols, turns, rows),
    )
    slopes = lax.all_to_all(slopes, "tile", 0, 0, tiled=True)
    other = lax.ppermute(tile_pick(owner_list, slopes, freq_x), "tile", mates)
    current = mask_update(owner_list, slopes, other, *held, freq_x)
    return (current, owner_error)


def solution(mesh):
    placed = (
        P(("stripe", "tile"), None, None),
        P(("stripe", "tile"), None),
        P("tile", None, None, None, None),
        P(),
        P("stripe", None),
    )
    return jax.shard_map(
        on_device,
        mesh=mesh,
        in_specs=placed,
        out_specs=(P(("stripe", "tile"), None, None), P(("stripe", "tile"))),
        check_vma=False,
    )
```
